32 devices in a mesh: dp: 8 (over y, x, core), mp: 4 (over z).
Axes of the slice: x: 2, y: 2, z: 4, core: 2. Of those that a mesh axis runs over, the one named last changes fastest.
Arguments:
- tokens: bfloat16 [16384, 512], P(('dp', 'mp')), may hold values from -6 to 6
- doc_ids: int32 [16, 1024], P('dp'), may hold values from 0 to 7, never falling along the last dimension, each value on 1 to 512 neighbouring positions
- resets: int32 [16], P('dp'), may hold values from 1 to 1023
- norm_one_gain: float32 [512], replicated, may hold values from 0.1 to 1.9
- norm_one_bias: float32 [512], replicated, may hold values from -3 to 3
- query_weight: bfloat16 [512, 512], P(None, 'mp'), may hold values from -0.25 to 0.25
- key_weight: bfloat16 [512, 512], P(None, 'mp'), may hold values from -0.25 to 0.25
- value_weight: bfloat16 [512, 512], P(None, 'mp'), may hold values from -0.25 to 0.25
- output_weight: bfloat16 [512, 512], P('mp'), may hold values from -2 to 2
- output_bias: float32 [512], replicated, may hold values from -3 to 3
- gate_one_weight: bfloat16 [512, 512], replicated, may hold values from -0.25 to 0.25
- gate_one_bias: float32 [512], replicated, may hold values from -3 to 3
- norm_two_gain: float32 [512], replicated, may hold values from 0.1 to 1.9
- norm_two_bias: float32 [512], replicated, may hold values from -3 to 3
- up_weight: bfloat16 [512, 2048], P(None, 'mp'), may hold values from -0.25 to 0.25
- up_bias: float32 [2048], P('mp'), may hold values from -3 to 3
- down_weight: bfloat16 [2048, 512], P('mp'), may hold values from -0.25 to 0.25
- down_bias: float32 [512], replicated, may hold values from -3 to 3
- gate_two_weight: bfloat16 [512, 512], replicated, may hold values from -0.25 to 0.25
- gate_two_bias: float32 [512], replicated, may hold values from -3 to 3
- cotangent: bfloat16 [16384, 512], P(('dp', 'mp')), may hold values from -6 to 6
Outputs:
- output: bfloat16 [16384, 512], P(('dp', 'mp'))
- grad_tokens: float32 [16384, 512], P(('dp', 'mp'))
- grad_norm_one_gain: float32 [512], replicated
- grad_norm_one_bias: float32 [512], replicated
- grad_query_weight: float32 [512, 512], P(None, 'mp')
- grad_key_weight: float32 [512, 512], P(None, 'mp')
- grad_value_weight: float32 [512, 512], P(None, 'mp')
- grad_output_weight: float32 [512, 512], P('mp')
- grad_output_bias: float32 [512], replicated
- grad_gate_one_weight: float32 [512, 512], replicated
- grad_gate_one_bias: float32 [512], replicated
- grad_norm_two_gain: float32 [512], replicated
- grad_norm_two_bias: float32 [512], replicated
- grad_up_weight: float32 [512, 2048], P(None, 'mp')
- grad_up_bias: float32 [2048], P('mp')
- grad_down_weight: float32 [2048, 512], P('mp')
- grad_down_bias: float32 [512], replicated
- grad_gate_two_weight: float32 [512, 512], replicated
- grad_gate_two_bias: float32 [512], replicated
The draws below stay inside these ranges and needn't reach their ends.
Inputs may be any that keep to these rules, and one draw needn't show every extreme that they name: `doc_ids`: within a row the ids never fall, and each id covers 1 to 512 tokens of the row.
All inputs are finite; a program needn't handle non-finite values.
Results may differ from the reference program's by a relative error of at most 0.018.
Values may be sent and summed in bfloat16 or wider, within the bound.
A program may use at most 128 MiB of HBM per device.

```python
import math
import jax
import jax.numpy as jnp
import numpy as np
from jax import lax

D = 512
HEADS = 8
HDIM = 64
FF = 2048
SEQ = 1024
ROWS = 16
TOKENS = 16384


def plant(array, stream_key, smallest, largest):
    extent = array.shape
    index_at = [jax.random.randint(jax.random.fold_in(stream_key, axis), (), 0, extent[axis]) for axis in range(len(extent))]
    array = array.at[tuple(index_at)].set(smallest)
    longest = extent.index(max(extent))
    index_at[longest] = (index_at[longest] + 1) % extent[longest]
    return array.at[tuple(index_at)].set(largest)


def block_levels(rng, shape, pieces, least, high):
    def one(axis_at, shards_of):
        heights = jax.random.uniform(jax.random.fold_in(jax.random.fold_in(rng, 6), axis_at), (shards_of,), jnp.float32, least / len(pieces), high / len(pieces))
        return jnp.repeat(jnp.exp(heights), shape[axis_at] // shards_of).reshape((-1,) + (1,) * (len(shape) - axis_at - 1))

    level = one(*pieces[0])
    for cut in pieces[1:]:
        level = level * one(*cut)
    return level


def split_up(number_of, total, limit, lean):
    weights = [(1 << 20) // math.isqrt(rank ** lean) + 1 for rank in range(2, number_of + 1)]
    rest, counts = total - limit - (number_of - 1), [1] * (number_of - 1)
    while rest > 0:
        movable = [i for i in range(number_of - 1) if counts[i] < limit]
        mass, remaining = sum([weights[i] for i in movable]), rest
        for i in movable:
            more = min(limit - counts[i], max(1, remaining * weights[i] // mass), rest)
            counts[i] = counts[i] + more
            rest = rest - more
    return np.array([limit] + counts)


def ragged(key, number_of, total, most, skew):
    if number_of == 2:
        one = jax.random.randint(key, (), max(1, total - most), min(most, total - 1) + 1)
        return jnp.stack([one, total - one])
    lengths = jnp.asarray(split_up(number_of, total, most, skew), jnp.int32)
    couples = (number_of - 1) // 2
    giver, taker = lengths[1:1 + 2 * couples:2], lengths[2:2 + 2 * couples:2]
    slack = jnp.minimum(giver - 1, most - taker)
    passed = jax.random.randint(jax.random.fold_in(key, 1), (couples,), 0, 1 << 20) % (slack + 1)
    lengths = lengths.at[1:1 + 2 * couples:2].set(giver - passed).at[2:2 + 2 * couples:2].set(taker + passed)
    return lengths[jax.random.permutation(jax.random.fold_in(key, 2), number_of)]


def centred(rng, dims, deviation, limit, cuts=(), kind=jnp.bfloat16):
    level = block_levels(rng, dims, cuts, -0.22, 0.18) if cuts else 1.0
    drawn = jax.random.normal(rng, dims, jnp.float32) * deviation * level
    return jnp.minimum(jnp.maximum(drawn, -limit), limit).astype(kind)


def setup_inputs(seed: int = 0) -> dict:
    splits = jax.random.split(jax.random.key(seed), 22)
    tokens = centred(splits[0], (TOKENS, D), 1.0, 6.0, ((0, 32),))
    doc_ids = jax.vmap(lambda own: jnp.searchsorted(jnp.cumsum(ragged(own, max(4, SEQ // 128), SEQ, SEQ // 2, 1)), jnp.arange(SEQ), side="right"))(jax.random.split(splits[1], ROWS)).reshape((ROWS, SEQ)).astype(jnp.int32)
    resets = plant(jax.random.randint(splits[2], (ROWS,), 1, SEQ), jax.random.fold_in(splits[2], 1), 1, SEQ - 1).astype(jnp.int32)
    norm_one_gain = jnp.clip(1.0 + 0.18 * jax.random.normal(splits[3], (D,), jnp.float32), 0.1, 1.9)
    norm_one_bias = centred(splits[4], (D,), 0.3, 3.0, (), jnp.float32)
    query_weight = centred(splits[5], (D, D), D ** -0.5, 0.25, ((1, 4),))
    key_weight = centred(splits[6], (D, D), D ** -0.5, 0.25, ((1, 4),))
    value_weight = centred(splits[7], (D, D), D ** -0.5, 0.25, ((1, 4),))
    output_weight = centred(splits[8], (D, D), (D // 64) ** -0.5, 2.0, ((0, 4),))
    output_bias = centred(splits[9], (D,), 0.3, 3.0, (), jnp.float32)
    gate_one_weight = centred(splits[10], (D, D), D ** -0.5, 0.25)
    gate_one_bias = centred(splits[11], (D,), 0.5, 3.0, (), jnp.float32)
    norm_two_gain = jnp.clip(1.0 + 0.18 * jax.random.normal(splits[12], (D,), jnp.float32), 0.1, 1.9)
    norm_two_bias = centred(splits[13], (D,), 0.3, 3.0, (), jnp.float32)
    up_weight = centred(splits[14], (D, FF), D ** -0.5, 0.25, ((1, 4),))
    up_bias = centred(splits[15], (FF,), 0.5, 3.0, ((0, 4),), jnp.float32)
    down_weight = centred(splits[16], (FF, D), (FF // 4) ** -0.5, 0.25, ((0, 4),))
    down_bias = centred(splits[17], (D,), 0.3, 3.0, (), jnp.float32)
    gate_two_weight = centred(splits[18], (D, D), D ** -0.5, 0.25)
    gate_two_bias = centred(splits[19], (D,), 0.5, 3.0, (), jnp.float32)
    cotangent = centred(splits[20], (TOKENS, D), 1.0, 6.0, ((0, 32),))
    return {"tokens": tokens, "doc_ids": doc_ids, "resets": resets, "norm_one_gain": norm_one_gain, "norm_one_bias": norm_one_bias, "query_weight": query_weight, "key_weight": key_weight, "value_weight": value_weight, "output_weight": output_weight, "output_bias": output_bias, "gate_one_weight": gate_one_weight, "gate_one_bias": gate_one_bias, "norm_two_gain": norm_two_gain, "norm_two_bias": norm_two_bias, "up_weight": up_weight, "up_bias": up_bias, "down_weight": down_weight, "down_bias": down_bias, "gate_two_weight": gate_two_weight, "gate_two_bias": gate_two_bias, "cotangent": cotangent}


@jax.custom_vjp
def low(v):
    return lax.optimization_barrier(v.astype(jnp.bfloat16)).astype(jnp.float32)

@jax.custom_vjp
def low_back(v):
    return v

def low_keep(v):
    return (low(v), None)

def low_pass(kept, grad):
    return (grad,)

def back_keep(v):
    return (v, None)

def back_low(kept, grad):
    return (low(grad),)
low.defvjp(low_keep, low_pass)
low_back.defvjp(back_keep, back_low)
HIGHEST = lax.Precision.HIGHEST

def matmul(left, right):
    return jnp.dot(left, right, precision=HIGHEST)

def layer_norm(values, gain, bias):
    centered = values - lax.optimization_barrier(jnp.mean(values, axis=-1, keepdims=True))
    variance = lax.optimization_barrier(jnp.mean(centered * centered, axis=-1, keepdims=True))
    return centered * lax.rsqrt(variance + 1e-05) * gain + bias

def rotary_tables(resets, seq_len):
    steps = jnp.arange(seq_len, dtype=jnp.int32)
    places = jnp.where(steps[None, :] >= resets[:, None], steps[None, :] - resets[:, None], steps[None, :])
    freqs = jnp.exp(jnp.arange(HDIM // 2, dtype=jnp.float32) * (-2.0 * math.log(10000.0) / HDIM))
    angles = places.astype(jnp.float32)[:, :, None] * freqs
    return (jnp.cos(angles)[:, :, None, :], jnp.sin(angles)[:, :, None, :])

def rotate(values, cosine, sine):
    first, second = jnp.split(values, 2, axis=-1)
    return jnp.concatenate([first * cosine - second * sine, second * cosine + first * sine], axis=-1)

def attend_row(query, keys, values, docs):
    scale = 1.0 / math.sqrt(HDIM)
    scores = low_back(jnp.einsum('qhd,khd->hqk', query, keys, precision=HIGHEST) * scale)
    places = jnp.arange(docs.shape[0], dtype=jnp.int32)
    allowed = (docs[:, None] == docs[None, :]) & (places[None, :] <= places[:, None])
    scores = jnp.where(allowed[None], scores, -1e+30)
    highest = lax.optimization_barrier(jnp.max(scores, axis=-1, keepdims=True))
    weights = jnp.exp(scores - highest)
    probs = weights / lax.optimization_barrier(jnp.sum(weights, axis=-1, keepdims=True))
    context = jnp.einsum('hqk,khd->qhd', low(probs), values, precision=HIGHEST)
    return low(low_back(context))

def block(inputs, norm_one_gain, norm_one_bias, query_weight, key_weight, value_weight, output_weight, output_bias, gate_one_weight, gate_one_bias, norm_two_gain, norm_two_bias, up_weight, up_bias, down_weight, down_bias, gate_two_weight, gate_two_bias, doc_ids, cosine, sine):
    row_count, seq_len = doc_ids.shape
    grid = (row_count, seq_len, HEADS, HDIM)
    normed_one = low(layer_norm(inputs, norm_one_gain, norm_one_bias))
    query = low(rotate(low_back(matmul(normed_one, query_weight)).reshape(grid), cosine, sine))
    keys = low(rotate(low_back(matmul(normed_one, key_weight)).reshape(grid), cosine, sine))
    values = low(low_back(matmul(normed_one, value_weight))).reshape(grid)
    context = lax.map(jax.checkpoint(lambda bundle: attend_row(*bundle)), (query, keys, values, doc_ids))
    context = context.reshape(row_count * seq_len, HEADS * HDIM)
    attended = low_back(matmul(context, output_weight)) + output_bias
    gate_one = jax.nn.sigmoid(low_back(matmul(normed_one, gate_one_weight)) + gate_one_bias)
    middle = inputs + gate_one * (attended - inputs)
    normed_two = low(layer_norm(middle, norm_two_gain, norm_two_bias))
    hidden = low(jax.nn.gelu(low_back(matmul(normed_two, up_weight)) + up_bias, approximate=True))
    branch = low_back(matmul(hidden, down_weight)) + down_bias
    gate_two = jax.nn.sigmoid(low_back(matmul(normed_two, gate_two_weight)) + gate_two_bias)
    return middle + gate_two * (branch - middle)

def reference(tokens, doc_ids, resets, norm_one_gain, norm_one_bias, query_weight, key_weight, value_weight, output_weight, output_bias, gate_one_weight, gate_one_bias, norm_two_gain, norm_two_bias, up_weight, up_bias, down_weight, down_bias, gate_two_weight, gate_two_bias, cotangent):
    cosine, sine = rotary_tables(resets, doc_ids.shape[1])
    floats = tuple((entry.astype(jnp.float32) for entry in (tokens, norm_one_gain, norm_one_bias, query_weight, key_weight, value_weight, output_weight, output_bias, gate_one_weight, gate_one_bias, norm_two_gain, norm_two_bias, up_weight, up_bias, down_weight, down_bias, gate_two_weight, gate_two_bias)))

    def forward(*params):
        return block(*params, doc_ids, cosine, sine)
    result, backward = jax.vjp(forward, *floats)
    grads = backward(cotangent.astype(jnp.float32))
    return (result.astype(jnp.bfloat16), grads[0], grads[1], grads[2], grads[3], grads[4], grads[5], grads[6], grads[7], grads[8], grads[9], grads[10], grads[11], grads[12], grads[13], grads[14], grads[15], grads[16], grads[17])
```

```python
import functools
import math
from types import SimpleNamespace

import jax
import jax.numpy as jnp
import numpy as np
from jax import lax
from jax.experimental import pallas as pl
from jax.experimental.pallas import tpu as pltpu
from jax.sharding import PartitionSpec as P

BF = jnp.bfloat16
F32 = jnp.float32
MESH = pl.DeviceIdType.MESH
D = 512
T = 512
S = 1024
HD = 64
CH = 256
NCOPY = 128
GELU_A = math.sqrt(2.0 / math.pi)
GELU_B = 0.044715


def mm(a, b):
    return lax.dot_general(a, b, (((1,), (0,)), ((), ())), preferred_element_type=F32)


def mmt(a, b):
    return lax.dot_general(a, b, (((1,), (1,)), ((), ())), preferred_element_type=F32)


def tmm(a, b):
    return lax.dot_general(a, b, (((0,), (0,)), ((), ())), preferred_element_type=F32)


def sigmoid(v):
    return 0.5 * jnp.tanh(0.5 * v) + 0.5


def colsum(v):
    return jnp.sum(v, axis=0, keepdims=True)


def rowmean(v):
    return jnp.mean(v, axis=-1, keepdims=True)


OUT_SHAPES = dict(
    o_out=((T, D), BF),
    o_gt=((T, D), F32),
    o_a=((8, 64, 512), BF),
    o_u=((8, 128, 256), BF),
    o_d=((8, 64, 512), BF),
    o_g1=((8, 4, 32, 256), BF),
    o_g2=((8, 4, 32, 256), BF),
    o_vec=((16, 512), F32),
)

SCRATCH = dict(
    xt=((T, D), BF), ct=((T, D), BF),
    info=((2, 8, S), F32), dcol=((S, 128), F32), drow=((8, S), F32),
    ctb=((S, 128), F32), stb=((S, 128), F32), cttb=((128, S), F32), sttb=((128, S), F32),
    wz=((4, 256, 512), BF), wt=((768, 512), BF), wo=((256, 512), BF),
    upz=((4, 512, 256), BF), dnz=((4, 256, 512), BF), ubz=((4, 8, 256), F32),
    n1=((S, D), BF), xh1=((T, D), F32), rs1=((T, 128), F32), g1=((T, D), F32),
    q=((S, 256), BF), k=((S, 256), BF), v=((S, 256), BF),
    km=((4, S, 256), BF), vm=((4, S, 256), BF),
    bias=((CH, 768), F32), pr=((4, CH, 2304), BF), ctx=((S, 256), BF),
    xs=((T, D), F32), xr=((T, D), F32), amx=((T, D), F32), mid=((T, D), F32),
    xh2=((T, D), F32), rs2=((T, 128), F32), n2=((S, D), BF),
    hid=((S, 1024), BF), gp=((S, 1024), BF),
    outb=((T, D), BF),
    bl=((S, D), BF), go2=((T, D), BF), gl2=((S, 256), BF),
    al=((S, D), BF), go1=((T, D), BF), gl1=((S, 256), BF),
    gmr=((T, D), F32),
    dc=((S, 256), BF), dct=((256, S), BF), qt=((256, S), BF),
    dkt=((256, S), F32), dvt=((256, S), F32), dq=((S, 768), BF), dt=((768, S), BF),
    a_s=((4, 256, 512), BF), a_a=((3, 4, 64, 512), BF), a_b=((4, 64, 512), BF), a_c=((3, 64, 512), BF),
    u_s=((4, 512, 256), BF), u_a=((3, 4, 128, 256), BF), u_b=((4, 128, 256), BF), u_c=((3, 128, 256), BF),
    d_s=((4, 256, 512), BF), d_a=((3, 4, 64, 512), BF), d_b=((4, 64, 512), BF), d_c=((3, 64, 512), BF),
    e_s=((4, 128, 256), BF), e_a=((3, 4, 32, 256), BF), e_b=((4, 32, 256), BF), e_c=((3, 32, 256), BF),
    f_s=((4, 128, 256), BF), f_a=((3, 4, 32, 256), BF), f_b=((4, 32, 256), BF), f_c=((3, 32, 256), BF),
    pk=((16, 512), F32), pk1=((2, 16, 512), F32), pk2=((4, 16, 512), F32), pk3=((4, 16, 512), F32),
)


def kernel(ndp, xbits, names, *refs):
    R = SimpleNamespace(**dict(zip(names, refs)))
    dp = lax.axis_index("dp")
    m = lax.axis_index("mp")
    bits = [lax.rem(lax.div(dp, 1 << b), 2) for b in range(ndp.bit_length() - 1)]
    c = bits[0]
    g = bits[1] + 2 * bits[2]
    mb = [lax.rem(m, 2), lax.div(m, 2)]

    def dpx(mask):
        value = dp
        for b in range(len(bits)):
            if mask >> b & 1:
                value = value + (1 - 2 * bits[b]) * (1 << b)
        return value

    def mx(mask):
        value = m
        for b in range(2):
            if mask >> b & 1:
                value = value + (1 - 2 * mb[b]) * (1 << b)
        return value

    def gx(mask):
        value = g
        for b in range(2):
            if mask >> b & 1:
                value = value + (1 - 2 * bits[1 + b]) * (1 << b)
        return value

    swap = (c + mb[0]) == 1
    r0 = pl.multiple_of(c * T, T)
    p0 = pl.multiple_of(T - c * T, T)
    slot = c + 2 * g
    counter = [0]

    def remote(src, dst, device):
        index = counter[0]
        counter[0] += 1
        return pltpu.make_async_remote_copy(
            src_ref=src, dst_ref=dst, send_sem=R.ss.at[index], recv_sem=R.rs.at[index],
            device_id=device, device_id_type=MESH,
        )

    def local(src, dst, index):
        return pltpu.make_async_copy(src, dst, R.ls.at[index])

    partner = (dpx(1), m)
    cross = (dpx(1), mx(1))
    barrier = pltpu.get_barrier_semaphore()
    friends = [(dpx(k), m) for k in range(1, 8)] + [(dp, mx(k)) for k in (1, 2, 3)] + [cross]
    friends += [(dpx(1 << b), m) for b in range(3, 3 + xbits)]
    for friend in friends:
        pl.semaphore_signal(barrier, inc=1, device_id=friend, device_id_type=MESH)
    own_up = local(R.up.at[:, pl.ds(pl.multiple_of(c * 256, 256), 256)], R.upz.at[m], 0)
    own_dn = local(R.down.at[pl.ds(pl.multiple_of(c * 256, 256), 256), :], R.dnz.at[m], 1)
    own_up.start()
    own_dn.start()
    loc_x = local(R.tokens, R.xt, 2)
    loc_c = local(R.cot, R.ct, 3)

    @pl.when(jnp.logical_not(swap))
    def _():
        loc_x.start()
        loc_c.start()

    lane = lax.broadcasted_iota(jnp.int32, (64, 128), 1)
    pick = (lane == lax.broadcasted_iota(jnp.int32, (64, 128), 0) + c * 64)
    pick = jnp.where(pick, 1.0, 0.0).astype(BF)
    wz = R.wz
    wz[m, 0:64, :] = mmt(pick, R.qw[...]).astype(BF)
    wz[m, 64:128, :] = mmt(pick, R.kw[...]).astype(BF)
    wz[m, 128:192, :] = mmt(pick, R.vw[...]).astype(BF)
    wz[m, 192:256, :] = R.ow[pl.ds(pl.multiple_of(c * 64, 64), 64), :]
    ubv = R.ub[...]
    ubv = jnp.where(c == 0, ubv[:, :256], ubv[:, 256:])
    R.ubz[m] = jnp.broadcast_to(ubv, (8, 256))
    info = R.info
    fl = lax.broadcasted_iota(jnp.int32, (2, 128), 1)
    freq = jnp.exp(lax.rem(fl, 32).astype(F32) * (-2.0 * math.log(10000.0) / HD))
    turn = jnp.where(
        lax.broadcasted_iota(jnp.int32, (2, 128), 0) == 0, R.resets[0:1, 0:1], R.resets[0:1, 1:2]
    ).astype(F32)
    info[0] = jnp.zeros((8, S), F32)
    info[0, 0:2, :] = R.docs[...].astype(F32)
    info[0, 2:4, 0:128] = jnp.cos(turn * freq)
    info[0, 2:4, 128:256] = jnp.sin(turn * freq)
    info[0, 2:4, 256:384] = turn

    pl.semaphore_wait(barrier, len(friends))

    swap_x = remote(R.tokens, R.xt, cross)
    swap_c = remote(R.cot, R.ct, cross)

    @pl.when(swap)
    def _():
        swap_x.start()

    w_1 = remote(wz.at[m], wz.at[m], (dp, mx(1)))
    w_3 = remote(wz.at[m], wz.at[m], (dp, mx(3)))
    w_3.start()
    w_1.start()
    send_info = remote(info.at[0], info.at[1], partner)
    send_info.start()
    ub_copies = [remote(R.ubz.at[m], R.ubz.at[m], (dp, mx(k))) for k in (1, 2, 3)]
    for copy in ub_copies:
        copy.start()

    send_info.wait()
    row = mb[1]
    mine = jnp.where(swap, 0.0, 1.0)

    def info_row(i):
        return info[0, pl.ds(i, 1), :] * mine + info[1, pl.ds(i, 1), :] * (1.0 - mine)

    doc = info_row(row)
    turn_row = info_row(row + 2)
    R.drow[...] = jnp.broadcast_to(doc, (8, S))
    R.dcol[...] = jnp.broadcast_to(doc, (128, S)).T
    cr, sr, rr = turn_row[:, 0:128], turn_row[:, 128:256], turn_row[:, 256:384]

    @pl.loop(0, 4)
    def _(i):
        rows = pl.ds(pl.multiple_of(i * CH, CH), CH)
        c0, s0 = R.ctab[rows, :], R.stab[rows, :]
        place = (lax.broadcasted_iota(jnp.int32, (CH, 128), 0) + i * CH).astype(F32)
        past = place >= rr
        cc = jnp.where(past, c0 * cr + s0 * sr, c0)
        sn = jnp.where(past, s0 * cr - c0 * sr, s0)
        R.ctb[rows, :] = cc
        R.stb[rows, :] = sn
        R.cttb[:, rows] = cc.T
        R.sttb[:, rows] = sn.T

    @pl.when(jnp.logical_not(swap))
    def _():
        loc_x.wait()
        loc_c.wait()

    @pl.when(swap)
    def _():
        swap_x.wait()

    n1 = R.n1

    @pl.loop(0, 2)
    def _(i):
        rows = pl.ds(pl.multiple_of(i * CH, CH), CH)
        x = R.xt[rows, :].astype(F32)
        x = x - rowmean(x)
        rstd = lax.rsqrt(rowmean(x * x) + 1e-05)
        xh = x * rstd
        R.xh1[rows, :] = xh
        R.rs1[rows, :] = jnp.broadcast_to(rstd, (CH, 128))
        n1[pl.ds(pl.multiple_of(r0 + i * CH, CH), CH), :] = (xh * R.n1g[...] + R.n1b[...]).astype(BF)

    own_rows = pl.ds(r0, T)
    partner_rows = pl.ds(p0, T)
    send_n1 = remote(n1.at[own_rows, :], n1.at[own_rows, :], partner)
    send_n1.start()

    @pl.loop(0, 2)
    def _(i):
        rows = pl.ds(pl.multiple_of(i * CH, CH), CH)
        gate = mm(n1[pl.ds(pl.multiple_of(r0 + i * CH, CH), CH), :], R.wg1[...]) + R.g1b[...]
        R.g1[rows, :] = sigmoid(gate)

    w_1.wait_recv()
    w_3.wait_recv()
    relay_3 = remote(wz.at[mx(1), 0:128, :], wz.at[mx(1), 0:128, :], (dp, mx(3)))
    relay_1 = remote(wz.at[mx(3), 128:256, :], wz.at[mx(3), 128:256, :], (dp, mx(1)))
    relay_3.start()
    relay_1.start()
    own_up.wait()
    own_dn.wait()
    upz, dnz = R.upz, R.dnz
    relay_3.wait_recv()
    relay_1.wait_recv()
    ff = []
    for z in (upz, dnz):
        for k in (3, 1):
            ff.append(remote(z.at[m], z.at[m], (dp, mx(k))))
    for copy in ff:
        copy.start()

    @pl.when(swap)
    def _():
        swap_c.start()

    wt = R.wt
    for z in range(4):
        wt[z * 32 : z * 32 + 32, :] = wz[z, 0:32, :]
        wt[128 + z * 32 : 160 + z * 32, :] = wz[z, 32:64, :]
        wt[256 + z * 32 : 288 + z * 32, :] = wz[z, 64:96, :]
        wt[384 + z * 32 : 416 + z * 32, :] = wz[z, 96:128, :]
        wt[512 + z * 64 : 576 + z * 64, :] = wz[z, 128:192, :]
        R.wo[z * 64 : z * 64 + 64, :] = wz[z, 192:256, :]

    flane = lax.broadcasted_iota(jnp.int32, (1, 256), 1)
    qmask = [jnp.where(lax.div(lax.rem(flane, 128), 32) == h, 1.0, 0.0).astype(BF) for h in range(4)]
    vmask = [jnp.where(lax.div(flane, 64) == h, 1.0, 0.0).astype(BF) for h in range(4)]

    def project(base):
        @pl.loop(0, 2)
        def _(i):
            rows = pl.ds(pl.multiple_of(base + i * CH, CH), CH)
            both = mmt(n1[rows, :], wt[...])
            cc, sn = R.ctb[rows, :], R.stb[rows, :]
            qa, qb = both[:, 0:128], both[:, 128:256]
            ka, kb = both[:, 256:384], both[:, 384:512]
            qq = jnp.concatenate([qa * cc - qb * sn, qb * cc + qa * sn], axis=1).astype(BF)
            kk = jnp.concatenate([ka * cc - kb * sn, kb * cc + ka * sn], axis=1).astype(BF)
            vv = both[:, 512:768].astype(BF)
            R.q[rows, :] = qq * jnp.asarray(0.125, BF)
            R.k[rows, :] = kk
            R.v[rows, :] = vv
            for h in range(4):
                R.km[h, rows, :] = kk * qmask[h]
                R.vm[h, rows, :] = vv * vmask[h]

    project(r0)
    send_n1.wait()
    project(p0)

    relays = []
    for j, (z, half) in enumerate(((upz, 256), (dnz, 128))):
        ff[2 * j].wait_recv()
        ff[2 * j + 1].wait_recv()
        relays.append(remote(z.at[mx(1), 0:half, :], z.at[mx(1), 0:half, :], (dp, mx(3))))
        relays.append(remote(z.at[mx(3), half : 2 * half, :], z.at[mx(3), half : 2 * half, :], (dp, mx(1))))
    for copy in relays:
        copy.start()

    def span(i):
        width = min(i + 1, 3) * CH
        return (i + 1) * CH - width, width

    def lead(i):
        return sum(span(j)[1] for j in range(i))

    for i in range(4):
        j0, width = span(i)
        rows = slice(i * CH, (i + 1) * CH)
        dcol = R.dcol[rows, :]
        qi = lax.broadcasted_iota(jnp.int32, (CH, 128), 0) + i * CH
        for w in range(width // 128):
            ki = lax.broadcasted_iota(jnp.int32, (CH, 128), 1) + (j0 + w * 128)
            ok = (dcol == R.drow[0:1, j0 + w * 128 : j0 + w * 128 + 128]) & (ki <= qi)
            R.bias[:, w * 128 : w * 128 + 128] = jnp.where(ok, 0.0, -1e30)
        qr = R.q[rows, :]
        total = jnp.zeros((CH, 256), F32)
        for h in range(4):
            sc = mmt(qr * qmask[h], R.k[j0 : j0 + width, :]) + R.bias[:, 0:width]
            e = jnp.exp(sc - jnp.max(sc, axis=-1, keepdims=True))
            p = (e * (1.0 / jnp.sum(e, axis=-1, keepdims=True))).astype(BF)
            R.pr[h, :, lead(i) : lead(i) + width] = p
            total = total + mm(p, R.vm[h, j0 : j0 + width, :])
        R.ctx[rows, :] = total.astype(BF)

    def chunks(body):
        pl.loop(0, 2)(body)

    def at(base, i):
        return pl.ds(pl.multiple_of(base + i * CH, CH), CH)

    @chunks
    def _(i):
        R.xs[at(0, i), :] = mm(R.ctx[at(p0, i), :], R.wo[...])

    send_at = remote(R.xs, R.xr, partner)
    send_at.start()

    @chunks
    def _(i):
        R.amx[at(0, i), :] = mm(R.ctx[at(r0, i), :], R.wo[...])

    send_at.wait()
    n2 = R.n2

    @chunks
    def _(i):
        rows = at(0, i)
        x = R.xt[rows, :].astype(F32)
        amx = R.amx[rows, :] + R.xr[rows, :] + R.ob[...] - x
        R.amx[rows, :] = amx
        mid = x + R.g1[rows, :] * amx
        R.mid[rows, :] = mid
        mid = mid - rowmean(mid)
        rstd = lax.rsqrt(rowmean(mid * mid) + 1e-05)
        xh = mid * rstd
        R.xh2[rows, :] = xh
        R.rs2[rows, :] = jnp.broadcast_to(rstd, (CH, 128))
        n2[at(r0, i), :] = (xh * R.n2g[...] + R.n2b[...]).astype(BF)

    send_n2 = remote(n2.at[own_rows, :], n2.at[own_rows, :], partner)
    send_n2.start()
    for copy in relays + ub_copies:
        copy.wait_recv()

    def up_part(base):
        @chunks
        def _(i):
            rows = at(base, i)
            a = n2[rows, :]
            for z in range(4):
                v = mm(a, upz[z]) + R.ubz[z, 0:1, :]
                v2 = v * v
                t = jnp.tanh(GELU_A * v * (1.0 + GELU_B * v2))
                half = 0.5 * (1.0 + t)
                R.hid[rows, z * 256 : z * 256 + 256] = (v * half).astype(BF)
                slope = half + (0.5 * GELU_A) * v * (1.0 - t * t) * (1.0 + (3.0 * GELU_B) * v2)
                R.gp[rows, z * 256 : z * 256 + 256] = slope.astype(BF)

    def down_part(base, dst):
        @chunks
        def _(i):
            rows = at(base, i)
            total = mm(R.hid[rows, 0:256], dnz[0])
            for z in range(1, 4):
                total = total + mm(R.hid[rows, z * 256 : z * 256 + 256], dnz[z])
            dst[at(0, i), :] = total

    up_part(r0)
    send_n2.wait()
    up_part(p0)
    down_part(p0, R.xs)
    send_br = remote(R.xs, R.xr, partner)
    send_br.start()
    down_part(r0, R.gmr)

    @pl.when(swap)
    def _():
        swap_c.wait()

    pk = R.pk
    pk[...] = jnp.zeros((16, 512), F32)
    send_br.wait()

    @chunks
    def _(i):
        rows = at(0, i)
        gate = sigmoid(mm(n2[at(r0, i), :], R.wg2[...]) + R.g2b[...])
        mid = R.mid[rows, :]
        bm = R.gmr[rows, :] + R.xr[rows, :] + R.db[...] - mid
        R.outb[rows, :] = (mid + gate * bm).astype(BF)
        cot = R.ct[rows, :].astype(F32)
        gb = gate * cot
        rest = cot - gb
        R.mid[rows, :] = rest
        gg = rest * bm * gate
        R.bl[at(r0, i), :] = gb.astype(BF)
        R.go2[rows, :] = gg.astype(BF)
        pk[6:7, :] += colsum(gb)
        pk[7:8, :] += colsum(gg)

    mine_cols = pl.ds(pl.multiple_of(c * 256, 256), 256)
    their_cols = pl.ds(pl.multiple_of(256 - c * 256, 256), 256)
    send_bl = remote(R.bl.at[own_rows, :], R.bl.at[own_rows, :], partner)
    send_bl.start()
    send_gl2 = remote(R.go2.at[:, their_cols], R.gl2.at[own_rows, :], partner)
    send_gl2.start()
    keep_gl2 = local(R.go2.at[:, mine_cols], R.gl2.at[own_rows, :], 4)
    keep_gl2.start()
    back_o = remote(R.outb, R.o_out, cross)
    keep_o = local(R.outb, R.o_out, 5)

    @pl.when(swap)
    def _():
        back_o.start()

    @pl.when(jnp.logical_not(swap))
    def _():
        keep_o.start()

    def hidden_back(base):
        sums = []
        for z in range(4):
            lanes = slice(z * 256, z * 256 + 256)

            def step(i, acc, lanes=lanes, z=z):
                rows = at(base, i)
                gpre = mmt(R.bl[rows, :], dnz[z]) * R.gp[rows, lanes].astype(F32)
                R.gp[rows, lanes] = gpre.astype(BF)
                return acc + colsum(gpre)

            both = lax.fori_loop(0, 2, step, jnp.zeros((1, 256), F32))
            pk[8 + z : 9 + z, 0:256] += jnp.where(c == 0, both, 0.0)
            pk[8 + z : 9 + z, 256:512] += jnp.where(c == 0, 0.0, both)

    def norm_two_part(base, dst):
        @chunks
        def _(i):
            rows = at(base, i)
            total = mmt(R.gp[rows, 0:256], upz[0])
            for z in range(1, 4):
                total = total + mmt(R.gp[rows, z * 256 : z * 256 + 256], upz[z])
            dst[at(0, i), :] = total

    hidden_back(r0)
    send_bl.wait()
    hidden_back(p0)
    norm_two_part(p0, R.xs)
    send_d2 = remote(R.xs, R.xr, partner)
    send_d2.start()
    norm_two_part(r0, R.gmr)

    def reduce_start(name, quarter):
        out = []
        for k in (1, 2, 3):
            rows = pl.ds(pl.multiple_of(gx(k) * quarter, quarter), quarter)
            copy = remote(getattr(R, name + "_s").at[:, rows, :], getattr(R, name + "_a").at[k - 1], (dpx(2 * k), m))
            copy.start()
            out.append(copy)
        return out

    def reduce_middle(name, quarter, copies):
        for copy in copies:
            copy.wait()
        rows = pl.ds(pl.multiple_of(g * quarter, quarter), quarter)
        for z in range(4):
            total = getattr(R, name + "_s")[z, rows, :].astype(F32)
            for k in range(3):
                total = total + getattr(R, name + "_a")[k, z].astype(F32)
            getattr(R, name + "_b")[z] = total.astype(BF)
        out = []
        for k in (1, 2, 3):
            copy = remote(getattr(R, name + "_b").at[mx(k)], getattr(R, name + "_c").at[k - 1], (dp, mx(k)))
            copy.start()
            out.append(copy)
        return out

    def reduce_total(name, copies):
        for copy in copies:
            copy.wait()
        total = getattr(R, name + "_b")[m].astype(F32)
        for k in range(3):
            total = total + getattr(R, name + "_c")[k].astype(F32)
        for b in range(xbits):
            getattr(R, name + "_x")[2 * b] = total.astype(BF)
            copy = remote(getattr(R, name + "_x").at[2 * b], getattr(R, name + "_x").at[2 * b + 1], (dpx(8 << b), m))
            copy.start()
            copy.wait()
            total = getattr(R, name + "_x")[2 * b].astype(F32) + getattr(R, name + "_x")[2 * b + 1].astype(F32)
        return total.astype(BF)

    def spread(out):
        copies = []
        for k in range(1, 8):
            copy = remote(out.at[slot], out.at[slot], (dpx(k), m))
            copy.start()
            copies.append(copy)
        return copies

    def reduce_end(name, out, copies):
        out[slot] = reduce_total(name, copies)
        return spread(out)

    def reduce_end_all(name, out, copies):
        out[slot, m] = reduce_total(name, copies)
        copies = []
        for k in (1, 2, 3):
            copy = remote(out.at[slot, m], out.at[slot, m], (dp, mx(k)))
            copy.start()
            copies.append(copy)
        return copies

    for z in range(4):
        R.d_s[z] = tmm(R.hid[:, z * 256 : z * 256 + 256], R.bl[...]).astype(BF)
    d_1 = reduce_start("d", 64)
    n2t = n2[...].T
    for z in range(4):
        R.u_s[z] = mm(n2t, R.gp[:, z * 256 : z * 256 + 256]).astype(BF)
    u_1 = reduce_start("u", 128)
    send_gl2.wait()
    keep_gl2.wait()
    full = mm(n2t, R.gl2[...]).astype(BF)
    for z in range(4):
        R.e_s[z] = full[z * 128 : z * 128 + 128, :]
    e_1 = reduce_start("e", 32)

    send_d2.wait()

    @chunks
    def _(i):
        rows = at(0, i)
        gn = R.gmr[rows, :] + R.xr[rows, :] + mmt(R.go2[rows, :], R.wg2[...])
        xh = R.xh2[rows, :]
        pk[4:5, :] += colsum(gn * xh)
        pk[5:6, :] += colsum(gn)
        e = gn * R.n2g[...]
        gm = R.rs2[rows, 0:1] * (e - rowmean(e) - xh * rowmean(e * xh)) + R.mid[rows, :]
        gate = R.g1[rows, :]
        ga = gate * gm
        gg = (gm - ga) * R.amx[rows, :] * gate
        R.mid[rows, :] = gm - ga
        R.al[at(r0, i), :] = ga.astype(BF)
        R.go1[rows, :] = gg.astype(BF)
        pk[2:3, :] += colsum(ga)
        pk[3:4, :] += colsum(gg)

    send_al = remote(R.al.at[own_rows, :], R.al.at[own_rows, :], partner)
    send_al.start()
    send_gl1 = remote(R.go1.at[:, their_cols], R.gl1.at[own_rows, :], partner)
    send_gl1.start()
    keep_gl1 = local(R.go1.at[:, mine_cols], R.gl1.at[own_rows, :], 6)
    keep_gl1.start()
    R.qt[...] = R.q[...].T
    n1t = n1[...].T
    send_al.wait()

    @pl.loop(0, 4)
    def _(i):
        rows = at(0, i)
        a = R.al[rows, :]
        R.dc[rows, :] = mmt(a, R.wo[...]).astype(BF)
        R.dct[:, rows] = mmt(R.wo[...], a).astype(BF)

    grad_wo = tmm(R.ctx[...], R.al[...]).astype(BF)
    for z in range(4):
        R.a_s[z, 192:256, :] = grad_wo[z * 64 : z * 64 + 64, :]
    send_gl1.wait()
    keep_gl1.wait()
    full = mm(n1t, R.gl1[...]).astype(BF)
    for z in range(4):
        R.f_s[z] = full[z * 128 : z * 128 + 128, :]
    f_1 = reduce_start("f", 32)

    dkt, dvt = R.dkt, R.dvt
    dkt[...] = jnp.zeros((256, S), F32)
    dvt[...] = jnp.zeros((256, S), F32)
    for i in range(4):
        j0, width = span(i)
        rows = slice(i * CH, (i + 1) * CH)
        keys = slice(j0, j0 + width)
        dcr = R.dc[rows, :]
        total = jnp.zeros((CH, 256), F32)
        for h in range(4):
            p = R.pr[h, :, lead(i) : lead(i) + width]
            pf = p.astype(F32)
            t = mmt(dcr * vmask[h], R.v[keys, :]) * pf
            ds = (t - pf * jnp.sum(t, axis=-1, keepdims=True)).astype(BF)
            total = total + mm(ds, R.km[h, keys, :])
            dvt[h * 64 : h * 64 + 64, keys] += mm(R.dct[h * 64 : h * 64 + 64, rows], p)
            qh = jnp.concatenate(
                [R.qt[h * 32 : h * 32 + 32, rows], R.qt[128 + h * 32 : 160 + h * 32, rows]], axis=0
            )
            dk = mm(qh, ds)
            dkt[h * 32 : h * 32 + 32, keys] += dk[0:32]
            dkt[128 + h * 32 : 160 + h * 32, keys] += dk[32:64]
        total = total * 0.125
        a, b = total[:, 0:128], total[:, 128:256]
        cc, sn = R.ctb[rows, :], R.stb[rows, :]
        R.dq[rows, 0:256] = jnp.concatenate([a * cc + b * sn, b * cc - a * sn], axis=1).astype(BF)
        if i == 1:
            d_2 = reduce_middle("d", 64, d_1)
            u_2 = reduce_middle("u", 128, u_1)
            e_2 = reduce_middle("e", 32, e_1)
        if i == 2:
            d_3 = reduce_end("d", R.o_d, d_2)
            u_3 = reduce_end("u", R.o_u, u_2)
            e_3 = reduce_end_all("e", R.o_g2, e_2)
    f_2 = reduce_middle("f", 32, f_1)

    dt = R.dt
    dt[512:768, :] = dvt[...].astype(BF)
    a, b = dkt[0:128, :], dkt[128:256, :]
    dt[256:384, :] = (a * R.cttb[...] + b * R.sttb[...]).astype(BF)
    dt[384:512, :] = (b * R.cttb[...] - a * R.sttb[...]).astype(BF)
    dt[0:256, :] = R.dq[:, 0:256].T
    R.dq[:, 256:768] = dt[256:768, :].T

    @chunks
    def _(i):
        R.xs[at(0, i), :] = mm(R.dq[at(p0, i), :], wt[...])

    send_d1 = remote(R.xs, R.xr, partner)
    send_d1.start()
    for part in range(3):
        grad = mm(dt[part * 256 : part * 256 + 256, :], n1[...]).astype(BF)
        for z in range(4):
            if part < 2:
                R.a_s[z, part * 64 : part * 64 + 32, :] = grad[z * 32 : z * 32 + 32, :]
                R.a_s[z, part * 64 + 32 : part * 64 + 64, :] = grad[128 + z * 32 : 160 + z * 32, :]
            else:
                R.a_s[z, 128:192, :] = grad[z * 64 : z * 64 + 64, :]
    a_1 = reduce_start("a", 64)

    for copy in e_3:
        copy.wait()
    e_4 = spread(R.o_g2)
    f_3 = reduce_end_all("f", R.o_g1, f_2)

    @chunks
    def _(i):
        R.gmr[at(0, i), :] = mm(R.dq[at(r0, i), :], wt[...])

    send_d1.wait()

    @chunks
    def _(i):
        rows = at(0, i)
        gn = R.gmr[rows, :] + R.xr[rows, :] + mmt(R.go1[rows, :], R.wg1[...])
        xh = R.xh1[rows, :]
        pk[0:1, :] += colsum(gn * xh)
        pk[1:2, :] += colsum(gn)
        e = gn * R.n1g[...]
        R.gmr[rows, :] = R.rs1[rows, 0:1] * (e - rowmean(e) - xh * rowmean(e * xh)) + R.mid[rows, :]

    back_t = remote(R.gmr, R.o_gt, cross)
    keep_t = local(R.gmr, R.o_gt, 7)

    pk1, pk2, pk3 = R.pk1, R.pk2, R.pk3
    pk1[c] = pk[...]
    p_1 = remote(pk1.at[c], pk1.at[c], partner)
    p_1.start()

    @pl.when(swap)
    def _():
        back_t.start()

    @pl.when(jnp.logical_not(swap))
    def _():
        keep_t.start()

    a_2 = reduce_middle("a", 64, a_1)
    p_1.wait()
    pk2[g] = pk1[0] + pk1[1]
    p_2 = [remote(pk2.at[g], pk2.at[g], (dpx(2 * k), m)) for k in (1, 2, 3)]
    for copy in p_2:
        copy.start()
    for copy in f_3:
        copy.wait()
    f_4 = spread(R.o_g1)
    for copy in p_2:
        copy.wait()
    pk3[m] = (pk2[0] + pk2[1]) + (pk2[2] + pk2[3])
    p_3 = [remote(pk3.at[m], pk3.at[m], (dp, mx(k))) for k in (1, 2, 3)]
    for copy in p_3:
        copy.start()
    a_3 = reduce_end("a", R.o_a, a_2)
    for copy in p_3:
        copy.wait()
    total = (pk3[0] + pk3[1]) + (pk3[2] + pk3[3])
    for b in range(xbits):
        R.p_x[2 * b] = total
        copy = remote(R.p_x.at[2 * b], R.p_x.at[2 * b + 1], (dpx(8 << b), m))
        copy.start()
        copy.wait()
        total = R.p_x[2 * b] + R.p_x[2 * b + 1]
    pk[...] = total
    R.o_vec[...] = total
    R.o_vec[8:9, :] = pk[pl.ds(8 + m, 1), :]

    for copy in [w_1, w_3, relay_1, relay_3] + ub_copies + ff + relays:
        copy.wait_send()
    for copy in d_3 + u_3 + e_4 + f_4 + a_3:
        copy.wait()

    @pl.when(swap)
    def _():
        back_o.wait()
        back_t.wait()

    @pl.when(jnp.logical_not(swap))
    def _():
        keep_o.wait()
        keep_t.wait()


def unpack(a, u, d, g1, g2, vec, out, gt, *outs):
    (oq, ok, ov, oo, ou, od, og1, og2, oout, ogt) = outs[:10]
    for j, ref in enumerate((oq, ok, ov)):
        both = jnp.concatenate([a[2 * j].astype(F32), a[2 * j + 1].astype(F32)], axis=0)
        ref[...] = both.T
    for c in range(2):
        oo[c * 64 : c * 64 + 64, :] = a[6 + c].astype(F32)
        for g in range(4):
            ou[g * 128 : g * 128 + 128, c * 256 : c * 256 + 256] = u[2 * g + c].astype(F32)
            od[c * 256 + g * 64 : c * 256 + g * 64 + 64, :] = d[2 * g + c].astype(F32)
            for z in range(4):
                rows = slice(z * 128 + g * 32, z * 128 + g * 32 + 32)
                og1[rows, c * 256 : c * 256 + 256] = g1[2 * g + c, z].astype(F32)
                og2[rows, c * 256 : c * 256 + 256] = g2[2 * g + c, z].astype(F32)
    oout[...] = out[...]
    ogt[...] = gt[...]
    for j, ref in enumerate(outs[10:]):
        ref[...] = vec[j : j + 1, :]


def tables():
    freqs = np.exp(np.arange(HD // 2, dtype=np.float32) * np.float32(-2.0 * math.log(10000.0) / HD))
    angles = np.arange(S, dtype=np.float32)[:, None] * freqs.astype(np.float32)
    angles = np.tile(angles.astype(np.float64), (1, 4))
    return np.cos(angles).astype(np.float32), np.sin(angles).astype(np.float32)


def shards(
    ndp, tokens, doc_ids, resets, n1g, n1b, qw, kw, vw, ow, ob, wg1, g1b, n2g, n2b, up, ub, down, db,
    wg2, g2b, cot,
):
    xbits = ndp.bit_length() - 4
    ctab, stab = tables()
    vector = lambda v: v.reshape(1, -1)
    values = dict(
        tokens=tokens, cot=cot, docs=doc_ids, resets=resets.reshape(1, 2), qw=qw, kw=kw, vw=vw, ow=ow,
        wg1=wg1, up=up, down=down, wg2=wg2, n1g=vector(n1g), n1b=vector(n1b), ob=vector(ob),
        g1b=vector(g1b), n2g=vector(n2g), n2b=vector(n2b), ub=vector(ub), db=vector(db), g2b=vector(g2b),
        ctab=jnp.asarray(ctab), stab=jnp.asarray(stab),
    )
    vmem = pl.BlockSpec(memory_space=pltpu.VMEM)
    anyspace = pl.BlockSpec(memory_space=pl.ANY)
    scratch = {name: pltpu.VMEM(shape, dtype) for name, (shape, dtype) in SCRATCH.items()}
    if xbits:
        more = dict(a_x=(64, 512), u_x=(128, 256), d_x=(64, 512), e_x=(32, 256), f_x=(32, 256))
        for name, shape in more.items():
            scratch[name] = pltpu.VMEM((2 * xbits,) + shape, BF)
        scratch.update(p_x=pltpu.VMEM((2 * xbits, 16, 512), F32))
    copies = pltpu.SemaphoreType.DMA((NCOPY + 6 * xbits,))
    scratch.update(ss=copies, rs=copies, ls=pltpu.SemaphoreType.DMA((8,)))
    in_specs = dict.fromkeys(values, vmem)
    in_specs.update(tokens=anyspace, cot=anyspace, up=anyspace, down=anyspace)
    packed = pl.pallas_call(
        functools.partial(kernel, ndp, xbits, (*values, *OUT_SHAPES, *scratch)),
        out_shape=[jax.ShapeDtypeStruct(shape, dtype) for shape, dtype in OUT_SHAPES.values()],
        in_specs=list(in_specs.values()),
        out_specs=[vmem] * len(OUT_SHAPES),
        scratch_shapes=list(scratch.values()),
        compiler_params=pltpu.CompilerParams(
            collective_id=0, has_side_effects=True, vmem_limit_bytes=64 << 20
        ),
        name="block",
    )(*values.values())
    out, gt, a, u, d, g1, g2, vec = packed
    f32 = lambda *shape: jax.ShapeDtypeStruct(shape, F32)
    shapes = [f32(D, 128)] * 3 + [f32(128, D)] + [f32(D, D)] * 4
    shapes += [jax.ShapeDtypeStruct((T, D), BF), f32(T, D)] + [f32(1, D)] * 9
    res = pl.pallas_call(
        unpack,
        out_shape=shapes,
        in_specs=[vmem] * 8,
        out_specs=[vmem] * len(shapes),
        compiler_params=pltpu.CompilerParams(vmem_limit_bytes=63 << 20),
        name="unpack",
    )(a, u, d, g1, g2, vec, out, gt)
    gq, gk, gv, go, gu, gd, gg1, gg2, out, gt = res[:10]
    rn1g, rn1b, rob, rg1b, rn2g, rn2b, rdb, rg2b, rub = [v.reshape(-1) for v in res[10:]]
    return (
        out, gt, rn1g, rn1b, gq, gk, gv, go, rob, gg1, rg1b, rn2g, rn2b, gu, rub, gd, rdb, gg2, rg2b,
    )


def solution(mesh):
    both, rep = P(("dp", "mp"), None), P()
    cols, rows = P(None, "mp"), P("mp", None)
    in_specs = (
        both, P("dp", None), P("dp"), rep, rep, cols, cols, cols, rows, rep, rep, rep, rep, rep, cols,
        P("mp"), rows, rep, rep, rep, both,
    )
    out_specs = (
        both, both, rep, rep, cols, cols, cols, rows, rep, rep, rep, rep, rep, cols, P("mp"), rows, rep,
        rep, rep,
    )
    fn = functools.partial(shards, mesh.shape["dp"])
    return jax.shard_map(fn, mesh=mesh, in_specs=in_specs, out_specs=out_specs, check_vma=False)
```

```python
import functools
import math
from types import SimpleNamespace

import jax
import jax.numpy as jnp
import numpy as np
from jax import lax
from jax.experimental import pallas as pl
from jax.experimental.pallas import tpu as pltpu
from jax.sharding import PartitionSpec as P

BF = jnp.bfloat16
F32 = jnp.float32
MESH = pl.DeviceIdType.MESH
D = 512
T = 512
S = 1024
HD = 64
CH = 256
NCOPY = 256
GELU_A = math.sqrt(2.0 / math.pi)
GELU_B = 0.044715


def mm(a, b):
    return lax.dot_general(a, b, (((1,), (0,)), ((), ())), preferred_element_type=F32)


def mmt(a, b):
    return lax.dot_general(a, b, (((1,), (1,)), ((), ())), preferred_element_type=F32)


def tmm(a, b):
    return lax.dot_general(a, b, (((0,), (0,)), ((), ())), preferred_element_type=F32)


def sigmoid(v):
    return 0.5 * jnp.tanh(0.5 * v) + 0.5


def colsum(v):
    return jnp.sum(v, axis=0, keepdims=True)


def rowmean(v):
    return jnp.mean(v, axis=-1, keepdims=True)


OUT_SHAPES = dict(
    o_out=((T, D), BF),
    o_gt=((T, D), BF),
    o_a=((8, 64, 512), BF),
    o_u=((8, 128, 256), BF),
    o_d=((8, 64, 512), BF),
    o_g1=((8, 4, 32, 256), BF),
    o_g2=((8, 4, 32, 256), BF),
    o_vec=((16, 512), F32),
)

SCRATCH = dict(
    xt=((T, D), BF), ct=((T, D), BF),
    info=((2, 8, S), F32), dcol=((S, 128), F32), drow=((8, S), F32),
    cttb=((32, S), F32), sttb=((32, S), F32),
    wz=((4, 256, 512), BF), wh=((768, 512), BF), wo=((256, 512), BF),
    upz=((4, 512, 256), BF), dnz=((4, 256, 512), BF), ubz=((4, 8, 256), F32),
    n1=((S, D), BF), xh1=((T, D), F32), rs1=((T, 128), F32), g1=((T, D), F32),
    qt=((4, 64, S), BF), kt=((4, 64, S), BF), vt=((4, 64, S), BF),
    bias=((CH, 2304), F32), pr=((4, CH, 2304), BF), ctxt=((256, S), BF),
    xs=((T, D), BF), xr=((T, D), BF), amx=((T, D), F32), mid=((T, D), F32),
    xh2=((T, D), F32), rs2=((T, 128), F32), n2=((S, D), BF),
    hid=((4, S, 256), BF), gp=((4, S, 256), BF), acc=((T, D), F32), outb=((T, D), BF),
    bl=((S, D), BF), go2=((T, D), BF), gl2=((S, 256), BF),
    al=((S, D), BF), go1=((T, D), BF), gl1=((S, 256), BF), gmr=((T, D), F32),
    dct=((256, S), BF),
    dkt=((64, S), F32), dvt=((64, S), F32), dt=((768, S), BF), gtb=((T, D), BF),
    a_s=((4, 256, 512), BF), a_h=((4, 8, 32, 512), BF), a_b=((4, 64, 512), BF), a_c=((3, 64, 512), BF),
    u_s=((4, 512, 256), BF), u_h=((4, 8, 64, 256), BF), u_b=((4, 128, 256), BF), u_c=((3, 128, 256), BF),
    d_s=((4, 256, 512), BF), d_h=((4, 8, 32, 512), BF), d_b=((4, 64, 512), BF), d_c=((3, 64, 512), BF),
    e_s=((4, 128, 256), BF), e_h=((8, 2, 32, 256), BF), e_b=((4, 32, 256), BF), e_c=((3, 32, 256), BF),
    f_s=((4, 128, 256), BF), f_h=((8, 2, 32, 256), BF), f_b=((4, 32, 256), BF), f_c=((3, 32, 256), BF),
    wg1v=((D, D), BF), wg2v=((D, D), BF),
    pk=((16, 512), F32), pk1=((2, 16, 512), F32), pk2=((4, 16, 512), F32), pk3=((4, 16, 512), F32),
)


def kernel(ndp, xbits, names, *refs):
    R = SimpleNamespace(**dict(zip(names, refs)))
    dp = lax.axis_index("dp")
    m = lax.axis_index("mp")
    bits = [lax.rem(lax.div(dp, 1 << b), 2) for b in range(ndp.bit_length() - 1)]
    c = bits[0]
    g = bits[1] + 2 * bits[2]
    mb = [lax.rem(m, 2), lax.div(m, 2)]

    def flip(value, own, mask):
        for b in range(len(own)):
            if mask >> b & 1:
                value = value + (1 - 2 * own[b]) * (1 << b)
        return value

    dpx = lambda mask: flip(dp, bits, mask)
    mx = lambda mask: flip(m, mb, mask)
    gx = lambda mask: flip(g, bits[1:3], mask)

    def ds(start, size):
        return pl.ds(pl.multiple_of(start, size), size)

    swap = (c + mb[0]) == 1
    r0 = pl.multiple_of(c * T, T)
    p0 = pl.multiple_of(T - c * T, T)
    slot = c * 4 + g
    counter = [0]
    unsent = []

    def remote(src, dst, device, keep=True):
        index = counter[0]
        counter[0] += 1
        copy = pltpu.make_async_remote_copy(
            src_ref=src, dst_ref=dst, send_sem=R.ss.at[index], recv_sem=R.rs.at[index],
            device_id=device, device_id_type=MESH,
        )
        if keep:
            copy.start()
            unsent.append(copy)
        return copy

    def local(src, dst, index):
        return pltpu.make_async_copy(src, dst, R.ls.at[index])

    def arrived(copies):
        for copy in copies:
            copy.wait_recv()

    partner = (dpx(1), m)
    cross = (dpx(1), mx(1))
    chip_x, chip_y = (dpx(2), m), (dpx(4), m)
    near, far = (dp, mx(1)), (dp, mx(3))
    own_rows = pl.ds(r0, T)
    mine_cols = ds(c * 256, 256)
    their_cols = ds(256 - c * 256, 256)

    barrier = pltpu.get_barrier_semaphore()
    friends = [partner, (dpx(2), m), (dpx(4), m), (dpx(6), m)] + [(dp, mx(k)) for k in (1, 2, 3)] + [cross]
    friends += [(dpx(1 << b), m) for b in range(3, 3 + xbits)]
    for friend in friends:
        pl.semaphore_signal(barrier, inc=1, device_id=friend, device_id_type=MESH)
    wz, upz, dnz = R.wz, R.upz, R.dnz
    loads = [
        local(src, dst, 9 + i)
        for i, (src, dst) in enumerate(((R.wg1, R.wg1v), (R.wg2, R.wg2v)))
    ]
    for copy in loads:
        copy.start()
    own_up = local(R.up.at[:, mine_cols], upz.at[m], 0)
    own_dn = local(R.down.at[ds(c * 256, 256), :], dnz.at[m], 1)
    own_up.start()
    own_dn.start()
    loc_x = local(R.tokens, R.xt, 2)
    loc_c = local(R.cot, R.ct, 3)

    @pl.when(jnp.logical_not(swap))
    def _():
        loc_x.start()
        loc_c.start()

    lane = lax.broadcasted_iota(jnp.int32, (64, 128), 1)
    pick = lane == lax.broadcasted_iota(jnp.int32, (64, 128), 0) + c * 64
    pick = jnp.where(pick, 1.0, 0.0).astype(BF)
    wz[m, 0:64, :] = mmt(pick, R.qw[...]).astype(BF)
    wz[m, 64:128, :] = mmt(pick, R.kw[...]).astype(BF)
    wz[m, 128:192, :] = mmt(pick, R.vw[...]).astype(BF)
    wz[m, 192:256, :] = R.ow[ds(c * 64, 64), :]
    ubv = R.ub[...]
    ubv = jnp.where(c == 0, ubv[:, :256], ubv[:, 256:])
    R.ubz[m] = jnp.broadcast_to(ubv, (8, 256))
    info = R.info
    turn = jnp.where(
        lax.broadcasted_iota(jnp.int32, (2, 128), 0) == 0, R.resets[0:1, 0:1], R.resets[0:1, 1:2]
    ).astype(F32)
    info[0] = jnp.zeros((8, S), F32)
    info[0, 0:2, :] = R.docs[...].astype(F32)
    info[0, 2:4, 0:128] = turn

    pl.semaphore_wait(barrier, len(friends))

    swap_x = remote(R.tokens, R.xt, cross, keep=False)
    swap_c = remote(R.cot, R.ct, cross, keep=False)

    near_first = (1, 2, 3)

    def gather(z, rows, lanes):
        quarter = rows // 4
        part = ds(g * quarter, quarter)
        pair = ds(bits[2] * 2 * quarter, 2 * quarter)
        other = ds(gx(2) * quarter, quarter)
        low, high = pl.ds(0, lanes // 2), pl.ds(lanes // 2, lanes // 2)

        def send(block, part, lanes, device):
            return remote(z.at[block, part, lanes], z.at[block, part, lanes], device)

        lines = [send(m, part, pl.ds(0, lanes), (dp, mx(k))) for k in near_first]
        yield
        one, two = [], []
        for k, line in zip(near_first, lines):
            line.wait_recv()
            one.append([send(mx(k), part, low, chip_x), send(mx(k), part, high, chip_y)])
            yield
        for k, copies in zip(near_first, one):
            arrived(copies)
            two.append([
                send(mx(k), pair, low, chip_y), send(mx(k), part, high, chip_x),
                send(mx(k), other, high, chip_x),
            ])
            yield
        for copies in two:
            arrived(copies)
            yield

    def go(steps, count):
        for _ in range(count):
            next(steps)

    get_w, get_u, get_d = gather(wz, 256, 512), gather(upz, 512, 256), gather(dnz, 256, 512)
    next(get_w)

    @pl.when(swap)
    def _():
        swap_x.start()

    own_up.wait()
    next(get_u)
    own_dn.wait()
    next(get_d)

    @pl.when(swap)
    def _():
        swap_c.start()

    send_info = remote(info.at[0], info.at[1], partner)
    ub_copies = [remote(R.ubz.at[m], R.ubz.at[m], (dp, mx(k))) for k in (1, 2, 3)]

    send_info.wait_recv()
    for copy in loads:
        copy.wait()
    row = mb[1]
    mine = jnp.where(swap, 0.0, 1.0)

    def info_row(i):
        return info[0, pl.ds(i, 1), :] * mine + info[1, pl.ds(i, 1), :] * (1.0 - mine)

    doc = info_row(row)
    turn = info_row(row + 2)[:, 0:1]
    R.drow[...] = jnp.broadcast_to(doc, (8, S))
    R.dcol[...] = jnp.broadcast_to(doc, (128, S)).T
    freq = jnp.exp(
        lax.broadcasted_iota(jnp.int32, (32, 1), 0).astype(F32) * (-2.0 * math.log(10000.0) / HD)
    )
    cr, sr = jnp.cos(turn * freq), jnp.sin(turn * freq)
    past = lax.broadcasted_iota(jnp.int32, (1, S), 1).astype(F32) >= turn
    c0, s0 = R.ctab[...], R.stab[...]
    R.cttb[...] = jnp.where(past, c0 * cr + s0 * sr, c0)
    R.sttb[...] = jnp.where(past, s0 * cr - c0 * sr, s0)

    def at(base, i):
        return ds(base + i * CH, CH)

    def chunks(body):
        pl.loop(0, 2)(body)

    go(get_w, 3)

    @pl.when(jnp.logical_not(swap))
    def _():
        loc_x.wait()
        loc_c.wait()

    @pl.when(swap)
    def _():
        swap_x.wait()

    n1 = R.n1

    @chunks
    def _(i):
        rows = at(0, i)
        x = R.xt[rows, :].astype(F32)
        x = x - rowmean(x)
        rstd = lax.rsqrt(rowmean(x * x) + 1e-05)
        xh = x * rstd
        R.xh1[rows, :] = xh
        R.rs1[rows, :] = jnp.broadcast_to(rstd, (CH, 128))
        n1[at(r0, i), :] = (xh * R.n1g[...] + R.n1b[...]).astype(BF)

    send_n1 = remote(n1.at[own_rows, :], n1.at[own_rows, :], partner)
    go(get_w, 3)

    def project(z, base):
        lanes = ds(base, T)
        both = mmt(wz[z, 0:192, :], n1[lanes, :])
        cc, sn = R.cttb[:, lanes], R.sttb[:, lanes]
        for dst, a, b, scale in ((R.qt, both[0:32], both[32:64], 0.125), (R.kt, both[64:96], both[96:128], 1.0)):
            dst[z, 0:32, lanes] = (a * cc - b * sn).astype(BF) * jnp.asarray(scale, BF)
            dst[z, 32:64, lanes] = (b * cc + a * sn).astype(BF) * jnp.asarray(scale, BF)
        R.vt[z, :, lanes] = both[128:192].astype(BF)
        R.wh[ds(z * 192, 192), :] = wz[z, 0:192, :]
        R.wo[ds(z * 64, 64), :] = wz[z, 192:256, :]

    def span(i):
        width = min(i + 1, 3) * CH
        return (i + 1) * CH - width, width

    def lead(i):
        return sum(span(j)[1] for j in range(i))

    def attend(z):
        for i in range(4):
            j0, width = span(i)
            rows, keys = slice(i * CH, (i + 1) * CH), slice(j0, j0 + width)
            here = slice(lead(i), lead(i) + width)
            sc = tmm(R.qt[z, :, rows], R.kt[z, :, keys]) + R.bias[:, here]
            e = jnp.exp(sc - jnp.max(sc, axis=-1, keepdims=True))
            p = (e * (1.0 / jnp.sum(e, axis=-1, keepdims=True))).astype(BF)
            R.pr[z, :, here] = p
            R.ctxt[ds(z * 64, 64), rows] = mmt(R.vt[z, :, keys], p).astype(BF)

    project(m, r0)
    for i in range(4):
        j0, width = span(i)
        dcol = R.dcol[i * CH : (i + 1) * CH, :]
        qi = lax.broadcasted_iota(jnp.int32, (CH, 128), 0) + i * CH
        for w in range(width // 128):
            ki = lax.broadcasted_iota(jnp.int32, (CH, 128), 1) + (j0 + w * 128)
            ok = (dcol == R.drow[0:1, j0 + w * 128 : j0 + w * 128 + 128]) & (ki <= qi)
            R.bias[:, lead(i) + w * 128 : lead(i) + w * 128 + 128] = jnp.where(ok, 0.0, -1e30)
    send_n1.wait_recv()
    go(get_u, 3)
    project(m, p0)
    go(get_d, 3)
    attend(m)

    @chunks
    def _(i):
        gate = mm(n1[at(r0, i), :], R.wg1v[...]) + R.g1b[...]
        R.g1[at(0, i), :] = sigmoid(gate)

    for k in near_first:
        go(get_w, 1)
        project(mx(k), r0)
        project(mx(k), p0)
        if k == 1:
            go(get_u, 3)
        if k == 2:
            go(get_d, 3)
        attend(mx(k))

    def hand_over(body):
        copies = []
        for i in range(2):
            rows = slice(i * CH, i * CH + CH)
            R.xs[rows, :] = body(i).astype(BF)
            copies.append(remote(R.xs.at[rows, :], R.xr.at[rows, :], partner, keep=False))
            copies[i].start()
        return copies

    def wait_all(copies):
        for copy in copies:
            copy.wait()

    send_at = hand_over(lambda i: tmm(R.ctxt[:, at(p0, i)], R.wo[...]))

    @chunks
    def _(i):
        R.amx[at(0, i), :] = tmm(R.ctxt[:, at(r0, i)], R.wo[...])

    wait_all(send_at)
    n2 = R.n2

    @chunks
    def _(i):
        rows = at(0, i)
        x = R.xt[rows, :].astype(F32)
        amx = R.amx[rows, :] + R.xr[rows, :].astype(F32) + R.ob[...] - x
        R.amx[rows, :] = amx
        mid = x + R.g1[rows, :] * amx
        R.mid[rows, :] = mid
        mid = mid - rowmean(mid)
        rstd = lax.rsqrt(rowmean(mid * mid) + 1e-05)
        xh = mid * rstd
        R.xh2[rows, :] = xh
        R.rs2[rows, :] = jnp.broadcast_to(rstd, (CH, 128))
        n2[at(r0, i), :] = (xh * R.n2g[...] + R.n2b[...]).astype(BF)

    send_n2 = remote(n2.at[own_rows, :], n2.at[own_rows, :], partner)
    arrived(ub_copies)

    def up_part(base, z):
        @chunks
        def _(i):
            rows = at(base, i)
            v = mm(n2[rows, :], upz[z]) + R.ubz[z, 0:1, :]
            v2 = v * v
            t = jnp.tanh(GELU_A * v * (1.0 + GELU_B * v2))
            half = 0.5 * (1.0 + t)
            R.hid[z, rows, :] = (v * half).astype(BF)
            slope = half + (0.5 * GELU_A) * v * (1.0 - t * t) * (1.0 + (3.0 * GELU_B) * v2)
            R.gp[z, rows, :] = slope.astype(BF)

    def down_part(base, dst, z, begin):
        @chunks
        def _(i):
            part = mm(R.hid[z, at(base, i), :], dnz[z])
            dst[at(0, i), :] = part if begin else dst[at(0, i), :] + part

    up_part(r0, m)
    send_n2.wait_recv()
    up_part(p0, m)
    for k in near_first:
        go(get_u, 1)
        up_part(r0, mx(k))
        up_part(p0, mx(k))
    down_part(p0, R.acc, m, True)
    down_part(r0, R.gmr, m, True)
    for k in near_first:
        go(get_d, 1)
        down_part(p0, R.acc, mx(k), False)
        if k == near_first[-1]:
            send_br = hand_over(lambda i: R.acc[i * CH : i * CH + CH, :])
        down_part(r0, R.gmr, mx(k), False)

    @pl.when(swap)
    def _():
        swap_c.wait()

    pk = R.pk
    pk[...] = jnp.zeros((16, 512), F32)
    wait_all(send_br)

    @chunks
    def _(i):
        rows = at(0, i)
        gate = sigmoid(mm(n2[at(r0, i), :], R.wg2v[...]) + R.g2b[...])
        mid = R.mid[rows, :]
        bm = R.gmr[rows, :] + R.xr[rows, :].astype(F32) + R.db[...] - mid
        R.outb[rows, :] = (mid + gate * bm).astype(BF)
        cot = R.ct[rows, :].astype(F32)
        gb = gate * cot
        rest = cot - gb
        R.mid[rows, :] = rest
        gg = rest * bm * gate
        R.bl[at(r0, i), :] = gb.astype(BF)
        R.go2[rows, :] = gg.astype(BF)
        pk[6:7, :] += colsum(gb)
        pk[7:8, :] += colsum(gg)

    send_bl = remote(R.bl.at[own_rows, :], R.bl.at[own_rows, :], partner)
    send_gl2 = remote(R.go2.at[:, their_cols], R.gl2.at[own_rows, :], partner)
    keep_gl2 = local(R.go2.at[:, mine_cols], R.gl2.at[own_rows, :], 4)
    keep_gl2.start()
    back_o = remote(R.outb, R.o_out, cross, keep=False)
    keep_o = local(R.outb, R.o_out, 5)

    @pl.when(jnp.logical_not(swap))
    def _():
        keep_o.start()

    def hidden_back(base):
        for z in range(4):
            def step(i, acc, z=z):
                rows = at(base, i)
                gpre = mmt(R.bl[rows, :], dnz[z]) * R.gp[z, rows, :].astype(F32)
                R.gp[z, rows, :] = gpre.astype(BF)
                return acc + colsum(gpre)

            both = lax.fori_loop(0, 2, step, jnp.zeros((1, 256), F32))
            pk[8 + z : 9 + z, 0:256] += jnp.where(c == 0, both, 0.0)
            pk[8 + z : 9 + z, 256:512] += jnp.where(c == 0, 0.0, both)

    def norm_two_part(rows):
        total = mmt(R.gp[0, rows, :], upz[0])
        for z in range(1, 4):
            total = total + mmt(R.gp[z, rows, :], upz[z])
        return total

    def halving(block, buf, dev_a, dev_b, a, b, store):
        f32 = lambda ref: ref[...].astype(F32)
        one = [
            remote(block(a ^ b, 0), buf.at[0], dev_a), remote(block(a ^ b, 1), buf.at[1], dev_b),
            remote(block(a, 0), buf.at[2], dev_a), remote(block(b, 1), buf.at[3], dev_b),
        ]
        yield
        arrived(one[0:2])
        buf[6] = (f32(block(b, 0)) + f32(buf.at[0])).astype(BF)
        buf[7] = (f32(block(a, 1)) + f32(buf.at[1])).astype(BF)
        two = [remote(buf.at[6], buf.at[4], dev_b), remote(buf.at[7], buf.at[5], dev_a)]
        yield
        arrived(one[2:4] + two)
        store(0, (f32(block(0, 0)) + f32(buf.at[2]) + f32(buf.at[4])).astype(BF))
        store(1, (f32(block(0, 1)) + f32(buf.at[3]) + f32(buf.at[5])).astype(BF))

    def exchange(total, buf, dtype):
        for b in range(xbits):
            buf[2 * b] = total.astype(dtype)
            copy = remote(buf.at[2 * b], buf.at[2 * b + 1], (dpx(8 << b), m))
            copy.wait_recv()
            total = buf[2 * b].astype(F32) + buf[2 * b + 1].astype(F32)
        return total

    def chips(out):
        copies = [remote(out.at[slot], out.at[slot], (dpx(2 * k), m)) for k in (1, 2, 3)]
        yield
        arrived(copies)

    def chips_both(out):
        size = out.shape[1] // 2
        low, high = pl.ds(0, size), pl.ds(size, size)
        other = c * 4 + gx(2)
        pair = ds(c * 4 + 2 * bits[2], 2)
        copies = [
            remote(out.at[slot, low], out.at[slot, low], chip_x),
            remote(out.at[slot, high], out.at[slot, high], chip_y),
        ]
        yield
        arrived(copies)
        copies = [
            remote(out.at[pair, low], out.at[pair, low], chip_y),
            remote(out.at[slot, high], out.at[slot, high], chip_x),
            remote(out.at[other, high], out.at[other, high], chip_x),
        ]
        yield
        arrived(copies)

    def cores(out):
        return [remote(out.at[ds(c * 4, 4)], out.at[ds(c * 4, 4)], partner)]

    def finish(out, total, route=chips_both):
        out[slot] = total.astype(BF)
        yield from route(out)
        copies = cores(out)
        yield
        arrived(copies)
        yield

    def finish_all(out, total):
        out[slot, m] = total.astype(BF)
        copies = [remote(out.at[slot, m], out.at[slot, m], (dp, mx(k))) for k in (1, 2, 3)]
        yield
        arrived(copies)
        yield from chips_both(out)
        copies = cores(out)
        yield
        arrived(copies)
        yield

    def over_mp(b_ref, c_ref):
        return [remote(b_ref.at[mx(k)], c_ref.at[k - 1], (dp, mx(k))) for k in (1, 2, 3)]

    def plane_first(s_ref, h_ref, b_ref, c_ref, x_ref, quarter, end, out):
        def block(k, half):
            return s_ref.at[2 * half : 2 * half + 2, ds(gx(k) * quarter, quarter), :]

        def store(half, value):
            b_ref[2 * half : 2 * half + 2] = value

        yield from halving(block, h_ref, chip_x, chip_y, 1, 2, store)
        copies = over_mp(b_ref, c_ref)
        yield True
        arrived(copies)
        total = b_ref[m].astype(F32)
        for k in range(3):
            total = total + c_ref[k].astype(F32)
        yield from end(out, exchange(total, x_ref, BF))

    def block_sum(name, k, quarter, out, route):
        s_ref, h_ref = getattr(R, name + "_s"), getattr(R, name + "_h").at[k]
        b_ref, c_ref = getattr(R, name + "_b"), getattr(R, name + "_c")
        half_rows = quarter // 2

        def block(kk, half):
            return s_ref.at[mx(k), ds(gx(kk) * quarter + half * half_rows, half_rows), :]

        def store(half, value):
            b_ref[k, half * half_rows : half * half_rows + half_rows] = value

        yield from halving(block, h_ref, chip_x, chip_y, 1, 2, store)
        if k:
            waiting.setdefault(name, []).append(remote(b_ref.at[k], c_ref.at[k - 1], (dp, mx(k))))
            return
        yield True
        arrived(waiting[name])
        total = b_ref[0].astype(F32)
        for j in range(3):
            total = total + c_ref[j].astype(F32)
        yield from finish(out, exchange(total, extra(name + "_x"), BF), route)

    waiting, queue, late = {}, [], []

    def begin(steps):
        next(steps)
        queue.append(steps)

    def advance(source):
        steps = source.pop(0)
        for last in steps:
            (late if last or source is late else queue).append(steps)
            break

    def pump(count):
        for _ in range(min(count, len(queue))):
            advance(queue)

    def pump_late(count):
        for _ in range(min(count, len(late))):
            advance(late)

    extra = lambda name: getattr(R, name, None)
    sum_e = plane_first(R.e_s, R.e_h, R.e_b, R.e_c, extra("e_x"), 32, finish_all, R.o_g2)
    sum_f = plane_first(R.f_s, R.f_h, R.f_b, R.f_c, extra("f_x"), 32, finish_all, R.o_g1)
    far_first = (3, 2, 1, 0)

    hidden_back(r0)
    send_bl.wait_recv()
    for k in far_first:
        R.d_s[mx(k)] = tmm(R.hid[mx(k)], R.bl[...]).astype(BF)
        begin(block_sum("d", k, 64, R.o_d, chips_both))
    hidden_back(p0)
    n2t = n2[...].T
    for k in far_first:
        R.u_s[mx(k)] = mm(n2t, R.gp[mx(k)]).astype(BF)
        begin(block_sum("u", k, 128, R.o_u, chips_both))
        pump(1)
    send_gl2.wait_recv()
    keep_gl2.wait()
    full = mm(n2t, R.gl2[...]).astype(BF)
    for z in range(4):
        R.e_s[z] = full[z * 128 : z * 128 + 128, :]
    begin(sum_e)

    send_d2 = hand_over(lambda i: norm_two_part(at(p0, i)))

    @chunks
    def _(i):
        R.gmr[at(0, i), :] = norm_two_part(at(r0, i))

    pump(2)
    wait_all(send_d2)

    @chunks
    def _(i):
        rows = at(0, i)
        gn = R.gmr[rows, :] + R.xr[rows, :].astype(F32) + mmt(R.go2[rows, :], R.wg2v[...])
        xh = R.xh2[rows, :]
        pk[4:5, :] += colsum(gn * xh)
        pk[5:6, :] += colsum(gn)
        e = gn * R.n2g[...]
        gm = R.rs2[rows, 0:1] * (e - rowmean(e) - xh * rowmean(e * xh)) + R.mid[rows, :]
        gate = R.g1[rows, :]
        ga = gate * gm
        gg = (gm - ga) * R.amx[rows, :] * gate
        R.mid[rows, :] = gm - ga
        R.al[at(r0, i), :] = ga.astype(BF)
        R.go1[rows, :] = gg.astype(BF)
        pk[2:3, :] += colsum(ga)
        pk[3:4, :] += colsum(gg)

    send_al = remote(R.al.at[own_rows, :], R.al.at[own_rows, :], partner)
    send_gl1 = remote(R.go1.at[:, their_cols], R.gl1.at[own_rows, :], partner)
    keep_gl1 = local(R.go1.at[:, mine_cols], R.gl1.at[own_rows, :], 6)
    keep_gl1.start()
    n1t = n1[...].T
    send_al.wait_recv()

    @pl.loop(0, 4)
    def _(i):
        rows = at(0, i)
        R.dct[:, rows] = mmt(R.wo[...], R.al[rows, :]).astype(BF)

    pump(3)
    grad_wo = mm(R.ctxt[...], R.al[...]).astype(BF)
    for z in range(4):
        R.a_s[z, 192:256, :] = grad_wo[z * 64 : z * 64 + 64, :]
    send_gl1.wait_recv()
    keep_gl1.wait()
    full = mm(n1t, R.gl1[...]).astype(BF)
    for z in range(4):
        R.f_s[z] = full[z * 128 : z * 128 + 128, :]

    begin(sum_f)
    pump(2)

    @pl.when(swap)
    def _():
        back_o.start()

    dkt, dvt, dt = R.dkt, R.dvt, R.dt

    for k in far_first:
        z = mx(k)
        dkt[...] = jnp.zeros((64, S), F32)
        dvt[...] = jnp.zeros((64, S), F32)
        mine_rows = ds(z * 64, 64)

        def dt_rows(start, size, z=z):
            return pl.ds(pl.multiple_of(z * 192 + start, 32), size)

        for i in range(4):
            j0, width = span(i)
            rows, keys = slice(i * CH, (i + 1) * CH), slice(j0, j0 + width)
            p = R.pr[z, :, lead(i) : lead(i) + width]
            pf = p.astype(F32)
            t = tmm(R.dct[mine_rows, rows], R.vt[z, :, keys]) * pf
            part = (t - pf * jnp.sum(t, axis=-1, keepdims=True)).astype(BF)
            dvt[:, keys] += mm(R.dct[mine_rows, rows], p)
            dkt[:, keys] += mm(R.qt[z, :, rows], part)
            dq = mmt(R.kt[z, :, keys], part) * 0.125
            a, b = dq[0:32], dq[32:64]
            cc, sn = R.cttb[:, rows], R.sttb[:, rows]
            dt[dt_rows(0, 32), rows] = (a * cc + b * sn).astype(BF)
            dt[dt_rows(32, 32), rows] = (b * cc - a * sn).astype(BF)
            pump(1)
            if k == 0:
                pump_late(1)
        a, b = dkt[0:32, :], dkt[32:64, :]
        cc, sn = R.cttb[...], R.sttb[...]
        dt[dt_rows(64, 32), :] = (a * cc + b * sn).astype(BF)
        dt[dt_rows(96, 32), :] = (b * cc - a * sn).astype(BF)
        dt[dt_rows(128, 64), :] = dvt[...].astype(BF)
        R.a_s[z, 0:192, :] = mm(dt[dt_rows(0, 192), :], n1[...]).astype(BF)
        begin(block_sum("a", k, 64, R.o_a, chips))

    send_d1 = hand_over(lambda i: tmm(dt[:, at(p0, i)], R.wh[...]))
    pump(3)

    @chunks
    def _(i):
        R.gmr[at(0, i), :] = tmm(dt[:, at(r0, i)], R.wh[...])

    pump(3)
    wait_all(send_d1)

    def norm_one_back(i):
        rows = slice(i * CH, i * CH + CH)
        gn = R.gmr[rows, :] + R.xr[rows, :].astype(F32) + mmt(R.go1[rows, :], R.wg1v[...])
        xh = R.xh1[rows, :]
        pk[0:1, :] += colsum(gn * xh)
        pk[1:2, :] += colsum(gn)
        e = gn * R.n1g[...]
        grad = R.rs1[rows, 0:1] * (e - rowmean(e) - xh * rowmean(e * xh)) + R.mid[rows, :]
        R.gtb[rows, :] = grad.astype(BF)

    back_t, keep_t = [], []
    for i in range(2):
        norm_one_back(i)
        rows = slice(i * CH, i * CH + CH)
        back_t.append(remote(R.gtb.at[rows, :], R.o_gt.at[rows, :], cross, keep=False))
        keep_t.append(local(R.gtb.at[rows, :], R.o_gt.at[rows, :], 7 + i))

        @pl.when(swap)
        def _():
            back_t[i].start()

        @pl.when(jnp.logical_not(swap))
        def _():
            keep_t[i].start()

    pk1, pk2, pk3 = R.pk1, R.pk2, R.pk3
    pk1[c] = pk[...]
    p_1 = remote(pk1.at[c], pk1.at[c], partner)
    pump(2)
    pump_late(4)
    p_1.wait_recv()
    pk2[g] = pk1[0] + pk1[1]
    p_2 = [remote(pk2.at[g], pk2.at[g], (dpx(2 * k), m)) for k in (1, 2, 3)]
    pump(4)
    pump_late(5)
    arrived(p_2)
    pk3[m] = (pk2[0] + pk2[1]) + (pk2[2] + pk2[3])
    p_3 = [remote(pk3.at[m], pk3.at[m], (dp, mx(k))) for k in (1, 2, 3)]
    pump_late(5)
    arrived(p_3)
    total = exchange((pk3[0] + pk3[1]) + (pk3[2] + pk3[3]), extra("p_x"), F32)
    pk[...] = total
    R.o_vec[...] = total
    R.o_vec[8:9, :] = pk[pl.ds(8 + m, 1), :]
    while late:
        pump_late(1)

    for copy in unsent:
        copy.wait_send()

    @pl.when(swap)
    def _():
        for copy in (back_o, *back_t):
            copy.wait()

    @pl.when(jnp.logical_not(swap))
    def _():
        for copy in (keep_o, *keep_t):
            copy.wait()


def unpack(a, u, d, g1, g2, vec, out, gt, *outs):
    (oq, ok, ov, oo, ou, od, og1, og2, oout, ogt) = outs[:10]
    for j, ref in enumerate((oq, ok, ov)):
        both = jnp.concatenate([a[j].astype(F32), a[4 + j].astype(F32)], axis=0)
        ref[...] = both.T
    for c in range(2):
        oo[c * 64 : c * 64 + 64, :] = a[4 * c + 3].astype(F32)
        for g in range(4):
            ou[g * 128 : g * 128 + 128, c * 256 : c * 256 + 256] = u[4 * c + g].astype(F32)
            od[c * 256 + g * 64 : c * 256 + g * 64 + 64, :] = d[4 * c + g].astype(F32)
            for z in range(4):
                rows = slice(z * 128 + g * 32, z * 128 + g * 32 + 32)
                og1[rows, c * 256 : c * 256 + 256] = g1[4 * c + g, z].astype(F32)
                og2[rows, c * 256 : c * 256 + 256] = g2[4 * c + g, z].astype(F32)
    oout[...] = out[...]
    ogt[...] = gt[...].astype(F32)
    for j, ref in enumerate(outs[10:]):
        ref[...] = vec[j : j + 1, :]


def tables():
    freqs = np.exp(np.arange(HD // 2, dtype=np.float32) * np.float32(-2.0 * math.log(10000.0) / HD))
    angles = np.arange(S, dtype=np.float32)[:, None] * freqs.astype(np.float32)
    angles = angles.T.astype(np.float64)
    return np.cos(angles).astype(np.float32), np.sin(angles).astype(np.float32)


def shards(
    ndp, tokens, doc_ids, resets, n1g, n1b, qw, kw, vw, ow, ob, wg1, g1b, n2g, n2b, up, ub, down, db,
    wg2, g2b, cot,
):
    xbits = ndp.bit_length() - 4
    ctab, stab = tables()
    vector = lambda v: v.reshape(1, -1)
    values = dict(
        tokens=tokens, cot=cot, docs=doc_ids, resets=resets.reshape(1, 2), qw=qw, kw=kw, vw=vw, ow=ow,
        wg1=wg1, up=up, down=down, wg2=wg2, n1g=vector(n1g), n1b=vector(n1b), ob=vector(ob),
        g1b=vector(g1b), n2g=vector(n2g), n2b=vector(n2b), ub=vector(ub), db=vector(db), g2b=vector(g2b),
        ctab=jnp.asarray(ctab), stab=jnp.asarray(stab),
    )
    vmem = pl.BlockSpec(memory_space=pltpu.VMEM)
    anyspace = pl.BlockSpec(memory_space=pl.ANY)
    scratch = {name: pltpu.VMEM(shape, dtype) for name, (shape, dtype) in SCRATCH.items()}
    if xbits:
        more = dict(a_x=(64, 512), u_x=(128, 256), d_x=(64, 512), e_x=(32, 256), f_x=(32, 256))
        for name, shape in more.items():
            scratch[name] = pltpu.VMEM((2 * xbits,) + shape, BF)
        scratch.update(p_x=pltpu.VMEM((2 * xbits, 16, 512), F32))
    copies = pltpu.SemaphoreType.DMA((NCOPY + 6 * xbits,))
    scratch.update(
        ss=copies, rs=copies, ls=pltpu.SemaphoreType.DMA((13,))
    )
    in_specs = dict.fromkeys(values, vmem)
    in_specs.update(tokens=anyspace, cot=anyspace, up=anyspace, down=anyspace)
    in_specs.update(wg1=anyspace, wg2=anyspace)
    packed = pl.pallas_call(
        functools.partial(kernel, ndp, xbits, (*values, *OUT_SHAPES, *scratch)),
        out_shape=[jax.ShapeDtypeStruct(shape, dtype) for shape, dtype in OUT_SHAPES.values()],
        in_specs=list(in_specs.values()),
        out_specs=[vmem] * len(OUT_SHAPES),
        scratch_shapes=list(scratch.values()),
        compiler_params=pltpu.CompilerParams(
            collective_id=0, has_side_effects=True, vmem_limit_bytes=64 << 20
        ),
        name="block",
    )(*values.values())
    out, gt, a, u, d, g1, g2, vec = packed
    f32 = lambda *shape: jax.ShapeDtypeStruct(shape, F32)
    shapes = [f32(D, 128)] * 3 + [f32(128, D)] + [f32(D, D)] * 4
    shapes += [jax.ShapeDtypeStruct((T, D), BF), f32(T, D)] + [f32(1, D)] * 9
    res = pl.pallas_call(
        unpack,
        out_shape=shapes,
        in_specs=[vmem] * 8,
        out_specs=[vmem] * len(shapes),
        compiler_params=pltpu.CompilerParams(vmem_limit_bytes=63 << 20),
        name="unpack",
    )(a, u, d, g1, g2, vec, out, gt)
    gq, gk, gv, go, gu, gd, gg1, gg2, out, gt = res[:10]
    rn1g, rn1b, rob, rg1b, rn2g, rn2b, rdb, rg2b, rub = [v.reshape(-1) for v in res[10:]]
    return (
        out, gt, rn1g, rn1b, gq, gk, gv, go, rob, gg1, rg1b, rn2g, rn2b, gu, rub, gd, rdb, gg2, rg2b,
    )


def solution(mesh):
    both, rep = P(("dp", "mp"), None), P()
    cols, rows = P(None, "mp"), P("mp", None)
    in_specs = (
        both, P("dp", None), P("dp"), rep, rep, cols, cols, cols, rows, rep, rep, rep, rep, rep, cols,
        P("mp"), rows, rep, rep, rep, both,
    )
    out_specs = (
        both, both, rep, rep, cols, cols, cols, rows, rep, rep, rep, rep, rep, cols, P("mp"), rows, rep,
        rep, rep,
    )
    fn = functools.partial(shards, mesh.shape["dp"])
    return jax.shard_map(fn, mesh=mesh, in_specs=in_specs, out_specs=out_specs, check_vma=False)
```

```python
import functools
import math
from types import SimpleNamespace

import jax
import jax.numpy as jnp
import numpy as np
from jax import lax
from jax.experimental import pallas as pl
from jax.experimental.pallas import tpu as pltpu
from jax.sharding import PartitionSpec as P

BF = jnp.bfloat16
F32 = jnp.float32
MESH = pl.DeviceIdType.MESH
D = 512
T = 512
S = 1024
HD = 64
CH = 256
NCOPY = 256
IN = "in_"
BIG = ("tokens", "cot", "up", "down", "wg1", "wg2")
GELU_A = math.sqrt(2.0 / math.pi)
GELU_B = 0.044715


def mm(a, b):
    return lax.dot_general(a, b, (((1,), (0,)), ((), ())), preferred_element_type=F32)


def mmt(a, b):
    return lax.dot_general(a, b, (((1,), (1,)), ((), ())), preferred_element_type=F32)


def tmm(a, b):
    return lax.dot_general(a, b, (((0,), (0,)), ((), ())), preferred_element_type=F32)


def sigmoid(v):
    return 0.5 * jnp.tanh(0.5 * v) + 0.5


def colsum(v):
    return jnp.sum(v, axis=0, keepdims=True)


def rowmean(v):
    return jnp.mean(v, axis=-1, keepdims=True)


OUT_SHAPES = dict(
    o_out=((T, D), BF),
    o_gt=((T, D), BF),
    o_a=((8, 64, 512), BF),
    o_u=((8, 128, 256), BF),
    o_d=((8, 64, 512), BF),
    o_g1=((8, 4, 32, 256), BF),
    o_g2=((8, 4, 32, 256), BF),
    o_vec=((16, 512), F32),
)

SCRATCH = dict(
    xt=((T, D), BF), ct=((T, D), BF),
    info=((2, 8, S), F32), dcol=((S, 128), F32), drow=((8, S), F32),
    cttb=((32, S), F32), sttb=((32, S), F32),
    wz=((4, 256, 512), BF), wh=((768, 512), BF), wo=((256, 512), BF),
    upz=((4, 512, 256), BF), dnz=((4, 256, 512), BF), ubz=((4, 8, 256), F32),
    n1=((S, D), BF), xh1=((T, D), F32), rs1=((T, 128), F32), g1=((T, D), F32),
    qt=((4, 64, S), BF), kt=((4, 64, S), BF), vt=((4, 64, S), BF),
    bias=((CH, 2304), F32), pr=((4, CH, 2304), BF), ctxt=((256, S), BF),
    xs=((T, D), BF), xr=((T, D), BF), amx=((T, D), F32), mid=((T, D), F32),
    xh2=((T, D), F32), rs2=((T, 128), F32), n2=((S, D), BF),
    hid=((4, S, 256), BF), gp=((4, S, 256), BF), acc=((T, D), F32), outb=((T, D), BF),
    bl=((S, D), BF), go2=((T, D), BF), gl2=((S, 256), BF),
    al=((S, D), BF), go1=((T, D), BF), gl1=((S, 256), BF), gmr=((T, D), F32),
    dct=((256, S), BF),
    dkt=((64, S), F32), dvt=((64, S), F32), dt=((768, S), BF), gtb=((T, D), BF),
    a_s=((4, 256, 512), BF), a_h=((4, 8, 32, 512), BF), a_b=((4, 64, 512), BF), a_c=((3, 64, 512), BF),
    u_s=((4, 512, 256), BF), u_h=((4, 8, 64, 256), BF), u_b=((4, 128, 256), BF), u_c=((3, 128, 256), BF),
    d_s=((4, 256, 512), BF), d_h=((4, 8, 32, 512), BF), d_b=((4, 64, 512), BF), d_c=((3, 64, 512), BF),
    e_s=((4, 128, 256), BF), e_h=((8, 2, 32, 256), BF), e_b=((4, 32, 256), BF), e_c=((3, 32, 256), BF),
    f_s=((4, 128, 256), BF), f_h=((8, 2, 32, 256), BF), f_b=((4, 32, 256), BF), f_c=((3, 32, 256), BF),
    wg1v=((D, D), BF), wg2v=((D, D), BF),
    p_a=((8, 64, 512), BF), p_u=((8, 128, 256), BF), p_d=((8, 64, 512), BF),
    p_g1=((8, 4, 32, 256), BF), p_g2=((8, 4, 32, 256), BF), p_vec=((16, 512), F32),
    pk=((16, 512), F32), pk1=((2, 16, 512), F32), pk2=((4, 16, 512), F32), pk3=((4, 16, 512), F32),
)


def kernel(ndp, xbits, names, *refs):
    R = SimpleNamespace(**dict(zip(names, refs)))
    dp = lax.axis_index("dp")
    m = lax.axis_index("mp")
    bits = [lax.rem(lax.div(dp, 1 << b), 2) for b in range(ndp.bit_length() - 1)]
    c = bits[0]
    g = bits[1] + 2 * bits[2]
    mb = [lax.rem(m, 2), lax.div(m, 2)]

    def flip(value, own, mask):
        for b in range(len(own)):
            if mask >> b & 1:
                value = value + (1 - 2 * own[b]) * (1 << b)
        return value

    dpx = lambda mask: flip(dp, bits, mask)
    mx = lambda mask: flip(m, mb, mask)
    gx = lambda mask: flip(g, bits[1:3], mask)

    def ds(start, size):
        return pl.ds(pl.multiple_of(start, size), size)

    swap = (c + mb[0]) == 1
    r0 = pl.multiple_of(c * T, T)
    p0 = pl.multiple_of(T - c * T, T)
    slot = c * 4 + g
    counter = [0]
    unsent = []

    def remote(src, dst, device, keep=True):
        index = counter[0]
        counter[0] += 1
        copy = pltpu.make_async_remote_copy(
            src_ref=src, dst_ref=dst, send_sem=R.ss.at[index], recv_sem=R.rs.at[index],
            device_id=device, device_id_type=MESH,
        )
        if keep:
            copy.start()
            unsent.append(copy)
        return copy

    def local(src, dst, index):
        return pltpu.make_async_copy(src, dst, R.ls.at[index])

    def arrived(copies):
        for copy in copies:
            copy.wait_recv()

    partner = (dpx(1), m)
    cross = (dpx(1), mx(1))
    chip_x, chip_y = (dpx(2), m), (dpx(4), m)
    near, far = (dp, mx(1)), (dp, mx(3))
    own_rows = pl.ds(r0, T)
    mine_cols = ds(c * 256, 256)
    their_cols = ds(256 - c * 256, 256)

    barrier = pltpu.get_barrier_semaphore()
    friends = [partner, (dpx(2), m), (dpx(4), m), (dpx(6), m)] + [(dp, mx(k)) for k in (1, 2, 3)] + [cross]
    friends += [(dpx(1 << b), m) for b in range(3, 3 + xbits)]
    for friend in friends:
        pl.semaphore_signal(barrier, inc=1, device_id=friend, device_id_type=MESH)
    wz, upz, dnz = R.wz, R.upz, R.dnz
    loads = [
        local(src, dst, 9 + i)
        for i, (src, dst) in enumerate(((R.wg1, R.wg1v), (R.wg2, R.wg2v)))
    ]
    for copy in loads:
        copy.start()
    small = [name for name in names if hasattr(R, IN + name)]
    enter = [
        pltpu.make_async_copy(getattr(R, name), getattr(R, IN + name), R.ins.at[i])
        for i, name in enumerate(small)
    ]
    for name, copy in zip(small, enter):
        copy.start()
        setattr(R, name, getattr(R, IN + name))
    own_up = local(R.up.at[:, mine_cols], upz.at[m], 0)
    own_dn = local(R.down.at[ds(c * 256, 256), :], dnz.at[m], 1)
    own_up.start()
    own_dn.start()
    loc_x = local(R.tokens, R.xt, 2)
    loc_c = local(R.cot, R.ct, 3)

    @pl.when(jnp.logical_not(swap))
    def _():
        loc_x.start()
        loc_c.start()

    for copy in enter:
        copy.wait()

    lane = lax.broadcasted_iota(jnp.int32, (64, 128), 1)
    pick = lane == lax.broadcasted_iota(jnp.int32, (64, 128), 0) + c * 64
    pick = jnp.where(pick, 1.0, 0.0).astype(BF)
    wz[m, 0:64, :] = mmt(pick, R.qw[...]).astype(BF)
    wz[m, 64:128, :] = mmt(pick, R.kw[...]).astype(BF)
    wz[m, 128:192, :] = mmt(pick, R.vw[...]).astype(BF)
    wz[m, 192:256, :] = R.ow[ds(c * 64, 64), :]
    ubv = R.ub[...]
    ubv = jnp.where(c == 0, ubv[:, :256], ubv[:, 256:])
    R.ubz[m] = jnp.broadcast_to(ubv, (8, 256))
    info = R.info
    turn = jnp.where(
        lax.broadcasted_iota(jnp.int32, (2, 128), 0) == 0, R.resets[0:1, 0:1], R.resets[0:1, 1:2]
    ).astype(F32)
    info[0] = jnp.zeros((8, S), F32)
    info[0, 0:2, :] = R.docs[...].astype(F32)
    info[0, 2:4, 0:128] = turn

    pl.semaphore_wait(barrier, len(friends))

    swap_x = remote(R.tokens, R.xt, cross, keep=False)
    swap_c = remote(R.cot, R.ct, cross, keep=False)

    near_first = (1, 2, 3)

    def gather(z, rows, lanes):
        quarter = rows // 4
        part = ds(g * quarter, quarter)
        pair = ds(bits[2] * 2 * quarter, 2 * quarter)
        other = ds(gx(2) * quarter, quarter)
        low, high = pl.ds(0, lanes // 2), pl.ds(lanes // 2, lanes // 2)

        def send(block, part, lanes, device):
            return remote(z.at[block, part, lanes], z.at[block, part, lanes], device)

        lines = [send(m, part, pl.ds(0, lanes), (dp, mx(k))) for k in near_first]
        yield
        one, two = [], []
        for k, line in zip(near_first, lines):
            line.wait_recv()
            one.append([send(mx(k), part, low, chip_x), send(mx(k), part, high, chip_y)])
            yield
        for k, copies in zip(near_first, one):
            arrived(copies)
            two.append([
                send(mx(k), pair, low, chip_y), send(mx(k), part, high, chip_x),
                send(mx(k), other, high, chip_x),
            ])
            yield
        for copies in two:
            arrived(copies)
            yield

    def go(steps, count):
        for _ in range(count):
            next(steps)

    get_w, get_u, get_d = gather(wz, 256, 512), gather(upz, 512, 256), gather(dnz, 256, 512)
    next(get_w)

    @pl.when(swap)
    def _():
        swap_x.start()

    own_up.wait()
    next(get_u)
    own_dn.wait()
    next(get_d)

    @pl.when(swap)
    def _():
        swap_c.start()

    send_info = remote(info.at[0], info.at[1], partner)
    ub_copies = [remote(R.ubz.at[m], R.ubz.at[m], (dp, mx(k))) for k in (1, 2, 3)]

    send_info.wait_recv()
    for copy in loads:
        copy.wait()
    row = mb[1]
    mine = jnp.where(swap, 0.0, 1.0)

    def info_row(i):
        return info[0, pl.ds(i, 1), :] * mine + info[1, pl.ds(i, 1), :] * (1.0 - mine)

    doc = info_row(row)
    turn = info_row(row + 2)[:, 0:1]
    R.drow[...] = jnp.broadcast_to(doc, (8, S))
    R.dcol[...] = jnp.broadcast_to(doc, (128, S)).T
    freq = jnp.exp(
        lax.broadcasted_iota(jnp.int32, (32, 1), 0).astype(F32) * (-2.0 * math.log(10000.0) / HD)
    )
    cr, sr = jnp.cos(turn * freq), jnp.sin(turn * freq)
    past = lax.broadcasted_iota(jnp.int32, (1, S), 1).astype(F32) >= turn
    c0, s0 = R.ctab[...], R.stab[...]
    R.cttb[...] = jnp.where(past, c0 * cr + s0 * sr, c0)
    R.sttb[...] = jnp.where(past, s0 * cr - c0 * sr, s0)

    def at(base, i):
        return ds(base + i * CH, CH)

    def chunks(body):
        pl.loop(0, 2)(body)

    go(get_w, 3)

    @pl.when(jnp.logical_not(swap))
    def _():
        loc_x.wait()
        loc_c.wait()

    @pl.when(swap)
    def _():
        swap_x.wait()

    n1 = R.n1

    @chunks
    def _(i):
        rows = at(0, i)
        x = R.xt[rows, :].astype(F32)
        x = x - rowmean(x)
        rstd = lax.rsqrt(rowmean(x * x) + 1e-05)
        xh = x * rstd
        R.xh1[rows, :] = xh
        R.rs1[rows, :] = jnp.broadcast_to(rstd, (CH, 128))
        n1[at(r0, i), :] = (xh * R.n1g[...] + R.n1b[...]).astype(BF)

    send_n1 = remote(n1.at[own_rows, :], n1.at[own_rows, :], partner)
    go(get_w, 3)

    def project(z, base):
        lanes = ds(base, T)
        both = mmt(wz[z, 0:192, :], n1[lanes, :])
        cc, sn = R.cttb[:, lanes], R.sttb[:, lanes]
        for dst, a, b, scale in ((R.qt, both[0:32], both[32:64], 0.125), (R.kt, both[64:96], both[96:128], 1.0)):
            dst[z, 0:32, lanes] = (a * cc - b * sn).astype(BF) * jnp.asarray(scale, BF)
            dst[z, 32:64, lanes] = (b * cc + a * sn).astype(BF) * jnp.asarray(scale, BF)
        R.vt[z, :, lanes] = both[128:192].astype(BF)
        R.wh[ds(z * 192, 192), :] = wz[z, 0:192, :]
        R.wo[ds(z * 64, 64), :] = wz[z, 192:256, :]

    def span(i):
        width = min(i + 1, 3) * CH
        return (i + 1) * CH - width, width

    def lead(i):
        return sum(span(j)[1] for j in range(i))

    def attend(z):
        for i in range(4):
            j0, width = span(i)
            rows, keys = slice(i * CH, (i + 1) * CH), slice(j0, j0 + width)
            here = slice(lead(i), lead(i) + width)
            sc = tmm(R.qt[z, :, rows], R.kt[z, :, keys]) + R.bias[:, here]
            e = jnp.exp(sc - jnp.max(sc, axis=-1, keepdims=True))
            p = (e * (1.0 / jnp.sum(e, axis=-1, keepdims=True))).astype(BF)
            R.pr[z, :, here] = p
            R.ctxt[ds(z * 64, 64), rows] = mmt(R.vt[z, :, keys], p).astype(BF)

    project(m, r0)
    for i in range(4):
        j0, width = span(i)
        dcol = R.dcol[i * CH : (i + 1) * CH, :]
        qi = lax.broadcasted_iota(jnp.int32, (CH, 128), 0) + i * CH
        for w in range(width // 128):
            ki = lax.broadcasted_iota(jnp.int32, (CH, 128), 1) + (j0 + w * 128)
            ok = (dcol == R.drow[0:1, j0 + w * 128 : j0 + w * 128 + 128]) & (ki <= qi)
            R.bias[:, lead(i) + w * 128 : lead(i) + w * 128 + 128] = jnp.where(ok, 0.0, -1e30)
    send_n1.wait_recv()
    go(get_u, 3)
    project(m, p0)
    go(get_d, 3)
    attend(m)

    @chunks
    def _(i):
        gate = mm(n1[at(r0, i), :], R.wg1v[...]) + R.g1b[...]
        R.g1[at(0, i), :] = sigmoid(gate)

    for k in near_first:
        go(get_w, 1)
        project(mx(k), r0)
        project(mx(k), p0)
        if k == 1:
            go(get_u, 3)
        if k == 2:
            go(get_d, 3)
        attend(mx(k))

    def hand_over(body):
        copies = []
        for i in range(2):
            rows = slice(i * CH, i * CH + CH)
            R.xs[rows, :] = body(i).astype(BF)
            copies.append(remote(R.xs.at[rows, :], R.xr.at[rows, :], partner, keep=False))
            copies[i].start()
        return copies

    def wait_all(copies):
        for copy in copies:
            copy.wait()

    send_at = hand_over(lambda i: tmm(R.ctxt[:, at(p0, i)], R.wo[...]))

    @chunks
    def _(i):
        R.amx[at(0, i), :] = tmm(R.ctxt[:, at(r0, i)], R.wo[...])

    wait_all(send_at)
    n2 = R.n2

    @chunks
    def _(i):
        rows = at(0, i)
        x = R.xt[rows, :].astype(F32)
        amx = R.amx[rows, :] + R.xr[rows, :].astype(F32) + R.ob[...] - x
        R.amx[rows, :] = amx
        mid = x + R.g1[rows, :] * amx
        R.mid[rows, :] = mid
        mid = mid - rowmean(mid)
        rstd = lax.rsqrt(rowmean(mid * mid) + 1e-05)
        xh = mid * rstd
        R.xh2[rows, :] = xh
        R.rs2[rows, :] = jnp.broadcast_to(rstd, (CH, 128))
        n2[at(r0, i), :] = (xh * R.n2g[...] + R.n2b[...]).astype(BF)

    send_n2 = remote(n2.at[own_rows, :], n2.at[own_rows, :], partner)
    arrived(ub_copies)

    def up_part(base, z):
        @chunks
        def _(i):
            rows = at(base, i)
            v = mm(n2[rows, :], upz[z]) + R.ubz[z, 0:1, :]
            v2 = v * v
            half = 0.5 * jnp.tanh(v * (GELU_A + (GELU_A * GELU_B) * v2)) + 0.5
            hid = v * half
            R.hid[z, rows, :] = hid.astype(BF)
            slope = half + hid * (1.0 - half) * (2.0 * GELU_A + (6.0 * GELU_A * GELU_B) * v2)
            R.gp[z, rows, :] = slope.astype(BF)

    def down_part(base, dst, z, begin):
        @chunks
        def _(i):
            part = mm(R.hid[z, at(base, i), :], dnz[z])
            dst[at(0, i), :] = part if begin else dst[at(0, i), :] + part

    up_part(r0, m)
    send_n2.wait_recv()
    up_part(p0, m)
    for k in near_first:
        go(get_u, 1)
        up_part(r0, mx(k))
        up_part(p0, mx(k))
    down_part(p0, R.acc, m, True)
    down_part(r0, R.gmr, m, True)
    for k in near_first:
        go(get_d, 1)
        down_part(p0, R.acc, mx(k), False)
        if k == near_first[-1]:
            send_br = hand_over(lambda i: R.acc[i * CH : i * CH + CH, :])
        down_part(r0, R.gmr, mx(k), False)

    @pl.when(swap)
    def _():
        swap_c.wait()

    pk = R.pk
    pk[...] = jnp.zeros((16, 512), F32)
    wait_all(send_br)

    @chunks
    def _(i):
        rows = at(0, i)
        gate = sigmoid(mm(n2[at(r0, i), :], R.wg2v[...]) + R.g2b[...])
        mid = R.mid[rows, :]
        bm = R.gmr[rows, :] + R.xr[rows, :].astype(F32) + R.db[...] - mid
        R.outb[rows, :] = (mid + gate * bm).astype(BF)
        cot = R.ct[rows, :].astype(F32)
        gb = gate * cot
        rest = cot - gb
        R.mid[rows, :] = rest
        gg = rest * bm * gate
        R.bl[at(r0, i), :] = gb.astype(BF)
        R.go2[rows, :] = gg.astype(BF)
        pk[6:7, :] += colsum(gb)
        pk[7:8, :] += colsum(gg)

    send_bl = remote(R.bl.at[own_rows, :], R.bl.at[own_rows, :], partner)
    send_gl2 = remote(R.go2.at[:, their_cols], R.gl2.at[own_rows, :], partner)
    keep_gl2 = local(R.go2.at[:, mine_cols], R.gl2.at[own_rows, :], 4)
    keep_gl2.start()
    back_o = remote(R.outb, R.o_out, cross, keep=False)
    keep_o = local(R.outb, R.o_out, 5)

    @pl.when(jnp.logical_not(swap))
    def _():
        keep_o.start()

    def hidden_back(base):
        for z in range(4):
            def step(i, acc, z=z):
                rows = at(base, i)
                gpre = mmt(R.bl[rows, :], dnz[z]) * R.gp[z, rows, :].astype(F32)
                R.gp[z, rows, :] = gpre.astype(BF)
                return acc + colsum(gpre)

            both = lax.fori_loop(0, 2, step, jnp.zeros((1, 256), F32))
            pk[8 + z : 9 + z, 0:256] += jnp.where(c == 0, both, 0.0)
            pk[8 + z : 9 + z, 256:512] += jnp.where(c == 0, 0.0, both)

    def norm_two_part(rows):
        total = mmt(R.gp[0, rows, :], upz[0])
        for z in range(1, 4):
            total = total + mmt(R.gp[z, rows, :], upz[z])
        return total

    def halving(block, buf, dev_a, dev_b, a, b, store):
        f32 = lambda ref: ref[...].astype(F32)
        one = [
            remote(block(a ^ b, 0), buf.at[0], dev_a), remote(block(a ^ b, 1), buf.at[1], dev_b),
            remote(block(a, 0), buf.at[2], dev_a), remote(block(b, 1), buf.at[3], dev_b),
        ]
        yield
        arrived(one[0:2])
        buf[6] = (f32(block(b, 0)) + f32(buf.at[0])).astype(BF)
        buf[7] = (f32(block(a, 1)) + f32(buf.at[1])).astype(BF)
        two = [remote(buf.at[6], buf.at[4], dev_b), remote(buf.at[7], buf.at[5], dev_a)]
        yield
        arrived(one[2:4] + two)
        store(0, (f32(block(0, 0)) + f32(buf.at[2]) + f32(buf.at[4])).astype(BF))
        store(1, (f32(block(0, 1)) + f32(buf.at[3]) + f32(buf.at[5])).astype(BF))

    def exchange(total, buf, dtype):
        for b in range(xbits):
            buf[2 * b] = total.astype(dtype)
            copy = remote(buf.at[2 * b], buf.at[2 * b + 1], (dpx(8 << b), m))
            copy.wait_recv()
            total = buf[2 * b].astype(F32) + buf[2 * b + 1].astype(F32)
        return total

    def chips(out):
        copies = [remote(out.at[slot], out.at[slot], (dpx(2 * k), m)) for k in (1, 2, 3)]
        yield
        arrived(copies)

    def chips_both(out):
        size = out.shape[1] // 2
        low, high = pl.ds(0, size), pl.ds(size, size)
        other = c * 4 + gx(2)
        pair = ds(c * 4 + 2 * bits[2], 2)
        copies = [
            remote(out.at[slot, low], out.at[slot, low], chip_x),
            remote(out.at[slot, high], out.at[slot, high], chip_y),
        ]
        yield
        arrived(copies)
        copies = [
            remote(out.at[pair, low], out.at[pair, low], chip_y),
            remote(out.at[slot, high], out.at[slot, high], chip_x),
            remote(out.at[other, high], out.at[other, high], chip_x),
        ]
        yield
        arrived(copies)

    def cores(out):
        return [remote(out.at[ds(c * 4, 4)], out.at[ds(c * 4, 4)], partner)]

    def flush(buf):
        copy = local(buf, homes[id(buf)], 12 + len(flushed))
        copy.start()
        flushed.append(copy)

    flushed = []
    homes = {
        id(R.p_a): R.o_a, id(R.p_u): R.o_u, id(R.p_d): R.o_d, id(R.p_g1): R.o_g1, id(R.p_g2): R.o_g2,
        id(R.p_vec): R.o_vec,
    }

    def finish(out, total, route=chips_both):
        out[slot] = total.astype(BF)
        yield from route(out)
        copies = cores(out)
        yield
        arrived(copies)
        flush(out)

    def finish_all(out, total):
        out[slot, m] = total.astype(BF)
        copies = [remote(out.at[slot, m], out.at[slot, m], (dp, mx(k))) for k in (1, 2, 3)]
        yield
        arrived(copies)
        yield from chips_both(out)
        copies = cores(out)
        yield
        arrived(copies)
        flush(out)

    def over_mp(b_ref, c_ref):
        return [remote(b_ref.at[mx(k)], c_ref.at[k - 1], (dp, mx(k))) for k in (1, 2, 3)]

    def plane_first(s_ref, h_ref, b_ref, c_ref, x_ref, quarter, end, out):
        def block(k, half):
            return s_ref.at[2 * half : 2 * half + 2, ds(gx(k) * quarter, quarter), :]

        def store(half, value):
            b_ref[2 * half : 2 * half + 2] = value

        yield from halving(block, h_ref, chip_x, chip_y, 1, 2, store)
        copies = over_mp(b_ref, c_ref)
        yield True
        arrived(copies)
        total = b_ref[m].astype(F32)
        for k in range(3):
            total = total + c_ref[k].astype(F32)
        yield from end(out, exchange(total, x_ref, BF))

    def block_sum(name, k, quarter, out, route):
        s_ref, h_ref = getattr(R, name + "_s"), getattr(R, name + "_h").at[k]
        b_ref, c_ref = getattr(R, name + "_b"), getattr(R, name + "_c")
        half_rows = quarter // 2

        def block(kk, half):
            return s_ref.at[mx(k), ds(gx(kk) * quarter + half * half_rows, half_rows), :]

        def store(half, value):
            b_ref[k, half * half_rows : half * half_rows + half_rows] = value

        def direct():
            copies = [
                remote(block(kk, half), h_ref.at[2 * kk - 2 + half], (dpx(2 * kk), m))
                for kk in (1, 2, 3) for half in (0, 1)
            ]
            yield
            arrived(copies)
            for half in (0, 1):
                total = block(0, half)[...].astype(F32)
                for kk in (1, 2, 3):
                    total = total + h_ref[2 * kk - 2 + half].astype(F32)
                store(half, total.astype(BF))

        if name == "a" and k == 0:
            yield from direct()
        else:
            yield from halving(block, h_ref, chip_x, chip_y, 1, 2, store)
        if k:
            waiting.setdefault(name, []).append(remote(b_ref.at[k], c_ref.at[k - 1], (dp, mx(k))))
            return
        yield True
        arrived(waiting[name])
        total = b_ref[0].astype(F32)
        for j in range(3):
            total = total + c_ref[j].astype(F32)
        yield from finish(out, exchange(total, extra(name + "_x"), BF), route)

    waiting, queue, late = {}, [], []

    def begin(steps):
        next(steps)
        queue.append(steps)

    def advance(source):
        steps = source.pop(0)
        for last in steps:
            (late if last or source is late else queue).append(steps)
            break

    def pump(count):
        for _ in range(min(count, len(queue))):
            advance(queue)

    def pump_late(count):
        for _ in range(min(count, len(late))):
            advance(late)

    extra = lambda name: getattr(R, name, None)
    sum_e = plane_first(R.e_s, R.e_h, R.e_b, R.e_c, extra("e_x"), 32, finish_all, R.p_g2)
    sum_f = plane_first(R.f_s, R.f_h, R.f_b, R.f_c, extra("f_x"), 32, finish_all, R.p_g1)
    far_first = (3, 2, 1, 0)

    hidden_back(r0)
    send_bl.wait_recv()
    for k in far_first:
        R.d_s[mx(k)] = tmm(R.hid[mx(k)], R.bl[...]).astype(BF)
        begin(block_sum("d", k, 64, R.p_d, chips_both))
    hidden_back(p0)
    n2t = n2[...].T
    for k in far_first:
        R.u_s[mx(k)] = mm(n2t, R.gp[mx(k)]).astype(BF)
        begin(block_sum("u", k, 128, R.p_u, chips_both))
        pump(1)
    send_gl2.wait_recv()
    keep_gl2.wait()
    full = mm(n2t, R.gl2[...]).astype(BF)
    for z in range(4):
        R.e_s[z] = full[z * 128 : z * 128 + 128, :]
    begin(sum_e)

    send_d2 = hand_over(lambda i: norm_two_part(at(p0, i)))

    @chunks
    def _(i):
        R.gmr[at(0, i), :] = norm_two_part(at(r0, i))

    pump(2)
    wait_all(send_d2)

    @chunks
    def _(i):
        rows = at(0, i)
        gn = R.gmr[rows, :] + R.xr[rows, :].astype(F32) + mmt(R.go2[rows, :], R.wg2v[...])
        xh = R.xh2[rows, :]
        pk[4:5, :] += colsum(gn * xh)
        pk[5:6, :] += colsum(gn)
        e = gn * R.n2g[...]
        gm = R.rs2[rows, 0:1] * (e - rowmean(e) - xh * rowmean(e * xh)) + R.mid[rows, :]
        gate = R.g1[rows, :]
        ga = gate * gm
        gg = (gm - ga) * R.amx[rows, :] * gate
        R.mid[rows, :] = gm - ga
        R.al[at(r0, i), :] = ga.astype(BF)
        R.go1[rows, :] = gg.astype(BF)
        pk[2:3, :] += colsum(ga)
        pk[3:4, :] += colsum(gg)

    send_al = remote(R.al.at[own_rows, :], R.al.at[own_rows, :], partner)
    send_gl1 = remote(R.go1.at[:, their_cols], R.gl1.at[own_rows, :], partner)
    keep_gl1 = local(R.go1.at[:, mine_cols], R.gl1.at[own_rows, :], 6)
    keep_gl1.start()
    n1t = n1[...].T
    send_al.wait_recv()

    @pl.loop(0, 4)
    def _(i):
        rows = at(0, i)
        R.dct[:, rows] = mmt(R.wo[...], R.al[rows, :]).astype(BF)

    pump(3)
    grad_wo = mm(R.ctxt[...], R.al[...]).astype(BF)
    for z in range(4):
        R.a_s[z, 192:256, :] = grad_wo[z * 64 : z * 64 + 64, :]
    send_gl1.wait_recv()
    keep_gl1.wait()
    full = mm(n1t, R.gl1[...]).astype(BF)
    for z in range(4):
        R.f_s[z] = full[z * 128 : z * 128 + 128, :]

    begin(sum_f)
    pump(2)

    @pl.when(swap)
    def _():
        back_o.start()

    dkt, dvt, dt = R.dkt, R.dvt, R.dt

    for k in far_first:
        z = mx(k)
        dkt[...] = jnp.zeros((64, S), F32)
        dvt[...] = jnp.zeros((64, S), F32)
        mine_rows = ds(z * 64, 64)

        def dt_rows(start, size, z=z):
            return pl.ds(pl.multiple_of(z * 192 + start, 32), size)

        for i in range(4):
            j0, width = span(i)
            rows, keys = slice(i * CH, (i + 1) * CH), slice(j0, j0 + width)
            p = R.pr[z, :, lead(i) : lead(i) + width]
            pf = p.astype(F32)
            t = tmm(R.dct[mine_rows, rows], R.vt[z, :, keys]) * pf
            part = (t - pf * jnp.sum(t, axis=-1, keepdims=True)).astype(BF)
            dvt[:, keys] += mm(R.dct[mine_rows, rows], p)
            dkt[:, keys] += mm(R.qt[z, :, rows], part)
            dq = mmt(R.kt[z, :, keys], part) * 0.125
            a, b = dq[0:32], dq[32:64]
            cc, sn = R.cttb[:, rows], R.sttb[:, rows]
            dt[dt_rows(0, 32), rows] = (a * cc + b * sn).astype(BF)
            dt[dt_rows(32, 32), rows] = (b * cc - a * sn).astype(BF)
            if i >= 4 - (4, 3, 3, 2)[3 - k]:
                pump(1)
            if k == 0:
                pump_late(1)
        a, b = dkt[0:32, :], dkt[32:64, :]
        cc, sn = R.cttb[...], R.sttb[...]
        dt[dt_rows(64, 32), :] = (a * cc + b * sn).astype(BF)
        dt[dt_rows(96, 32), :] = (b * cc - a * sn).astype(BF)
        dt[dt_rows(128, 64), :] = dvt[...].astype(BF)
        R.a_s[z, 0:192, :] = mm(dt[dt_rows(0, 192), :], n1[...]).astype(BF)
        begin(block_sum("a", k, 64, R.p_a, chips))

    send_d1 = hand_over(lambda i: tmm(dt[:, at(p0, i)], R.wh[...]))
    pump(3)

    @chunks
    def _(i):
        R.gmr[at(0, i), :] = tmm(dt[:, at(r0, i)], R.wh[...])

    pump(3)
    wait_all(send_d1)

    def norm_one_back(i):
        rows = slice(i * CH, i * CH + CH)
        gn = R.gmr[rows, :] + R.xr[rows, :].astype(F32) + mmt(R.go1[rows, :], R.wg1v[...])
        xh = R.xh1[rows, :]
        pk[0:1, :] += colsum(gn * xh)
        pk[1:2, :] += colsum(gn)
        e = gn * R.n1g[...]
        grad = R.rs1[rows, 0:1] * (e - rowmean(e) - xh * rowmean(e * xh)) + R.mid[rows, :]
        R.gtb[rows, :] = grad.astype(BF)

    back_t, keep_t = [], []
    for i in range(2):
        norm_one_back(i)
        rows = slice(i * CH, i * CH + CH)
        back_t.append(remote(R.gtb.at[rows, :], R.o_gt.at[rows, :], cross, keep=False))
        keep_t.append(local(R.gtb.at[rows, :], R.o_gt.at[rows, :], 7 + i))

        @pl.when(swap)
        def _():
            back_t[i].start()

        @pl.when(jnp.logical_not(swap))
        def _():
            keep_t[i].start()

    pk1, pk2, pk3 = R.pk1, R.pk2, R.pk3
    pk1[c] = pk[...]
    p_1 = remote(pk1.at[c], pk1.at[c], partner)
    pump(2)
    pump_late(4)
    p_1.wait_recv()
    pk2[g] = pk1[0] + pk1[1]
    p_2 = [remote(pk2.at[g], pk2.at[g], (dpx(2 * k), m)) for k in (1, 2, 3)]
    pump(4)
    pump_late(5)
    arrived(p_2)
    pk3[m] = (pk2[0] + pk2[1]) + (pk2[2] + pk2[3])
    p_3 = [remote(pk3.at[m], pk3.at[m], (dp, mx(k))) for k in (1, 2, 3)]
    pump_late(5)
    arrived(p_3)
    total = exchange((pk3[0] + pk3[1]) + (pk3[2] + pk3[3]), extra("p_x"), F32)
    pk[...] = total
    R.p_vec[...] = total
    R.p_vec[8:9, :] = pk[pl.ds(8 + m, 1), :]
    flush(R.p_vec)
    while queue or late:
        pump(1)
        pump_late(1)

    for copy in unsent:
        copy.wait_send()
    for copy in flushed:
        copy.wait()

    @pl.when(swap)
    def _():
        for copy in (back_o, *back_t):
            copy.wait()

    @pl.when(jnp.logical_not(swap))
    def _():
        for copy in (keep_o, *keep_t):
            copy.wait()


def unpack(a, u, d, g1, g2, vec, out, gt, *outs):
    (oq, ok, ov, oo, ou, od, og1, og2, oout, ogt) = outs[:10]
    for j, ref in enumerate((oq, ok, ov)):
        both = jnp.concatenate([a[j].astype(F32), a[4 + j].astype(F32)], axis=0)
        ref[...] = both.T
    for c in range(2):
        oo[c * 64 : c * 64 + 64, :] = a[4 * c + 3].astype(F32)
        for g in range(4):
            ou[g * 128 : g * 128 + 128, c * 256 : c * 256 + 256] = u[4 * c + g].astype(F32)
            od[c * 256 + g * 64 : c * 256 + g * 64 + 64, :] = d[4 * c + g].astype(F32)
            for z in range(4):
                rows = slice(z * 128 + g * 32, z * 128 + g * 32 + 32)
                og1[rows, c * 256 : c * 256 + 256] = g1[4 * c + g, z].astype(F32)
                og2[rows, c * 256 : c * 256 + 256] = g2[4 * c + g, z].astype(F32)
    oout[...] = out[...]
    ogt[...] = gt[...].astype(F32)
    for j, ref in enumerate(outs[10:]):
        ref[...] = vec[j : j + 1, :]


def tables():
    freqs = np.exp(np.arange(HD // 2, dtype=np.float32) * np.float32(-2.0 * math.log(10000.0) / HD))
    angles = np.arange(S, dtype=np.float32)[:, None] * freqs.astype(np.float32)
    angles = angles.T.astype(np.float64)
    return np.cos(angles).astype(np.float32), np.sin(angles).astype(np.float32)


def shards(
    ndp, tokens, doc_ids, resets, n1g, n1b, qw, kw, vw, ow, ob, wg1, g1b, n2g, n2b, up, ub, down, db,
    wg2, g2b, cot,
):
    xbits = ndp.bit_length() - 4
    ctab, stab = tables()
    vector = lambda v: v.reshape(1, -1)
    values = dict(
        tokens=tokens, cot=cot, docs=doc_ids, resets=resets.reshape(1, 2), qw=qw, kw=kw, vw=vw, ow=ow,
        wg1=wg1, up=up, down=down, wg2=wg2, n1g=vector(n1g), n1b=vector(n1b), ob=vector(ob),
        g1b=vector(g1b), n2g=vector(n2g), n2b=vector(n2b), ub=vector(ub), db=vector(db), g2b=vector(g2b),
        ctab=jnp.asarray(ctab), stab=jnp.asarray(stab),
    )
    vmem = pl.BlockSpec(memory_space=pltpu.VMEM)
    anyspace = pl.BlockSpec(memory_space=pl.ANY)
    scratch = {name: pltpu.VMEM(shape, dtype) for name, (shape, dtype) in SCRATCH.items()}
    if xbits:
        more = dict(a_x=(64, 512), u_x=(128, 256), d_x=(64, 512), e_x=(32, 256), f_x=(32, 256))
        for name, shape in more.items():
            scratch[name] = pltpu.VMEM((2 * xbits,) + shape, BF)
        scratch.update(p_x=pltpu.VMEM((2 * xbits, 16, 512), F32))
    copies = pltpu.SemaphoreType.DMA((NCOPY + 6 * xbits,))
    scratch.update(
        ss=copies, rs=copies, ls=pltpu.SemaphoreType.DMA((20,))
    )
    in_specs = dict.fromkeys(values, anyspace)
    small = [name for name in values if name not in BIG]
    for name in small:
        scratch[IN + name] = pltpu.VMEM(values[name].shape, values[name].dtype)
    scratch.update(ins=pltpu.SemaphoreType.DMA((len(small),)))
    packed = pl.pallas_call(
        functools.partial(kernel, ndp, xbits, (*values, *OUT_SHAPES, *scratch)),
        out_shape=[jax.ShapeDtypeStruct(shape, dtype) for shape, dtype in OUT_SHAPES.values()],
        in_specs=list(in_specs.values()),
        out_specs=[anyspace] * len(OUT_SHAPES),
        scratch_shapes=list(scratch.values()),
        compiler_params=pltpu.CompilerParams(
            collective_id=0, has_side_effects=True, vmem_limit_bytes=64 << 20
        ),
        name="block",
    )(*values.values())
    out, gt, a, u, d, g1, g2, vec = packed
    f32 = lambda *shape: jax.ShapeDtypeStruct(shape, F32)
    shapes = [f32(D, 128)] * 3 + [f32(128, D)] + [f32(D, D)] * 4
    shapes += [jax.ShapeDtypeStruct((T, D), BF), f32(T, D)] + [f32(1, D)] * 9
    res = pl.pallas_call(
        unpack,
        out_shape=shapes,
        in_specs=[vmem] * 8,
        out_specs=[vmem] * len(shapes),
        compiler_params=pltpu.CompilerParams(vmem_limit_bytes=63 << 20),
        name="unpack",
    )(a, u, d, g1, g2, vec, out, gt)
    gq, gk, gv, go, gu, gd, gg1, gg2, out, gt = res[:10]
    rn1g, rn1b, rob, rg1b, rn2g, rn2b, rdb, rg2b, rub = [v.reshape(-1) for v in res[10:]]
    return (
        out, gt, rn1g, rn1b, gq, gk, gv, go, rob, gg1, rg1b, rn2g, rn2b, gu, rub, gd, rdb, gg2, rg2b,
    )


def solution(mesh):
    both, rep = P(("dp", "mp"), None), P()
    cols, rows = P(None, "mp"), P("mp", None)
    in_specs = (
        both, P("dp", None), P("dp"), rep, rep, cols, cols, cols, rows, rep, rep, rep, rep, rep, cols,
        P("mp"), rows, rep, rep, rep, both,
    )
    out_specs = (
        both, both, rep, rep, cols, cols, cols, rows, rep, rep, rep, rep, rep, cols, P("mp"), rows, rep,
        rep, rep,
    )
    fn = functools.partial(shards, mesh.shape["dp"])
    return jax.shard_map(fn, mesh=mesh, in_specs=in_specs, out_specs=out_specs, check_vma=False)
```

```python
import functools
import math
from types import SimpleNamespace

import jax
import jax.numpy as jnp
import numpy as np
from jax import lax
from jax.experimental import pallas as pl
from jax.experimental.pallas import tpu as pltpu
from jax.sharding import PartitionSpec as P

BF = jnp.bfloat16
F32 = jnp.float32
MESH = pl.DeviceIdType.MESH
D = 512
T = 512
S = 1024
HD = 64
CH = 256
NCOPY = 256
IN = "in_"
BIG = ("tokens", "cot", "up", "down", "wg1", "wg2")
GELU_A = math.sqrt(2.0 / math.pi)
GELU_B = 0.044715


def mm(a, b):
    return lax.dot_general(a, b, (((1,), (0,)), ((), ())), preferred_element_type=F32)


def mmt(a, b):
    return lax.dot_general(a, b, (((1,), (1,)), ((), ())), preferred_element_type=F32)


def tmm(a, b):
    return lax.dot_general(a, b, (((0,), (0,)), ((), ())), preferred_element_type=F32)


def sigmoid(v):
    return 0.5 * jnp.tanh(0.5 * v) + 0.5


def colsum(v):
    return jnp.sum(v, axis=0, keepdims=True)


def rowmean(v):
    return jnp.mean(v, axis=-1, keepdims=True)


OUT_SHAPES = dict(
    o_out=((T, D), BF),
    o_gt=((T, D), BF),
    o_a=((8, 64, 512), BF),
    o_u=((8, 128, 256), BF),
    o_d=((8, 64, 512), BF),
    o_g1=((8, 4, 32, 256), BF),
    o_g2=((8, 4, 32, 256), BF),
    o_vec=((16, 512), F32),
)

SCRATCH = dict(
    xt=((T, D), BF), ct=((T, D), BF),
    info=((2, 8, S), F32), dcol=((S, 128), F32), drow=((8, S), F32),
    cttb=((32, S), F32), sttb=((32, S), F32),
    wz=((4, 256, 512), BF), wh=((768, 512), BF), wo=((256, 512), BF),
    upz=((4, 512, 256), BF), dnz=((4, 256, 512), BF), ubz=((4, 8, 256), F32),
    n1=((S, D), BF), xh1=((T, D), F32), rs1=((T, 128), F32), g1=((T, D), F32),
    qt=((4, 64, S), BF), kt=((4, 64, S), BF), vt=((4, 64, S), BF),
    bias=((CH, 2304), F32), pr=((4, CH, 2304), BF), ctxt=((256, S), BF),
    xs=((T, D), BF), xr=((T, D), BF), amx=((T, D), F32), mid=((T, D), F32),
    xh2=((T, D), F32), rs2=((T, 128), F32), n2=((S, D), BF),
    hid=((4, S, 256), BF), gp=((4, S, 256), BF), acc=((T, D), F32), outb=((T, D), BF),
    bl=((S, D), BF), go2=((T, D), BF), gl2=((S, 256), BF),
    al=((S, D), BF), go1=((T, D), BF), gl1=((S, 256), BF), gmr=((T, D), F32),
    dct=((256, S), BF),
    dkt=((64, S), F32), dvt=((64, S), F32), dt=((768, S), BF), gtb=((T, D), BF),
    a_s=((4, 256, 512), BF), a_h=((4, 8, 32, 512), BF), a_b=((4, 64, 512), BF), a_c=((3, 64, 512), BF),
    u_s=((4, 512, 256), BF), u_h=((4, 8, 64, 256), BF), u_b=((4, 128, 256), BF), u_c=((3, 128, 256), BF),
    d_s=((4, 256, 512), BF), d_h=((4, 8, 32, 512), BF), d_b=((4, 64, 512), BF), d_c=((3, 64, 512), BF),
    e_s=((4, 128, 256), BF), e_h=((8, 2, 32, 256), BF), e_b=((4, 32, 256), BF), e_c=((3, 32, 256), BF),
    f_s=((4, 128, 256), BF), f_h=((8, 2, 32, 256), BF), f_b=((4, 32, 256), BF), f_c=((3, 32, 256), BF),
    wg1v=((D, D), BF), wg2v=((D, D), BF),
    p_a=((8, 64, 512), BF), p_u=((8, 128, 256), BF), p_d=((8, 64, 512), BF),
    p_g1=((8, 4, 32, 256), BF), p_g2=((8, 4, 32, 256), BF), p_vec=((16, 512), F32),
    pk=((16, 512), F32), pk1=((2, 16, 512), F32), pk2=((4, 16, 512), F32), pk3=((4, 16, 512), F32),
)


def kernel(ndp, xbits, names, *refs):
    R = SimpleNamespace(**dict(zip(names, refs)))
    dp = lax.axis_index("dp")
    m = lax.axis_index("mp")
    bits = [lax.rem(lax.div(dp, 1 << b), 2) for b in range(ndp.bit_length() - 1)]
    c = bits[0]
    g = bits[1] + 2 * bits[2]
    mb = [lax.rem(m, 2), lax.div(m, 2)]

    def flip(value, own, mask):
        for b in range(len(own)):
            if mask >> b & 1:
                value = value + (1 - 2 * own[b]) * (1 << b)
        return value

    dpx = lambda mask: flip(dp, bits, mask)
    mx = lambda mask: flip(m, mb, mask)
    gx = lambda mask: flip(g, bits[1:3], mask)

    def ds(start, size):
        return pl.ds(pl.multiple_of(start, size), size)

    swap = (c + mb[0]) == 1
    r0 = pl.multiple_of(c * T, T)
    p0 = pl.multiple_of(T - c * T, T)
    slot = c * 4 + g
    counter = [0]
    unsent = []

    def remote(src, dst, device, keep=True):
        index = counter[0]
        counter[0] += 1
        copy = pltpu.make_async_remote_copy(
            src_ref=src, dst_ref=dst, send_sem=R.ss.at[index], recv_sem=R.rs.at[index],
            device_id=device, device_id_type=MESH,
        )
        if keep:
            copy.start()
            unsent.append(copy)
        return copy

    def local(src, dst, index):
        return pltpu.make_async_copy(src, dst, R.ls.at[index])

    def arrived(copies):
        for copy in copies:
            copy.wait_recv()

    partner = (dpx(1), m)
    cross = (dpx(1), mx(1))
    chip_x, chip_y = (dpx(2), m), (dpx(4), m)
    near, far = (dp, mx(1)), (dp, mx(3))
    own_rows = pl.ds(r0, T)
    mine_cols = ds(c * 256, 256)
    their_cols = ds(256 - c * 256, 256)

    barrier = pltpu.get_barrier_semaphore()
    friends = [partner, (dpx(2), m), (dpx(4), m), (dpx(6), m)] + [(dp, mx(k)) for k in (1, 2, 3)] + [cross]
    friends += [(dpx(1 << b), m) for b in range(3, 3 + xbits)]
    for friend in friends:
        pl.semaphore_signal(barrier, inc=1, device_id=friend, device_id_type=MESH)
    wz, upz, dnz = R.wz, R.upz, R.dnz
    loads = [
        local(src, dst, 9 + i)
        for i, (src, dst) in enumerate(((R.wg1, R.wg1v), (R.wg2, R.wg2v)))
    ]
    for copy in loads:
        copy.start()
    small = [name for name in names if hasattr(R, IN + name)]
    enter = [
        pltpu.make_async_copy(getattr(R, name), getattr(R, IN + name), R.ins.at[i])
        for i, name in enumerate(small)
    ]
    for name, copy in zip(small, enter):
        copy.start()
        setattr(R, name, getattr(R, IN + name))
    own_up = local(R.up.at[:, mine_cols], upz.at[m], 0)
    own_dn = local(R.down.at[ds(c * 256, 256), :], dnz.at[m], 1)
    own_up.start()
    own_dn.start()
    loc_x = local(R.tokens, R.xt, 2)
    loc_c = local(R.cot, R.ct, 3)

    @pl.when(jnp.logical_not(swap))
    def _():
        loc_x.start()
        loc_c.start()

    for copy in enter:
        copy.wait()

    lane = lax.broadcasted_iota(jnp.int32, (64, 128), 1)
    pick = lane == lax.broadcasted_iota(jnp.int32, (64, 128), 0) + c * 64
    pick = jnp.where(pick, 1.0, 0.0).astype(BF)
    wz[m, 0:64, :] = mmt(pick, R.qw[...]).astype(BF)
    wz[m, 64:128, :] = mmt(pick, R.kw[...]).astype(BF)
    wz[m, 128:192, :] = mmt(pick, R.vw[...]).astype(BF)
    wz[m, 192:256, :] = R.ow[ds(c * 64, 64), :]
    ubv = R.ub[...]
    ubv = jnp.where(c == 0, ubv[:, :256], ubv[:, 256:])
    R.ubz[m] = jnp.broadcast_to(ubv, (8, 256))
    info = R.info
    turn = jnp.where(
        lax.broadcasted_iota(jnp.int32, (2, 128), 0) == 0, R.resets[0:1, 0:1], R.resets[0:1, 1:2]
    ).astype(F32)
    info[0] = jnp.zeros((8, S), F32)
    info[0, 0:2, :] = R.docs[...].astype(F32)
    info[0, 2:4, 0:128] = turn

    pl.semaphore_wait(barrier, len(friends))

    swap_x = remote(R.tokens, R.xt, cross, keep=False)
    swap_c = remote(R.cot, R.ct, cross, keep=False)

    near_first = (1, 2, 3)

    def gather(z, rows, lanes):
        quarter = rows // 4
        part = ds(g * quarter, quarter)
        pair = ds(bits[2] * 2 * quarter, 2 * quarter)
        other = ds(gx(2) * quarter, quarter)
        low, high = pl.ds(0, lanes // 2), pl.ds(lanes // 2, lanes // 2)

        def send(block, part, lanes, device):
            return remote(z.at[block, part, lanes], z.at[block, part, lanes], device)

        lines = [send(m, part, pl.ds(0, lanes), (dp, mx(k))) for k in near_first]
        yield
        one, two = [], []
        for k, line in zip(near_first, lines):
            line.wait_recv()
            one.append([send(mx(k), part, low, chip_x), send(mx(k), part, high, chip_y)])
            yield
        for k, copies in zip(near_first, one):
            arrived(copies)
            two.append([
                send(mx(k), pair, low, chip_y), send(mx(k), part, high, chip_x),
                send(mx(k), other, high, chip_x),
            ])
            yield
        for copies in two:
            arrived(copies)
            yield

    def go(steps, count):
        for _ in range(count):
            next(steps)

    get_w, get_u, get_d = gather(wz, 256, 512), gather(upz, 512, 256), gather(dnz, 256, 512)
    next(get_w)

    @pl.when(swap)
    def _():
        swap_x.start()

    own_up.wait()
    next(get_u)
    own_dn.wait()
    next(get_d)

    @pl.when(swap)
    def _():
        swap_c.start()

    send_info = remote(info.at[0], info.at[1], partner)
    ub_copies = [remote(R.ubz.at[m], R.ubz.at[m], (dp, mx(k))) for k in (1, 2, 3)]

    send_info.wait_recv()
    for copy in loads:
        copy.wait()
    row = mb[1]
    mine = jnp.where(swap, 0.0, 1.0)

    def info_row(i):
        return info[0, pl.ds(i, 1), :] * mine + info[1, pl.ds(i, 1), :] * (1.0 - mine)

    doc = info_row(row)
    turn = info_row(row + 2)[:, 0:1]
    R.drow[...] = jnp.broadcast_to(doc, (8, S))
    R.dcol[...] = jnp.broadcast_to(doc, (128, S)).T
    freq = jnp.exp(
        lax.broadcasted_iota(jnp.int32, (32, 1), 0).astype(F32) * (-2.0 * math.log(10000.0) / HD)
    )
    cr, sr = jnp.cos(turn * freq), jnp.sin(turn * freq)
    past = lax.broadcasted_iota(jnp.int32, (1, S), 1).astype(F32) >= turn
    c0, s0 = R.ctab[...], R.stab[...]
    R.cttb[...] = jnp.where(past, c0 * cr + s0 * sr, c0)
    R.sttb[...] = jnp.where(past, s0 * cr - c0 * sr, s0)

    def at(base, i):
        return ds(base + i * CH, CH)

    def chunks(body):
        pl.loop(0, 2)(body)

    go(get_w, 3)

    @pl.when(jnp.logical_not(swap))
    def _():
        loc_x.wait()
        loc_c.wait()

    @pl.when(swap)
    def _():
        swap_x.wait()

    n1 = R.n1

    @chunks
    def _(i):
        rows = at(0, i)
        x = R.xt[rows, :].astype(F32)
        x = x - rowmean(x)
        rstd = lax.rsqrt(rowmean(x * x) + 1e-05)
        xh = x * rstd
        R.xh1[rows, :] = xh
        R.rs1[rows, :] = jnp.broadcast_to(rstd, (CH, 128))
        n1[at(r0, i), :] = (xh * R.n1g[...] + R.n1b[...]).astype(BF)

    send_n1 = remote(n1.at[own_rows, :], n1.at[own_rows, :], partner)
    go(get_w, 3)

    def project(z, base):
        lanes = ds(base, T)
        both = mmt(wz[z, 0:192, :], n1[lanes, :])
        cc, sn = R.cttb[:, lanes], R.sttb[:, lanes]
        for dst, a, b, scale in ((R.qt, both[0:32], both[32:64], 0.125), (R.kt, both[64:96], both[96:128], 1.0)):
            dst[z, 0:32, lanes] = (a * cc - b * sn).astype(BF) * jnp.asarray(scale, BF)
            dst[z, 32:64, lanes] = (b * cc + a * sn).astype(BF) * jnp.asarray(scale, BF)
        R.vt[z, :, lanes] = both[128:192].astype(BF)
        R.wh[ds(z * 192, 192), :] = wz[z, 0:192, :]
        R.wo[ds(z * 64, 64), :] = wz[z, 192:256, :]

    def span(i):
        width = min(i + 1, 3) * CH
        return (i + 1) * CH - width, width

    def lead(i):
        return sum(span(j)[1] for j in range(i))

    def attend(z):
        for i in range(4):
            j0, width = span(i)
            rows, keys = slice(i * CH, (i + 1) * CH), slice(j0, j0 + width)
            here = slice(lead(i), lead(i) + width)
            sc = tmm(R.qt[z, :, rows], R.kt[z, :, keys]) + R.bias[:, here]
            e = jnp.exp(sc - jnp.max(sc, axis=-1, keepdims=True))
            p = (e * (1.0 / jnp.sum(e, axis=-1, keepdims=True))).astype(BF)
            R.pr[z, :, here] = p
            R.ctxt[ds(z * 64, 64), rows] = mmt(R.vt[z, :, keys], p).astype(BF)

    project(m, r0)
    for i in range(4):
        j0, width = span(i)
        dcol = R.dcol[i * CH : (i + 1) * CH, :]
        qi = lax.broadcasted_iota(jnp.int32, (CH, 128), 0) + i * CH
        for w in range(width // 128):
            ki = lax.broadcasted_iota(jnp.int32, (CH, 128), 1) + (j0 + w * 128)
            ok = (dcol == R.drow[0:1, j0 + w * 128 : j0 + w * 128 + 128]) & (ki <= qi)
            R.bias[:, lead(i) + w * 128 : lead(i) + w * 128 + 128] = jnp.where(ok, 0.0, -1e30)
    send_n1.wait_recv()
    go(get_u, 3)
    project(m, p0)
    attend(m)
    go(get_d, 3)

    @chunks
    def _(i):
        gate = mm(n1[at(r0, i), :], R.wg1v[...]) + R.g1b[...]
        R.g1[at(0, i), :] = sigmoid(gate)

    for k in near_first:
        go(get_w, 1)
        project(mx(k), r0)
        project(mx(k), p0)
        if k == 1:
            go(get_u, 3)
        if k == 2:
            go(get_d, 3)
        attend(mx(k))

    def hand_over(body):
        copies = []
        for i in range(2):
            rows = slice(i * CH, i * CH + CH)
            R.xs[rows, :] = body(i).astype(BF)
            copies.append(remote(R.xs.at[rows, :], R.xr.at[rows, :], partner, keep=False))
            copies[i].start()
        return copies

    def wait_all(copies):
        for copy in copies:
            copy.wait()

    send_at = hand_over(lambda i: tmm(R.ctxt[:, at(p0, i)], R.wo[...]))

    @chunks
    def _(i):
        R.amx[at(0, i), :] = tmm(R.ctxt[:, at(r0, i)], R.wo[...])

    wait_all(send_at)
    n2 = R.n2

    @chunks
    def _(i):
        rows = at(0, i)
        x = R.xt[rows, :].astype(F32)
        amx = R.amx[rows, :] + R.xr[rows, :].astype(F32) + R.ob[...] - x
        R.amx[rows, :] = amx
        mid = x + R.g1[rows, :] * amx
        R.mid[rows, :] = mid
        mid = mid - rowmean(mid)
        rstd = lax.rsqrt(rowmean(mid * mid) + 1e-05)
        xh = mid * rstd
        R.xh2[rows, :] = xh
        R.rs2[rows, :] = jnp.broadcast_to(rstd, (CH, 128))
        n2[at(r0, i), :] = (xh * R.n2g[...] + R.n2b[...]).astype(BF)

    send_n2 = remote(n2.at[own_rows, :], n2.at[own_rows, :], partner)
    arrived(ub_copies)

    def up_part(base, z):
        @chunks
        def _(i):
            rows = at(base, i)
            v = mm(n2[rows, :], upz[z]) + R.ubz[z, 0:1, :]
            v2 = v * v
            half = 0.5 * jnp.tanh(v * (GELU_A + (GELU_A * GELU_B) * v2)) + 0.5
            hid = v * half
            R.hid[z, rows, :] = hid.astype(BF)
            slope = half + hid * (1.0 - half) * (2.0 * GELU_A + (6.0 * GELU_A * GELU_B) * v2)
            R.gp[z, rows, :] = slope.astype(BF)

    def down_part(base, dst, z, begin):
        @chunks
        def _(i):
            part = mm(R.hid[z, at(base, i), :], dnz[z])
            dst[at(0, i), :] = part if begin else dst[at(0, i), :] + part

    up_part(r0, m)
    send_n2.wait_recv()
    up_part(p0, m)
    for k in near_first:
        go(get_u, 1)
        up_part(r0, mx(k))
        up_part(p0, mx(k))
    down_part(p0, R.acc, m, True)
    down_part(r0, R.gmr, m, True)
    for k in near_first:
        go(get_d, 1)
        down_part(p0, R.acc, mx(k), False)
        if k == near_first[-1]:
            send_br = hand_over(lambda i: R.acc[i * CH : i * CH + CH, :])
        down_part(r0, R.gmr, mx(k), False)

    @pl.when(swap)
    def _():
        swap_c.wait()

    pk = R.pk
    pk[...] = jnp.zeros((16, 512), F32)
    wait_all(send_br)

    @chunks
    def _(i):
        rows = at(0, i)
        gate = sigmoid(mm(n2[at(r0, i), :], R.wg2v[...]) + R.g2b[...])
        mid = R.mid[rows, :]
        bm = R.gmr[rows, :] + R.xr[rows, :].astype(F32) + R.db[...] - mid
        R.outb[rows, :] = (mid + gate * bm).astype(BF)
        cot = R.ct[rows, :].astype(F32)
        gb = gate * cot
        rest = cot - gb
        R.mid[rows, :] = rest
        gg = rest * bm * gate
        R.bl[at(r0, i), :] = gb.astype(BF)
        R.go2[rows, :] = gg.astype(BF)
        pk[6:7, :] += colsum(gb)
        pk[7:8, :] += colsum(gg)

    send_bl = remote(R.bl.at[own_rows, :], R.bl.at[own_rows, :], partner)
    send_gl2 = remote(R.go2.at[:, their_cols], R.gl2.at[own_rows, :], partner)
    keep_gl2 = local(R.go2.at[:, mine_cols], R.gl2.at[own_rows, :], 4)
    keep_gl2.start()
    back_o = remote(R.outb, R.o_out, cross, keep=False)
    keep_o = local(R.outb, R.o_out, 5)

    @pl.when(swap)
    def _():
        back_o.start()

    @pl.when(jnp.logical_not(swap))
    def _():
        keep_o.start()

    def hidden_back(base):
        for z in range(4):
            def step(i, acc, z=z):
                rows = at(base, i)
                gpre = mmt(R.bl[rows, :], dnz[z]) * R.gp[z, rows, :].astype(F32)
                R.gp[z, rows, :] = gpre.astype(BF)
                return acc + colsum(gpre)

            both = lax.fori_loop(0, 2, step, jnp.zeros((1, 256), F32))
            pk[8 + z : 9 + z, 0:256] += jnp.where(c == 0, both, 0.0)
            pk[8 + z : 9 + z, 256:512] += jnp.where(c == 0, 0.0, both)

    def norm_two_part(rows):
        total = mmt(R.gp[0, rows, :], upz[0])
        for z in range(1, 4):
            total = total + mmt(R.gp[z, rows, :], upz[z])
        return total

    def halving(block, buf, dev_a, dev_b, a, b, store):
        f32 = lambda ref: ref[...].astype(F32)
        one = [
            remote(block(a ^ b, 0), buf.at[0], dev_a), remote(block(a ^ b, 1), buf.at[1], dev_b),
            remote(block(a, 0), buf.at[2], dev_a), remote(block(b, 1), buf.at[3], dev_b),
        ]
        yield
        arrived(one[0:2])
        buf[6] = (f32(block(b, 0)) + f32(buf.at[0])).astype(BF)
        buf[7] = (f32(block(a, 1)) + f32(buf.at[1])).astype(BF)
        two = [remote(buf.at[6], buf.at[4], dev_b), remote(buf.at[7], buf.at[5], dev_a)]
        yield
        arrived(one[2:4] + two)
        store(0, (f32(block(0, 0)) + f32(buf.at[2]) + f32(buf.at[4])).astype(BF))
        store(1, (f32(block(0, 1)) + f32(buf.at[3]) + f32(buf.at[5])).astype(BF))

    def exchange(total, buf, dtype):
        for b in range(xbits):
            buf[2 * b] = total.astype(dtype)
            copy = remote(buf.at[2 * b], buf.at[2 * b + 1], (dpx(8 << b), m))
            copy.wait_recv()
            total = buf[2 * b].astype(F32) + buf[2 * b + 1].astype(F32)
        return total

    def chips(out):
        copies = [remote(out.at[slot], out.at[slot], (dpx(2 * k), m)) for k in (1, 2, 3)]
        yield
        arrived(copies)

    def chips_both(out):
        size = out.shape[1] // 2
        low, high = pl.ds(0, size), pl.ds(size, size)
        other = c * 4 + gx(2)
        pair = ds(c * 4 + 2 * bits[2], 2)
        copies = [
            remote(out.at[slot, low], out.at[slot, low], chip_x),
            remote(out.at[slot, high], out.at[slot, high], chip_y),
        ]
        yield
        arrived(copies)
        copies = [
            remote(out.at[pair, low], out.at[pair, low], chip_y),
            remote(out.at[slot, high], out.at[slot, high], chip_x),
            remote(out.at[other, high], out.at[other, high], chip_x),
        ]
        yield
        arrived(copies)

    def cores(out):
        return [remote(out.at[ds(c * 4, 4)], out.at[ds(c * 4, 4)], partner)]

    def flush(buf):
        copy = local(buf, homes[id(buf)], 12 + len(flushed))
        copy.start()
        flushed.append(copy)

    flushed = []
    homes = {
        id(R.p_a): R.o_a, id(R.p_u): R.o_u, id(R.p_d): R.o_d, id(R.p_g1): R.o_g1, id(R.p_g2): R.o_g2,
        id(R.p_vec): R.o_vec,
    }

    def finish(out, total, route=chips_both):
        out[slot] = total.astype(BF)
        yield from route(out)
        copies = cores(out)
        yield
        arrived(copies)
        flush(out)

    def finish_all(out, total):
        out[slot, m] = total.astype(BF)
        copies = [remote(out.at[slot, m], out.at[slot, m], (dp, mx(k))) for k in (1, 2, 3)]
        yield
        arrived(copies)
        yield from chips_both(out)
        copies = cores(out)
        yield
        arrived(copies)
        flush(out)

    def over_mp(b_ref, c_ref):
        return [remote(b_ref.at[mx(k)], c_ref.at[k - 1], (dp, mx(k))) for k in (1, 2, 3)]

    def plane_first(s_ref, h_ref, b_ref, c_ref, x_ref, quarter, end, out):
        def block(k, half):
            return s_ref.at[2 * half : 2 * half + 2, ds(gx(k) * quarter, quarter), :]

        def store(half, value):
            b_ref[2 * half : 2 * half + 2] = value

        yield from halving(block, h_ref, chip_x, chip_y, 1, 2, store)
        copies = over_mp(b_ref, c_ref)
        yield True
        arrived(copies)
        total = b_ref[m].astype(F32)
        for k in range(3):
            total = total + c_ref[k].astype(F32)
        yield from end(out, exchange(total, x_ref, BF))

    def block_sum(name, k, quarter, out, route):
        s_ref, h_ref = getattr(R, name + "_s"), getattr(R, name + "_h").at[k]
        b_ref, c_ref = getattr(R, name + "_b"), getattr(R, name + "_c")
        half_rows = quarter // 2

        def block(kk, half):
            return s_ref.at[mx(k), ds(gx(kk) * quarter + half * half_rows, half_rows), :]

        def store(half, value):
            b_ref[k, half * half_rows : half * half_rows + half_rows] = value

        def direct():
            copies = [
                remote(block(kk, half), h_ref.at[2 * kk - 2 + half], (dpx(2 * kk), m))
                for kk in (1, 2, 3) for half in (0, 1)
            ]
            yield
            arrived(copies)
            for half in (0, 1):
                total = block(0, half)[...].astype(F32)
                for kk in (1, 2, 3):
                    total = total + h_ref[2 * kk - 2 + half].astype(F32)
                store(half, total.astype(BF))

        if name == "a" and k == 0:
            yield from direct()
        else:
            yield from halving(block, h_ref, chip_x, chip_y, 1, 2, store)
        if k:
            waiting.setdefault(name, []).append(remote(b_ref.at[k], c_ref.at[k - 1], (dp, mx(k))))
            return
        yield True
        arrived(waiting[name])
        total = b_ref[0].astype(F32)
        for j in range(3):
            total = total + c_ref[j].astype(F32)
        yield from finish(out, exchange(total, extra(name + "_x"), BF), route)

    waiting, queue, late = {}, [], []

    def begin(steps):
        next(steps)
        queue.append(steps)

    def advance(source):
        steps = source.pop(0)
        for last in steps:
            (late if last or source is late else queue).append(steps)
            break

    def pump(count):
        for _ in range(min(count, len(queue))):
            advance(queue)

    def pump_late(count):
        for _ in range(min(count, len(late))):
            advance(late)

    extra = lambda name: getattr(R, name, None)
    sum_e = plane_first(R.e_s, R.e_h, R.e_b, R.e_c, extra("e_x"), 32, finish_all, R.p_g2)
    sum_f = plane_first(R.f_s, R.f_h, R.f_b, R.f_c, extra("f_x"), 32, finish_all, R.p_g1)
    far_first = (3, 2, 1, 0)

    hidden_back(r0)
    send_bl.wait_recv()
    for k in far_first:
        R.d_s[mx(k)] = tmm(R.hid[mx(k)], R.bl[...]).astype(BF)
        begin(block_sum("d", k, 64, R.p_d, chips_both))
    hidden_back(p0)
    n2t = n2[...].T
    for k in far_first:
        R.u_s[mx(k)] = mm(n2t, R.gp[mx(k)]).astype(BF)
        begin(block_sum("u", k, 128, R.p_u, chips_both))
        pump(1)
    send_gl2.wait_recv()
    keep_gl2.wait()
    full = mm(n2t, R.gl2[...]).astype(BF)
    for z in range(4):
        R.e_s[z] = full[z * 128 : z * 128 + 128, :]
    begin(sum_e)

    send_d2 = hand_over(lambda i: norm_two_part(at(p0, i)))

    @chunks
    def _(i):
        R.gmr[at(0, i), :] = norm_two_part(at(r0, i))

    pump(2)
    wait_all(send_d2)

    @chunks
    def _(i):
        rows = at(0, i)
        gn = R.gmr[rows, :] + R.xr[rows, :].astype(F32) + mmt(R.go2[rows, :], R.wg2v[...])
        xh = R.xh2[rows, :]
        pk[4:5, :] += colsum(gn * xh)
        pk[5:6, :] += colsum(gn)
        e = gn * R.n2g[...]
        gm = R.rs2[rows, 0:1] * (e - rowmean(e) - xh * rowmean(e * xh)) + R.mid[rows, :]
        gate = R.g1[rows, :]
        ga = gate * gm
        gg = (gm - ga) * R.amx[rows, :] * gate
        R.mid[rows, :] = gm - ga
        R.al[at(r0, i), :] = ga.astype(BF)
        R.go1[rows, :] = gg.astype(BF)
        pk[2:3, :] += colsum(ga)
        pk[3:4, :] += colsum(gg)

    send_al = remote(R.al.at[own_rows, :], R.al.at[own_rows, :], partner)
    send_gl1 = remote(R.go1.at[:, their_cols], R.gl1.at[own_rows, :], partner)
    keep_gl1 = local(R.go1.at[:, mine_cols], R.gl1.at[own_rows, :], 6)
    keep_gl1.start()
    n1t = n1[...].T
    send_al.wait_recv()

    @pl.loop(0, 4)
    def _(i):
        rows = at(0, i)
        R.dct[:, rows] = mmt(R.wo[...], R.al[rows, :]).astype(BF)

    pump(3)
    grad_wo = mm(R.ctxt[...], R.al[...]).astype(BF)
    for z in range(4):
        R.a_s[z, 192:256, :] = grad_wo[z * 64 : z * 64 + 64, :]
    send_gl1.wait_recv()
    keep_gl1.wait()
    full = mm(n1t, R.gl1[...]).astype(BF)
    for z in range(4):
        R.f_s[z] = full[z * 128 : z * 128 + 128, :]

    begin(sum_f)
    pump(2)

    dkt, dvt, dt = R.dkt, R.dvt, R.dt

    for k in far_first:
        z = mx(k)
        dkt[...] = jnp.zeros((64, S), F32)
        dvt[...] = jnp.zeros((64, S), F32)
        mine_rows = ds(z * 64, 64)

        def dt_rows(start, size, z=z):
            return pl.ds(pl.multiple_of(z * 192 + start, 32), size)

        for i in range(4):
            j0, width = span(i)
            rows, keys = slice(i * CH, (i + 1) * CH), slice(j0, j0 + width)
            p = R.pr[z, :, lead(i) : lead(i) + width]
            pf = p.astype(F32)
            t = tmm(R.dct[mine_rows, rows], R.vt[z, :, keys]) * pf
            part = (t - pf * jnp.sum(t, axis=-1, keepdims=True)).astype(BF)
            dvt[:, keys] += mm(R.dct[mine_rows, rows], p)
            dkt[:, keys] += mm(R.qt[z, :, rows], part)
            dq = mmt(R.kt[z, :, keys], part) * 0.125
            a, b = dq[0:32], dq[32:64]
            cc, sn = R.cttb[:, rows], R.sttb[:, rows]
            dt[dt_rows(0, 32), rows] = (a * cc + b * sn).astype(BF)
            dt[dt_rows(32, 32), rows] = (b * cc - a * sn).astype(BF)
            if i >= 4 - (4, 3, 3, 2)[3 - k]:
                pump(1)
            if k == 0:
                pump_late(1)
        a, b = dkt[0:32, :], dkt[32:64, :]
        cc, sn = R.cttb[...], R.sttb[...]
        dt[dt_rows(64, 32), :] = (a * cc + b * sn).astype(BF)
        dt[dt_rows(96, 32), :] = (b * cc - a * sn).astype(BF)
        dt[dt_rows(128, 64), :] = dvt[...].astype(BF)
        R.a_s[z, 0:192, :] = mm(dt[dt_rows(0, 192), :], n1[...]).astype(BF)
        begin(block_sum("a", k, 64, R.p_a, chips))

    send_d1 = hand_over(lambda i: tmm(dt[:, at(p0, i)], R.wh[...]))
    pump(3)

    @chunks
    def _(i):
        R.gmr[at(0, i), :] = tmm(dt[:, at(r0, i)], R.wh[...])

    pump(3)
    wait_all(send_d1)

    def norm_one_back(i):
        rows = slice(i * CH, i * CH + CH)
        gn = R.gmr[rows, :] + R.xr[rows, :].astype(F32) + mmt(R.go1[rows, :], R.wg1v[...])
        xh = R.xh1[rows, :]
        pk[0:1, :] += colsum(gn * xh)
        pk[1:2, :] += colsum(gn)
        e = gn * R.n1g[...]
        grad = R.rs1[rows, 0:1] * (e - rowmean(e) - xh * rowmean(e * xh)) + R.mid[rows, :]
        R.gtb[rows, :] = grad.astype(BF)

    back_t, keep_t = [], []
    for i in range(2):
        norm_one_back(i)
        rows = slice(i * CH, i * CH + CH)
        back_t.append(remote(R.gtb.at[rows, :], R.o_gt.at[rows, :], cross, keep=False))
        keep_t.append(local(R.gtb.at[rows, :], R.o_gt.at[rows, :], 7 + i))

        @pl.when(swap)
        def _():
            back_t[i].start()

        @pl.when(jnp.logical_not(swap))
        def _():
            keep_t[i].start()

    pk1, pk2, pk3 = R.pk1, R.pk2, R.pk3
    pk1[c] = pk[...]
    p_1 = remote(pk1.at[c], pk1.at[c], partner)
    pump(2)
    pump_late(4)
    p_1.wait_recv()
    pk2[g] = pk1[0] + pk1[1]
    p_2 = [remote(pk2.at[g], pk2.at[g], (dpx(2 * k), m)) for k in (1, 2, 3)]
    pump(4)
    pump_late(5)
    arrived(p_2)
    pk3[m] = (pk2[0] + pk2[1]) + (pk2[2] + pk2[3])
    p_3 = [remote(pk3.at[m], pk3.at[m], (dp, mx(k))) for k in (1, 2, 3)]
    pump_late(5)
    arrived(p_3)
    total = exchange((pk3[0] + pk3[1]) + (pk3[2] + pk3[3]), extra("p_x"), F32)
    pk[...] = total
    R.p_vec[...] = total
    R.p_vec[8:9, :] = pk[pl.ds(8 + m, 1), :]
    flush(R.p_vec)
    while queue or late:
        pump(1)
        pump_late(1)

    for copy in unsent:
        copy.wait_send()
    for copy in flushed:
        copy.wait()

    @pl.when(swap)
    def _():
        for copy in (back_o, *back_t):
            copy.wait()

    @pl.when(jnp.logical_not(swap))
    def _():
        for copy in (keep_o, *keep_t):
            copy.wait()


def unpack(a, u, d, g1, g2, vec, out, gt, *outs):
    (oq, ok, ov, oo, ou, od, og1, og2, oout, ogt) = outs[:10]
    for j, ref in enumerate((oq, ok, ov)):
        both = jnp.concatenate([a[j].astype(F32), a[4 + j].astype(F32)], axis=0)
        ref[...] = both.T
    for c in range(2):
        oo[c * 64 : c * 64 + 64, :] = a[4 * c + 3].astype(F32)
        for g in range(4):
            ou[g * 128 : g * 128 + 128, c * 256 : c * 256 + 256] = u[4 * c + g].astype(F32)
            od[c * 256 + g * 64 : c * 256 + g * 64 + 64, :] = d[4 * c + g].astype(F32)
            for z in range(4):
                rows = slice(z * 128 + g * 32, z * 128 + g * 32 + 32)
                og1[rows, c * 256 : c * 256 + 256] = g1[4 * c + g, z].astype(F32)
                og2[rows, c * 256 : c * 256 + 256] = g2[4 * c + g, z].astype(F32)
    oout[...] = out[...]
    ogt[...] = gt[...].astype(F32)
    for j, ref in enumerate(outs[10:]):
        ref[...] = vec[j : j + 1, :]


def tables():
    freqs = np.exp(np.arange(HD // 2, dtype=np.float32) * np.float32(-2.0 * math.log(10000.0) / HD))
    angles = np.arange(S, dtype=np.float32)[:, None] * freqs.astype(np.float32)
    angles = angles.T.astype(np.float64)
    return np.cos(angles).astype(np.float32), np.sin(angles).astype(np.float32)


def shards(
    ndp, tokens, doc_ids, resets, n1g, n1b, qw, kw, vw, ow, ob, wg1, g1b, n2g, n2b, up, ub, down, db,
    wg2, g2b, cot,
):
    xbits = ndp.bit_length() - 4
    ctab, stab = tables()
    vector = lambda v: v.reshape(1, -1)
    values = dict(
        tokens=tokens, cot=cot, docs=doc_ids, resets=resets.reshape(1, 2), qw=qw, kw=kw, vw=vw, ow=ow,
        wg1=wg1, up=up, down=down, wg2=wg2, n1g=vector(n1g), n1b=vector(n1b), ob=vector(ob),
        g1b=vector(g1b), n2g=vector(n2g), n2b=vector(n2b), ub=vector(ub), db=vector(db), g2b=vector(g2b),
        ctab=jnp.asarray(ctab), stab=jnp.asarray(stab),
    )
    vmem = pl.BlockSpec(memory_space=pltpu.VMEM)
    anyspace = pl.BlockSpec(memory_space=pl.ANY)
    scratch = {name: pltpu.VMEM(shape, dtype) for name, (shape, dtype) in SCRATCH.items()}
    if xbits:
        more = dict(a_x=(64, 512), u_x=(128, 256), d_x=(64, 512), e_x=(32, 256), f_x=(32, 256))
        for name, shape in more.items():
            scratch[name] = pltpu.VMEM((2 * xbits,) + shape, BF)
        scratch.update(p_x=pltpu.VMEM((2 * xbits, 16, 512), F32))
    copies = pltpu.SemaphoreType.DMA((NCOPY + 6 * xbits,))
    scratch.update(
        ss=copies, rs=copies, ls=pltpu.SemaphoreType.DMA((20,))
    )
    in_specs = dict.fromkeys(values, anyspace)
    small = [name for name in values if name not in BIG]
    for name in small:
        scratch[IN + name] = pltpu.VMEM(values[name].shape, values[name].dtype)
    scratch.update(ins=pltpu.SemaphoreType.DMA((len(small),)))
    packed = pl.pallas_call(
        functools.partial(kernel, ndp, xbits, (*values, *OUT_SHAPES, *scratch)),
        out_shape=[jax.ShapeDtypeStruct(shape, dtype) for shape, dtype in OUT_SHAPES.values()],
        in_specs=list(in_specs.values()),
        out_specs=[anyspace] * len(OUT_SHAPES),
        scratch_shapes=list(scratch.values()),
        compiler_params=pltpu.CompilerParams(
            collective_id=0, has_side_effects=True, vmem_limit_bytes=64 << 20
        ),
        name="block",
    )(*values.values())
    out, gt, a, u, d, g1, g2, vec = packed
    f32 = lambda *shape: jax.ShapeDtypeStruct(shape, F32)
    shapes = [f32(D, 128)] * 3 + [f32(128, D)] + [f32(D, D)] * 4
    shapes += [jax.ShapeDtypeStruct((T, D), BF), f32(T, D)] + [f32(1, D)] * 9
    res = pl.pallas_call(
        unpack,
        out_shape=shapes,
        in_specs=[vmem] * 8,
        out_specs=[vmem] * len(shapes),
        compiler_params=pltpu.CompilerParams(vmem_limit_bytes=63 << 20),
        name="unpack",
    )(a, u, d, g1, g2, vec, out, gt)
    gq, gk, gv, go, gu, gd, gg1, gg2, out, gt = res[:10]
    rn1g, rn1b, rob, rg1b, rn2g, rn2b, rdb, rg2b, rub = [v.reshape(-1) for v in res[10:]]
    return (
        out, gt, rn1g, rn1b, gq, gk, gv, go, rob, gg1, rg1b, rn2g, rn2b, gu, rub, gd, rdb, gg2, rg2b,
    )


def solution(mesh):
    both, rep = P(("dp", "mp"), None), P()
    cols, rows = P(None, "mp"), P("mp", None)
    in_specs = (
        both, P("dp", None), P("dp"), rep, rep, cols, cols, cols, rows, rep, rep, rep, rep, rep, cols,
        P("mp"), rows, rep, rep, rep, both,
    )
    out_specs = (
        both, both, rep, rep, cols, cols, cols, rows, rep, rep, rep, rep, rep, cols, P("mp"), rows, rep,
        rep, rep,
    )
    fn = functools.partial(shards, mesh.shape["dp"])
    return jax.shard_map(fn, mesh=mesh, in_specs=in_specs, out_specs=out_specs, check_vma=False)
```

```python
import functools
import math
from types import SimpleNamespace

import jax
import jax.numpy as jnp
import numpy as np
from jax import lax
from jax.experimental import pallas as pl
from jax.experimental.pallas import tpu as pltpu
from jax.sharding import PartitionSpec as P

BF = jnp.bfloat16
F32 = jnp.float32
MESH = pl.DeviceIdType.MESH
D = 512
T = 512
S = 1024
HD = 64
CH = 256
NCOPY = 256
IN = "in_"
BIG = ("tokens", "cot", "up", "down", "wg1", "wg2")
GELU_A = math.sqrt(2.0 / math.pi)
GELU_B = 0.044715


def mm(a, b):
    return lax.dot_general(a, b, (((1,), (0,)), ((), ())), preferred_element_type=F32)


def mmt(a, b):
    return lax.dot_general(a, b, (((1,), (1,)), ((), ())), preferred_element_type=F32)


def tmm(a, b):
    return lax.dot_general(a, b, (((0,), (0,)), ((), ())), preferred_element_type=F32)


def sigmoid(v):
    return 0.5 * jnp.tanh(0.5 * v) + 0.5


def colsum(v):
    return jnp.sum(v, axis=0, keepdims=True)


def rowmean(v):
    return jnp.mean(v, axis=-1, keepdims=True)


OUT_SHAPES = dict(
    o_out=((T, D), BF),
    o_gt=((T, D), BF),
    o_a=((8, 64, 512), BF),
    o_u=((8, 128, 256), BF),
    o_d=((8, 64, 512), BF),
    o_g1=((8, 4, 32, 256), BF),
    o_g2=((8, 4, 32, 256), BF),
    o_vec=((16, 512), F32),
)

SCRATCH = dict(
    xt=((T, D), BF), ct=((T, D), BF),
    info=((2, 8, S), F32), dcol=((S, 128), F32), drow=((8, S), F32),
    cttb=((32, S), F32), sttb=((32, S), F32),
    wz=((4, 256, 512), BF), wh=((768, 512), BF), wo=((256, 512), BF),
    upz=((4, 512, 256), BF), dnz=((4, 256, 512), BF), ubz=((4, 8, 256), F32),
    n1=((S, D), BF), xh1=((T, D), F32), rs1=((T, 128), F32), g1=((T, D), F32),
    qt=((4, 64, S), BF), kt=((4, 64, S), BF), vt=((4, 64, S), BF),
    bias=((CH, 2304), F32), pr=((4, CH, 2304), BF), ctxt=((256, S), BF),
    xs=((T, D), BF), xr=((T, D), BF), amx=((T, D), F32), mid=((T, D), F32),
    xh2=((T, D), F32), rs2=((T, 128), F32), n2=((S, D), BF),
    hid=((4, S, 256), BF), gp=((4, S, 256), BF), acc=((T, D), F32), outb=((T, D), BF),
    bl=((S, D), BF), go2=((T, D), BF), gl2=((S, 256), BF),
    al=((S, D), BF), go1=((T, D), BF), gl1=((S, 256), BF), gmr=((T, D), F32),
    dct=((256, S), BF),
    dkt=((64, S), F32), dvt=((64, S), F32), dt=((768, S), BF), gtb=((T, D), BF),
    a_s=((4, 256, 512), BF), a_h=((4, 8, 32, 512), BF), a_b=((4, 64, 512), BF), a_c=((3, 64, 512), BF),
    u_s=((4, 512, 256), BF), u_h=((4, 8, 64, 256), BF), u_b=((4, 128, 256), BF), u_c=((3, 128, 256), BF),
    d_s=((4, 256, 512), BF), d_h=((4, 8, 32, 512), BF), d_b=((4, 64, 512), BF), d_c=((3, 64, 512), BF),
    e_s=((4, 128, 256), BF), e_h=((8, 2, 32, 256), BF), e_b=((4, 32, 256), BF), e_c=((3, 32, 256), BF),
    f_s=((4, 128, 256), BF), f_h=((8, 2, 32, 256), BF), f_b=((4, 32, 256), BF), f_c=((3, 32, 256), BF),
    wg1v=((D, D), BF), wg2v=((D, D), BF),
    p_a=((8, 64, 512), BF), p_u=((8, 128, 256), BF), p_d=((8, 64, 512), BF),
    p_g1=((8, 4, 32, 256), BF), p_g2=((8, 4, 32, 256), BF), p_vec=((16, 512), F32),
    pk=((16, 512), F32), pk1=((2, 16, 512), F32), pk2=((4, 16, 512), F32), pk3=((4, 16, 512), F32),
)


def kernel(ndp, xbits, names, *refs):
    R = SimpleNamespace(**dict(zip(names, refs)))
    dp = lax.axis_index("dp")
    m = lax.axis_index("mp")
    bits = [lax.rem(lax.div(dp, 1 << b), 2) for b in range(ndp.bit_length() - 1)]
    c = bits[0]
    g = bits[1] + 2 * bits[2]
    mb = [lax.rem(m, 2), lax.div(m, 2)]

    def flip(value, own, mask):
        for b in range(len(own)):
            if mask >> b & 1:
                value = value + (1 - 2 * own[b]) * (1 << b)
        return value

    dpx = lambda mask: flip(dp, bits, mask)
    mx = lambda mask: flip(m, mb, mask)
    gx = lambda mask: flip(g, bits[1:3], mask)

    def ds(start, size):
        return pl.ds(pl.multiple_of(start, size), size)

    swap = (c + mb[0]) == 1
    r0 = pl.multiple_of(c * T, T)
    p0 = pl.multiple_of(T - c * T, T)
    slot = c * 4 + g
    counter = [0]
    unsent = []

    def remote(src, dst, device, keep=True):
        index = counter[0]
        counter[0] += 1
        copy = pltpu.make_async_remote_copy(
            src_ref=src, dst_ref=dst, send_sem=R.ss.at[index], recv_sem=R.rs.at[index],
            device_id=device, device_id_type=MESH,
        )
        if keep:
            copy.start()
            unsent.append(copy)
        return copy

    def local(src, dst, index):
        return pltpu.make_async_copy(src, dst, R.ls.at[index])

    def arrived(copies):
        for copy in copies:
            copy.wait_recv()

    partner = (dpx(1), m)
    cross = (dpx(1), mx(1))
    chip_x, chip_y = (dpx(2), m), (dpx(4), m)
    near, far = (dp, mx(1)), (dp, mx(3))
    own_rows = pl.ds(r0, T)
    mine_cols = ds(c * 256, 256)
    their_cols = ds(256 - c * 256, 256)

    barrier = pltpu.get_barrier_semaphore()
    friends = [partner, (dpx(2), m), (dpx(4), m), (dpx(6), m)] + [(dp, mx(k)) for k in (1, 2, 3)] + [cross]
    friends += [(dpx(1 << b), m) for b in range(3, 3 + xbits)]
    for friend in friends:
        pl.semaphore_signal(barrier, inc=1, device_id=friend, device_id_type=MESH)
    wz, upz, dnz = R.wz, R.upz, R.dnz
    loads = [
        local(src, dst, 9 + i)
        for i, (src, dst) in enumerate(((R.wg1, R.wg1v), (R.wg2, R.wg2v)))
    ]
    for copy in loads:
        copy.start()
    small = [name for name in names if hasattr(R, IN + name)]
    enter = [
        pltpu.make_async_copy(getattr(R, name), getattr(R, IN + name), R.ins.at[i])
        for i, name in enumerate(small)
    ]
    for name, copy in zip(small, enter):
        copy.start()
        setattr(R, name, getattr(R, IN + name))
    own_up = local(R.up.at[:, mine_cols], upz.at[m], 0)
    own_dn = local(R.down.at[ds(c * 256, 256), :], dnz.at[m], 1)
    own_up.start()
    own_dn.start()
    loc_x = local(R.tokens, R.xt, 2)
    loc_c = local(R.cot, R.ct, 3)

    @pl.when(jnp.logical_not(swap))
    def _():
        loc_x.start()
        loc_c.start()

    for copy in enter:
        copy.wait()

    lane = lax.broadcasted_iota(jnp.int32, (64, 128), 1)
    pick = lane == lax.broadcasted_iota(jnp.int32, (64, 128), 0) + c * 64
    pick = jnp.where(pick, 1.0, 0.0).astype(BF)
    wz[m, 0:64, :] = mmt(pick, R.qw[...]).astype(BF)
    wz[m, 64:128, :] = mmt(pick, R.kw[...]).astype(BF)
    wz[m, 128:192, :] = mmt(pick, R.vw[...]).astype(BF)
    wz[m, 192:256, :] = R.ow[ds(c * 64, 64), :]
    ubv = R.ub[...]
    ubv = jnp.where(c == 0, ubv[:, :256], ubv[:, 256:])
    R.ubz[m] = jnp.broadcast_to(ubv, (8, 256))
    info = R.info
    turn = jnp.where(
        lax.broadcasted_iota(jnp.int32, (2, 128), 0) == 0, R.resets[0:1, 0:1], R.resets[0:1, 1:2]
    ).astype(F32)
    info[0] = jnp.zeros((8, S), F32)
    info[0, 0:2, :] = R.docs[...].astype(F32)
    info[0, 2:4, 0:128] = turn

    pl.semaphore_wait(barrier, len(friends))

    swap_x = remote(R.tokens, R.xt, cross, keep=False)
    swap_c = remote(R.cot, R.ct, cross, keep=False)

    near_first = (1, 2, 3)

    def gather(z, rows, lanes):
        quarter = rows // 4
        part = ds(g * quarter, quarter)
        pair = ds(bits[2] * 2 * quarter, 2 * quarter)
        other = ds(gx(2) * quarter, quarter)
        low, high = pl.ds(0, lanes // 2), pl.ds(lanes // 2, lanes // 2)

        def send(block, part, lanes, device):
            return remote(z.at[block, part, lanes], z.at[block, part, lanes], device)

        lines = [send(m, part, pl.ds(0, lanes), (dp, mx(k))) for k in near_first]
        yield
        one, two = [], []
        for k, line in zip(near_first, lines):
            line.wait_recv()
            one.append([send(mx(k), part, low, chip_x), send(mx(k), part, high, chip_y)])
            yield
        for k, copies in zip(near_first, one):
            arrived(copies)
            two.append([
                send(mx(k), pair, low, chip_y), send(mx(k), part, high, chip_x),
                send(mx(k), other, high, chip_x),
            ])
            yield
        for copies in two:
            arrived(copies)
            yield

    def go(steps, count):
        for _ in range(count):
            next(steps)

    get_w, get_u, get_d = gather(wz, 256, 512), gather(upz, 512, 256), gather(dnz, 256, 512)
    next(get_w)

    @pl.when(swap)
    def _():
        swap_x.start()

    own_up.wait()
    next(get_u)
    own_dn.wait()
    next(get_d)

    send_info = remote(info.at[0], info.at[1], partner)
    ub_copies = [remote(R.ubz.at[m], R.ubz.at[m], (dp, mx(k))) for k in (1, 2, 3)]

    send_info.wait_recv()
    for copy in loads:
        copy.wait()
    row = mb[1]
    mine = jnp.where(swap, 0.0, 1.0)

    def info_row(i):
        return info[0, pl.ds(i, 1), :] * mine + info[1, pl.ds(i, 1), :] * (1.0 - mine)

    doc = info_row(row)
    turn = info_row(row + 2)[:, 0:1]
    R.drow[...] = jnp.broadcast_to(doc, (8, S))
    R.dcol[...] = jnp.broadcast_to(doc, (128, S)).T
    freq = jnp.exp(
        lax.broadcasted_iota(jnp.int32, (32, 1), 0).astype(F32) * (-2.0 * math.log(10000.0) / HD)
    )
    cr, sr = jnp.cos(turn * freq), jnp.sin(turn * freq)
    past = lax.broadcasted_iota(jnp.int32, (1, S), 1).astype(F32) >= turn
    c0, s0 = R.ctab[...], R.stab[...]
    R.cttb[...] = jnp.where(past, c0 * cr + s0 * sr, c0)
    R.sttb[...] = jnp.where(past, s0 * cr - c0 * sr, s0)

    def at(base, i):
        return ds(base + i * CH, CH)

    def chunks(body):
        pl.loop(0, 2)(body)

    go(get_w, 3)

    @pl.when(jnp.logical_not(swap))
    def _():
        loc_x.wait()
        loc_c.wait()

    @pl.when(swap)
    def _():
        swap_x.wait()

    n1 = R.n1

    @chunks
    def _(i):
        rows = at(0, i)
        x = R.xt[rows, :].astype(F32)
        x = x - rowmean(x)
        rstd = lax.rsqrt(rowmean(x * x) + 1e-05)
        xh = x * rstd
        R.xh1[rows, :] = xh
        R.rs1[rows, :] = jnp.broadcast_to(rstd, (CH, 128))
        n1[at(r0, i), :] = (xh * R.n1g[...] + R.n1b[...]).astype(BF)

    send_n1 = remote(n1.at[own_rows, :], n1.at[own_rows, :], partner)
    go(get_w, 3)

    def project(z, base):
        lanes = ds(base, T)
        both = mmt(wz[z, 0:192, :], n1[lanes, :])
        cc, sn = R.cttb[:, lanes], R.sttb[:, lanes]
        for dst, a, b, scale in ((R.qt, both[0:32], both[32:64], 0.125), (R.kt, both[64:96], both[96:128], 1.0)):
            dst[z, 0:32, lanes] = (a * cc - b * sn).astype(BF) * jnp.asarray(scale, BF)
            dst[z, 32:64, lanes] = (b * cc + a * sn).astype(BF) * jnp.asarray(scale, BF)
        R.vt[z, :, lanes] = both[128:192].astype(BF)
        R.wh[ds(z * 192, 192), :] = wz[z, 0:192, :]
        R.wo[ds(z * 64, 64), :] = wz[z, 192:256, :]

    def span(i):
        width = min(i + 1, 3) * CH
        return (i + 1) * CH - width, width

    def lead(i):
        return sum(span(j)[1] for j in range(i))

    def attend(z):
        for i in range(4):
            j0, width = span(i)
            rows, keys = slice(i * CH, (i + 1) * CH), slice(j0, j0 + width)
            here = slice(lead(i), lead(i) + width)
            sc = tmm(R.qt[z, :, rows], R.kt[z, :, keys]) + R.bias[:, here]
            e = jnp.exp(sc - jnp.max(sc, axis=-1, keepdims=True))
            p = (e * (1.0 / jnp.sum(e, axis=-1, keepdims=True))).astype(BF)
            R.pr[z, :, here] = p
            R.ctxt[ds(z * 64, 64), rows] = mmt(R.vt[z, :, keys], p).astype(BF)

    project(m, r0)
    for i in range(4):
        j0, width = span(i)
        dcol = R.dcol[i * CH : (i + 1) * CH, :]
        qi = lax.broadcasted_iota(jnp.int32, (CH, 128), 0) + i * CH
        for w in range(width // 128):
            ki = lax.broadcasted_iota(jnp.int32, (CH, 128), 1) + (j0 + w * 128)
            ok = (dcol == R.drow[0:1, j0 + w * 128 : j0 + w * 128 + 128]) & (ki <= qi)
            R.bias[:, lead(i) + w * 128 : lead(i) + w * 128 + 128] = jnp.where(ok, 0.0, -1e30)
    send_n1.wait_recv()
    go(get_u, 3)
    project(m, p0)
    attend(m)
    go(get_d, 3)

    @pl.when(swap)
    def _():
        swap_c.start()


    @chunks
    def _(i):
        gate = mm(n1[at(r0, i), :], R.wg1v[...]) + R.g1b[...]
        R.g1[at(0, i), :] = sigmoid(gate)

    for k in near_first:
        go(get_w, 1)
        project(mx(k), r0)
        project(mx(k), p0)
        if k == 1:
            go(get_u, 3)
        if k == 2:
            go(get_d, 3)
        attend(mx(k))

    def hand_over(body):
        copies = []
        for i in range(2):
            rows = slice(i * CH, i * CH + CH)
            R.xs[rows, :] = body(i).astype(BF)
            copies.append(remote(R.xs.at[rows, :], R.xr.at[rows, :], partner, keep=False))
            copies[i].start()
        return copies

    def wait_all(copies):
        for copy in copies:
            copy.wait()

    send_at = hand_over(lambda i: tmm(R.ctxt[:, at(p0, i)], R.wo[...]))

    @chunks
    def _(i):
        R.amx[at(0, i), :] = tmm(R.ctxt[:, at(r0, i)], R.wo[...])

    wait_all(send_at)
    n2 = R.n2

    @chunks
    def _(i):
        rows = at(0, i)
        x = R.xt[rows, :].astype(F32)
        amx = R.amx[rows, :] + R.xr[rows, :].astype(F32) + R.ob[...] - x
        R.amx[rows, :] = amx
        mid = x + R.g1[rows, :] * amx
        R.mid[rows, :] = mid
        mid = mid - rowmean(mid)
        rstd = lax.rsqrt(rowmean(mid * mid) + 1e-05)
        xh = mid * rstd
        R.xh2[rows, :] = xh
        R.rs2[rows, :] = jnp.broadcast_to(rstd, (CH, 128))
        n2[at(r0, i), :] = (xh * R.n2g[...] + R.n2b[...]).astype(BF)

    send_n2 = remote(n2.at[own_rows, :], n2.at[own_rows, :], partner)
    arrived(ub_copies)

    def up_part(base, z):
        @chunks
        def _(i):
            rows = at(base, i)
            v = mm(n2[rows, :], upz[z]) + R.ubz[z, 0:1, :]
            v2 = v * v
            half = 0.5 * jnp.tanh(v * (GELU_A + (GELU_A * GELU_B) * v2)) + 0.5
            hid = v * half
            R.hid[z, rows, :] = hid.astype(BF)
            slope = half + hid * (1.0 - half) * (2.0 * GELU_A + (6.0 * GELU_A * GELU_B) * v2)
            R.gp[z, rows, :] = slope.astype(BF)

    def down_part(base, dst, z, begin):
        @chunks
        def _(i):
            part = mm(R.hid[z, at(base, i), :], dnz[z])
            dst[at(0, i), :] = part if begin else dst[at(0, i), :] + part

    up_part(r0, m)
    send_n2.wait_recv()
    up_part(p0, m)
    for k in near_first:
        go(get_u, 1)
        up_part(r0, mx(k))
        up_part(p0, mx(k))
    down_part(p0, R.acc, m, True)
    down_part(r0, R.gmr, m, True)
    for k in near_first:
        go(get_d, 1)
        down_part(p0, R.acc, mx(k), False)
        if k == near_first[-1]:
            send_br = hand_over(lambda i: R.acc[i * CH : i * CH + CH, :])
        down_part(r0, R.gmr, mx(k), False)

    @pl.when(swap)
    def _():
        swap_c.wait()

    pk = R.pk
    pk[...] = jnp.zeros((16, 512), F32)
    wait_all(send_br)

    @chunks
    def _(i):
        rows = at(0, i)
        gate = sigmoid(mm(n2[at(r0, i), :], R.wg2v[...]) + R.g2b[...])
        mid = R.mid[rows, :]
        bm = R.gmr[rows, :] + R.xr[rows, :].astype(F32) + R.db[...] - mid
        R.outb[rows, :] = (mid + gate * bm).astype(BF)
        cot = R.ct[rows, :].astype(F32)
        gb = gate * cot
        rest = cot - gb
        R.mid[rows, :] = rest
        gg = rest * bm * gate
        R.bl[at(r0, i), :] = gb.astype(BF)
        R.go2[rows, :] = gg.astype(BF)
        pk[6:7, :] += colsum(gb)
        pk[7:8, :] += colsum(gg)

    send_bl = remote(R.bl.at[own_rows, :], R.bl.at[own_rows, :], partner)
    send_gl2 = remote(R.go2.at[:, their_cols], R.gl2.at[own_rows, :], partner)
    keep_gl2 = local(R.go2.at[:, mine_cols], R.gl2.at[own_rows, :], 4)
    keep_gl2.start()
    back_o = remote(R.outb, R.o_out, cross, keep=False)
    keep_o = local(R.outb, R.o_out, 5)

    @pl.when(swap)
    def _():
        back_o.start()

    @pl.when(jnp.logical_not(swap))
    def _():
        keep_o.start()

    def hidden_back(base):
        for z in range(4):
            def step(i, acc, z=z):
                rows = at(base, i)
                gpre = mmt(R.bl[rows, :], dnz[z]) * R.gp[z, rows, :].astype(F32)
                R.gp[z, rows, :] = gpre.astype(BF)
                return acc + colsum(gpre)

            both = lax.fori_loop(0, 2, step, jnp.zeros((1, 256), F32))
            pk[8 + z : 9 + z, 0:256] += jnp.where(c == 0, both, 0.0)
            pk[8 + z : 9 + z, 256:512] += jnp.where(c == 0, 0.0, both)

    def norm_two_part(rows):
        total = mmt(R.gp[0, rows, :], upz[0])
        for z in range(1, 4):
            total = total + mmt(R.gp[z, rows, :], upz[z])
        return total

    def halving(block, buf, dev_a, dev_b, a, b, store):
        f32 = lambda ref: ref[...].astype(F32)
        one = [
            remote(block(a ^ b, 0), buf.at[0], dev_a), remote(block(a ^ b, 1), buf.at[1], dev_b),
            remote(block(a, 0), buf.at[2], dev_a), remote(block(b, 1), buf.at[3], dev_b),
        ]
        yield
        arrived(one[0:2])
        buf[6] = (f32(block(b, 0)) + f32(buf.at[0])).astype(BF)
        buf[7] = (f32(block(a, 1)) + f32(buf.at[1])).astype(BF)
        two = [remote(buf.at[6], buf.at[4], dev_b), remote(buf.at[7], buf.at[5], dev_a)]
        yield
        arrived(one[2:4] + two)
        store(0, (f32(block(0, 0)) + f32(buf.at[2]) + f32(buf.at[4])).astype(BF))
        store(1, (f32(block(0, 1)) + f32(buf.at[3]) + f32(buf.at[5])).astype(BF))

    def exchange(total, buf, dtype):
        for b in range(xbits):
            buf[2 * b] = total.astype(dtype)
            copy = remote(buf.at[2 * b], buf.at[2 * b + 1], (dpx(8 << b), m))
            copy.wait_recv()
            total = buf[2 * b].astype(F32) + buf[2 * b + 1].astype(F32)
        return total

    def chips(out):
        copies = [remote(out.at[slot], out.at[slot], (dpx(2 * k), m)) for k in (1, 2, 3)]
        yield
        arrived(copies)

    def chips_both(out):
        size = out.shape[1] // 2
        low, high = pl.ds(0, size), pl.ds(size, size)
        other = c * 4 + gx(2)
        pair = ds(c * 4 + 2 * bits[2], 2)
        copies = [
            remote(out.at[slot, low], out.at[slot, low], chip_x),
            remote(out.at[slot, high], out.at[slot, high], chip_y),
        ]
        yield
        arrived(copies)
        copies = [
            remote(out.at[pair, low], out.at[pair, low], chip_y),
            remote(out.at[slot, high], out.at[slot, high], chip_x),
            remote(out.at[other, high], out.at[other, high], chip_x),
        ]
        yield
        arrived(copies)

    def cores(out):
        return [remote(out.at[ds(c * 4, 4)], out.at[ds(c * 4, 4)], partner)]

    def flush(buf):
        copy = local(buf, homes[id(buf)], 12 + len(flushed))
        copy.start()
        flushed.append(copy)

    flushed = []
    homes = {
        id(R.p_a): R.o_a, id(R.p_u): R.o_u, id(R.p_d): R.o_d, id(R.p_g1): R.o_g1, id(R.p_g2): R.o_g2,
        id(R.p_vec): R.o_vec,
    }

    def finish(out, total, route=chips_both):
        out[slot] = total.astype(BF)
        yield from route(out)
        copies = cores(out)
        yield
        arrived(copies)
        flush(out)

    def finish_all(out, total):
        out[slot, m] = total.astype(BF)
        copies = [remote(out.at[slot, m], out.at[slot, m], (dp, mx(k))) for k in (1, 2, 3)]
        yield
        arrived(copies)
        yield from chips_both(out)
        copies = cores(out)
        yield
        arrived(copies)
        flush(out)

    def over_mp(b_ref, c_ref):
        return [remote(b_ref.at[mx(k)], c_ref.at[k - 1], (dp, mx(k))) for k in (1, 2, 3)]

    def plane_first(s_ref, h_ref, b_ref, c_ref, x_ref, quarter, end, out):
        def block(k, half):
            return s_ref.at[2 * half : 2 * half + 2, ds(gx(k) * quarter, quarter), :]

        def store(half, value):
            b_ref[2 * half : 2 * half + 2] = value

        yield from halving(block, h_ref, chip_x, chip_y, 1, 2, store)
        copies = over_mp(b_ref, c_ref)
        yield True
        arrived(copies)
        total = b_ref[m].astype(F32)
        for k in range(3):
            total = total + c_ref[k].astype(F32)
        yield from end(out, exchange(total, x_ref, BF))

    def block_sum(name, k, quarter, out, route):
        s_ref, h_ref = getattr(R, name + "_s"), getattr(R, name + "_h").at[k]
        b_ref, c_ref = getattr(R, name + "_b"), getattr(R, name + "_c")
        half_rows = quarter // 2

        def block(kk, half):
            return s_ref.at[mx(k), ds(gx(kk) * quarter + half * half_rows, half_rows), :]

        def store(half, value):
            b_ref[k, half * half_rows : half * half_rows + half_rows] = value

        def direct():
            copies = [
                remote(block(kk, half), h_ref.at[2 * kk - 2 + half], (dpx(2 * kk), m))
                for kk in (1, 2, 3) for half in (0, 1)
            ]
            yield
            arrived(copies)
            for half in (0, 1):
                total = block(0, half)[...].astype(F32)
                for kk in (1, 2, 3):
                    total = total + h_ref[2 * kk - 2 + half].astype(F32)
                store(half, total.astype(BF))

        if name == "a" and k == 0:
            yield from direct()
        else:
            yield from halving(block, h_ref, chip_x, chip_y, 1, 2, store)
        if k:
            waiting.setdefault(name, []).append(remote(b_ref.at[k], c_ref.at[k - 1], (dp, mx(k))))
            return
        yield True
        arrived(waiting[name])
        total = b_ref[0].astype(F32)
        for j in range(3):
            total = total + c_ref[j].astype(F32)
        yield from finish(out, exchange(total, extra(name + "_x"), BF), route)

    waiting, queue, late = {}, [], []

    def begin(steps):
        next(steps)
        queue.append(steps)

    def advance(source):
        steps = source.pop(0)
        for last in steps:
            (late if last or source is late else queue).append(steps)
            break

    def pump(count):
        for _ in range(min(count, len(queue))):
            advance(queue)

    def pump_late(count):
        for _ in range(min(count, len(late))):
            advance(late)

    extra = lambda name: getattr(R, name, None)
    sum_e = plane_first(R.e_s, R.e_h, R.e_b, R.e_c, extra("e_x"), 32, finish_all, R.p_g2)
    sum_f = plane_first(R.f_s, R.f_h, R.f_b, R.f_c, extra("f_x"), 32, finish_all, R.p_g1)
    far_first = (3, 2, 1, 0)

    hidden_back(r0)
    send_bl.wait_recv()
    for k in far_first:
        R.d_s[mx(k)] = tmm(R.hid[mx(k)], R.bl[...]).astype(BF)
        begin(block_sum("d", k, 64, R.p_d, chips_both))
    hidden_back(p0)
    n2t = n2[...].T
    for k in far_first:
        R.u_s[mx(k)] = mm(n2t, R.gp[mx(k)]).astype(BF)
        begin(block_sum("u", k, 128, R.p_u, chips_both))
        pump(1)
    send_gl2.wait_recv()
    keep_gl2.wait()
    full = mm(n2t, R.gl2[...]).astype(BF)
    for z in range(4):
        R.e_s[z] = full[z * 128 : z * 128 + 128, :]
    begin(sum_e)

    send_d2 = hand_over(lambda i: norm_two_part(at(p0, i)))

    @chunks
    def _(i):
        R.gmr[at(0, i), :] = norm_two_part(at(r0, i))

    pump(2)
    wait_all(send_d2)

    @chunks
    def _(i):
        rows = at(0, i)
        gn = R.gmr[rows, :] + R.xr[rows, :].astype(F32) + mmt(R.go2[rows, :], R.wg2v[...])
        xh = R.xh2[rows, :]
        pk[4:5, :] += colsum(gn * xh)
        pk[5:6, :] += colsum(gn)
        e = gn * R.n2g[...]
        gm = R.rs2[rows, 0:1] * (e - rowmean(e) - xh * rowmean(e * xh)) + R.mid[rows, :]
        gate = R.g1[rows, :]
        ga = gate * gm
        gg = (gm - ga) * R.amx[rows, :] * gate
        R.mid[rows, :] = gm - ga
        R.al[at(r0, i), :] = ga.astype(BF)
        R.go1[rows, :] = gg.astype(BF)
        pk[2:3, :] += colsum(ga)
        pk[3:4, :] += colsum(gg)

    send_al = remote(R.al.at[own_rows, :], R.al.at[own_rows, :], partner)
    send_gl1 = remote(R.go1.at[:, their_cols], R.gl1.at[own_rows, :], partner)
    keep_gl1 = local(R.go1.at[:, mine_cols], R.gl1.at[own_rows, :], 6)
    keep_gl1.start()
    n1t = n1[...].T
    send_al.wait_recv()

    @pl.loop(0, 4)
    def _(i):
        rows = at(0, i)
        R.dct[:, rows] = mmt(R.wo[...], R.al[rows, :]).astype(BF)

    pump(3)
    grad_wo = mm(R.ctxt[...], R.al[...]).astype(BF)
    for z in range(4):
        R.a_s[z, 192:256, :] = grad_wo[z * 64 : z * 64 + 64, :]
    send_gl1.wait_recv()
    keep_gl1.wait()
    full = mm(n1t, R.gl1[...]).astype(BF)
    for z in range(4):
        R.f_s[z] = full[z * 128 : z * 128 + 128, :]

    begin(sum_f)
    pump(2)

    dkt, dvt, dt = R.dkt, R.dvt, R.dt

    for k in far_first:
        z = mx(k)
        dkt[...] = jnp.zeros((64, S), F32)
        dvt[...] = jnp.zeros((64, S), F32)
        mine_rows = ds(z * 64, 64)

        def dt_rows(start, size, z=z):
            return pl.ds(pl.multiple_of(z * 192 + start, 32), size)

        for i in range(4):
            j0, width = span(i)
            rows, keys = slice(i * CH, (i + 1) * CH), slice(j0, j0 + width)
            p = R.pr[z, :, lead(i) : lead(i) + width]
            pf = p.astype(F32)
            t = tmm(R.dct[mine_rows, rows], R.vt[z, :, keys]) * pf
            part = (t - pf * jnp.sum(t, axis=-1, keepdims=True)).astype(BF)
            dvt[:, keys] += mm(R.dct[mine_rows, rows], p)
            dkt[:, keys] += mm(R.qt[z, :, rows], part)
            dq = mmt(R.kt[z, :, keys], part) * 0.125
            a, b = dq[0:32], dq[32:64]
            cc, sn = R.cttb[:, rows], R.sttb[:, rows]
            dt[dt_rows(0, 32), rows] = (a * cc + b * sn).astype(BF)
            dt[dt_rows(32, 32), rows] = (b * cc - a * sn).astype(BF)
            if i >= 4 - (4, 3, 3, 2)[3 - k]:
                pump(1)
            if k == 0:
                pump_late(1)
        a, b = dkt[0:32, :], dkt[32:64, :]
        cc, sn = R.cttb[...], R.sttb[...]
        dt[dt_rows(64, 32), :] = (a * cc + b * sn).astype(BF)
        dt[dt_rows(96, 32), :] = (b * cc - a * sn).astype(BF)
        dt[dt_rows(128, 64), :] = dvt[...].astype(BF)
        R.a_s[z, 0:192, :] = mm(dt[dt_rows(0, 192), :], n1[...]).astype(BF)
        begin(block_sum("a", k, 64, R.p_a, chips))

    send_d1 = hand_over(lambda i: tmm(dt[:, at(p0, i)], R.wh[...]))
    pump(3)

    @chunks
    def _(i):
        R.gmr[at(0, i), :] = tmm(dt[:, at(r0, i)], R.wh[...])

    pump(3)
    wait_all(send_d1)

    def norm_one_back(i):
        rows = slice(i * CH, i * CH + CH)
        gn = R.gmr[rows, :] + R.xr[rows, :].astype(F32) + mmt(R.go1[rows, :], R.wg1v[...])
        xh = R.xh1[rows, :]
        pk[0:1, :] += colsum(gn * xh)
        pk[1:2, :] += colsum(gn)
        e = gn * R.n1g[...]
        grad = R.rs1[rows, 0:1] * (e - rowmean(e) - xh * rowmean(e * xh)) + R.mid[rows, :]
        R.gtb[rows, :] = grad.astype(BF)

    back_t, keep_t = [], []
    for i in range(2):
        norm_one_back(i)
        rows = slice(i * CH, i * CH + CH)
        back_t.append(remote(R.gtb.at[rows, :], R.o_gt.at[rows, :], cross, keep=False))
        keep_t.append(local(R.gtb.at[rows, :], R.o_gt.at[rows, :], 7 + i))

        @pl.when(swap)
        def _():
            back_t[i].start()

        @pl.when(jnp.logical_not(swap))
        def _():
            keep_t[i].start()

    pk1, pk2, pk3 = R.pk1, R.pk2, R.pk3
    pk1[c] = pk[...]
    p_1 = remote(pk1.at[c], pk1.at[c], partner)
    pump(2)
    pump_late(4)
    p_1.wait_recv()
    pk2[g] = pk1[0] + pk1[1]
    p_2 = [remote(pk2.at[g], pk2.at[g], (dpx(2 * k), m)) for k in (1, 2, 3)]
    pump(4)
    pump_late(5)
    arrived(p_2)
    pk3[m] = (pk2[0] + pk2[1]) + (pk2[2] + pk2[3])
    p_3 = [remote(pk3.at[m], pk3.at[m], (dp, mx(k))) for k in (1, 2, 3)]
    pump_late(5)
    arrived(p_3)
    total = exchange((pk3[0] + pk3[1]) + (pk3[2] + pk3[3]), extra("p_x"), F32)
    pk[...] = total
    R.p_vec[...] = total
    R.p_vec[8:9, :] = pk[pl.ds(8 + m, 1), :]
    flush(R.p_vec)
    while queue or late:
        pump(1)
        pump_late(1)

    for copy in unsent:
        copy.wait_send()
    for copy in flushed:
        copy.wait()

    @pl.when(swap)
    def _():
        for copy in (back_o, *back_t):
            copy.wait()

    @pl.when(jnp.logical_not(swap))
    def _():
        for copy in (keep_o, *keep_t):
            copy.wait()


def unpack(a, u, d, g1, g2, vec, out, gt, *outs):
    (oq, ok, ov, oo, ou, od, og1, og2, oout, ogt) = outs[:10]
    for j, ref in enumerate((oq, ok, ov)):
        both = jnp.concatenate([a[j].astype(F32), a[4 + j].astype(F32)], axis=0)
        ref[...] = both.T
    for c in range(2):
        oo[c * 64 : c * 64 + 64, :] = a[4 * c + 3].astype(F32)
        for g in range(4):
            ou[g * 128 : g * 128 + 128, c * 256 : c * 256 + 256] = u[4 * c + g].astype(F32)
            od[c * 256 + g * 64 : c * 256 + g * 64 + 64, :] = d[4 * c + g].astype(F32)
            for z in range(4):
                rows = slice(z * 128 + g * 32, z * 128 + g * 32 + 32)
                og1[rows, c * 256 : c * 256 + 256] = g1[4 * c + g, z].astype(F32)
                og2[rows, c * 256 : c * 256 + 256] = g2[4 * c + g, z].astype(F32)
    oout[...] = out[...]
    ogt[...] = gt[...].astype(F32)
    for j, ref in enumerate(outs[10:]):
        ref[...] = vec[j : j + 1, :]


def tables():
    freqs = np.exp(np.arange(HD // 2, dtype=np.float32) * np.float32(-2.0 * math.log(10000.0) / HD))
    angles = np.arange(S, dtype=np.float32)[:, None] * freqs.astype(np.float32)
    angles = angles.T.astype(np.float64)
    return np.cos(angles).astype(np.float32), np.sin(angles).astype(np.float32)


def shards(
    ndp, tokens, doc_ids, resets, n1g, n1b, qw, kw, vw, ow, ob, wg1, g1b, n2g, n2b, up, ub, down, db,
    wg2, g2b, cot,
):
    xbits = ndp.bit_length() - 4
    ctab, stab = tables()
    vector = lambda v: v.reshape(1, -1)
    values = dict(
        tokens=tokens, cot=cot, docs=doc_ids, resets=resets.reshape(1, 2), qw=qw, kw=kw, vw=vw, ow=ow,
        wg1=wg1, up=up, down=down, wg2=wg2, n1g=vector(n1g), n1b=vector(n1b), ob=vector(ob),
        g1b=vector(g1b), n2g=vector(n2g), n2b=vector(n2b), ub=vector(ub), db=vector(db), g2b=vector(g2b),
        ctab=jnp.asarray(ctab), stab=jnp.asarray(stab),
    )
    vmem = pl.BlockSpec(memory_space=pltpu.VMEM)
    anyspace = pl.BlockSpec(memory_space=pl.ANY)
    scratch = {name: pltpu.VMEM(shape, dtype) for name, (shape, dtype) in SCRATCH.items()}
    if xbits:
        more = dict(a_x=(64, 512), u_x=(128, 256), d_x=(64, 512), e_x=(32, 256), f_x=(32, 256))
        for name, shape in more.items():
            scratch[name] = pltpu.VMEM((2 * xbits,) + shape, BF)
        scratch.update(p_x=pltpu.VMEM((2 * xbits, 16, 512), F32))
    copies = pltpu.SemaphoreType.DMA((NCOPY + 6 * xbits,))
    scratch.update(
        ss=copies, rs=copies, ls=pltpu.SemaphoreType.DMA((20,))
    )
    in_specs = dict.fromkeys(values, anyspace)
    small = [name for name in values if name not in BIG]
    for name in small:
        scratch[IN + name] = pltpu.VMEM(values[name].shape, values[name].dtype)
    scratch.update(ins=pltpu.SemaphoreType.DMA((len(small),)))
    packed = pl.pallas_call(
        functools.partial(kernel, ndp, xbits, (*values, *OUT_SHAPES, *scratch)),
        out_shape=[jax.ShapeDtypeStruct(shape, dtype) for shape, dtype in OUT_SHAPES.values()],
        in_specs=list(in_specs.values()),
        out_specs=[anyspace] * len(OUT_SHAPES),
        scratch_shapes=list(scratch.values()),
        compiler_params=pltpu.CompilerParams(
            collective_id=0, has_side_effects=True, vmem_limit_bytes=64 << 20
        ),
        name="block",
    )(*values.values())
    out, gt, a, u, d, g1, g2, vec = packed
    f32 = lambda *shape: jax.ShapeDtypeStruct(shape, F32)
    shapes = [f32(D, 128)] * 3 + [f32(128, D)] + [f32(D, D)] * 4
    shapes += [jax.ShapeDtypeStruct((T, D), BF), f32(T, D)] + [f32(1, D)] * 9
    res = pl.pallas_call(
        unpack,
        out_shape=shapes,
        in_specs=[vmem] * 8,
        out_specs=[vmem] * len(shapes),
        compiler_params=pltpu.CompilerParams(vmem_limit_bytes=63 << 20),
        name="unpack",
    )(a, u, d, g1, g2, vec, out, gt)
    gq, gk, gv, go, gu, gd, gg1, gg2, out, gt = res[:10]
    rn1g, rn1b, rob, rg1b, rn2g, rn2b, rdb, rg2b, rub = [v.reshape(-1) for v in res[10:]]
    return (
        out, gt, rn1g, rn1b, gq, gk, gv, go, rob, gg1, rg1b, rn2g, rn2b, gu, rub, gd, rdb, gg2, rg2b,
    )


def solution(mesh):
    both, rep = P(("dp", "mp"), None), P()
    cols, rows = P(None, "mp"), P("mp", None)
    in_specs = (
        both, P("dp", None), P("dp"), rep, rep, cols, cols, cols, rows, rep, rep, rep, rep, rep, cols,
        P("mp"), rows, rep, rep, rep, both,
    )
    out_specs = (
        both, both, rep, rep, cols, cols, cols, rows, rep, rep, rep, rep, rep, cols, P("mp"), rows, rep,
        rep, rep,
    )
    fn = functools.partial(shards, mesh.shape["dp"])
    return jax.shard_map(fn, mesh=mesh, in_specs=in_specs, out_specs=out_specs, check_vma=False)
```
